32 devices in a mesh: rows: 16 (over z, x, core), field: 2 (over y).
Axes of the slice: x: 2, y: 2, z: 4, core: 2. Of those that a mesh axis runs over, the one named last changes fastest.
Arguments:
- dense: bfloat16 [73728, 96], P('rows', 'field'), may hold values from -6 to 6
- ids: int32 [73728, 26], P('rows', 'field'), may hold values from 0 to 1023
- table: float32 [26, 1024, 16], P('field'), may hold values from -6 to 6
- sizes: int32 [16, 256], P('rows'), may hold values from 1 to 64, 4608 in all within a row
- labels: int32 [73728, 2], P('rows'), may hold values from 0 to 1
- w_expert: bfloat16 [512, 2048], P('field'), may hold values from -0.25 to 0.25
- b_expert: float32 [2048], replicated, may hold values from -3 to 3
- w_gate: bfloat16 [512, 16], P('field'), may hold values from -0.125 to 0.125
- b_gate: float32 [16], replicated, may hold values from -0.3 to 0.3
- w_inner: bfloat16 [8, 256, 128], replicated, may hold values from -0.375 to 0.375
- b_inner: float32 [8, 128], replicated, may hold values from -3 to 3
- w_tower: bfloat16 [2, 128, 64], replicated, may hold values from -0.5 to 0.5
- b_tower: float32 [2, 64], replicated, may hold values from -3 to 3
- w_head: bfloat16 [2, 64], replicated, may hold values from -1.5 to 1.5
- b_head: float32 [2], replicated, may hold values from -3 to 3
Outputs:
- predicted: float32 [73728, 2], P('rows')
- loss_total: float32 [], replicated
- d_dense: float32 [73728, 96], P('rows', 'field')
- d_table: float32 [26, 1024, 16], P('field', 'rows')
- d_w_expert: float32 [512, 2048], P('field', 'rows')
- d_b_expert: float32 [2048], replicated
- d_w_gate: float32 [512, 16], P('field')
- d_b_gate: float32 [16], replicated
- d_w_inner: float32 [8, 256, 128], replicated
- d_b_inner: float32 [8, 128], replicated
- d_w_tower: float32 [2, 128, 64], replicated
- d_b_tower: float32 [2, 64], replicated
- d_w_head: float32 [2, 64], replicated
- d_b_head: float32 [2], replicated
The draws below stay inside these ranges and needn't reach their ends.
Inputs may be any that keep to these rules, and one draw needn't show every extreme that they name: Each row shard's 256 group sizes sum to 4608; every shard has a group of exactly 64 rows.
All inputs are finite; a program needn't handle non-finite values.
Results may differ from the reference program's by a relative error of at most 0.015.
Values may be sent and summed in bfloat16 or wider, within the bound.
No kernel may reach another device: no remote copies, remote signals or barrier semaphores. Data moves between devices by JAX's collectives and lax.ppermute only.
A program may use at most 384 MiB of HBM per device.

```python
import math
import jax
import jax.numpy as jnp
import numpy as np
from jax import lax

FIELDS = 26
EMB = 16
DENSE = 96
VOCAB = 1024
EXPERTS = 8
H1 = 256
H2 = 128
TASKS = 2
TOWER = 64
GROUPS_DEV = 256
MOST = 64
ROWS_DEV = 4608
IN = 512
NE = 2048
NG = 16
ROWS = 73728
N_ROWS = 16
N_FIELD = 2


def draw_labels(key, part):
    key = jax.random.fold_in(key, 7)
    shard = jnp.arange(ROWS, dtype=jnp.int32) // ROWS_DEV
    threshold = 50 + 450 * shard // max(N_ROWS - 1, 1)
    draws = jax.random.randint(key, (ROWS, TASKS), 0, 1000, dtype=jnp.int32)
    return (draws < threshold[:, None]).astype(jnp.int32)


def touch_ends(result, stream_key, smallest, high):
    dims = result.shape
    spot = [jax.random.randint(jax.random.fold_in(stream_key, axis), (), 0, dims[axis]) for axis in range(len(dims))]
    result = result.at[tuple(spot)].set(smallest)
    longest = dims.index(max(dims))
    spot[longest] = (spot[longest] + 1) % dims[longest]
    return result.at[tuple(spot)].set(high)


def level_of(stream_key, dims, cuts, low, largest):
    def one(axis_at, blocks):
        steps = jax.random.uniform(jax.random.fold_in(jax.random.fold_in(stream_key, 6), axis_at), (blocks,), jnp.float32, low / len(cuts), largest / len(cuts))
        return jnp.repeat(jnp.exp(steps), dims[axis_at] // blocks).reshape((-1,) + (1,) * (len(dims) - axis_at - 1))

    level = one(*cuts[0])
    for cut in cuts[1:]:
        level = level * one(*cut)
    return level


def rank_bounds(amount, skew):
    weights = [(1 << 20) // math.isqrt(standing ** skew) + 1 for standing in range(1, amount + 1)]
    scale = 1 + sum(weights) // (1 << 30)
    return np.cumsum(np.array([max(1, weight // scale) for weight in weights]))


def ranked(key, dims, number_of, slope):
    grid = rank_bounds(number_of, slope)
    pick = jax.random.randint(jax.random.fold_in(key, 1), dims, 0, int(grid[number_of - 1]))
    grade = jnp.searchsorted(jnp.asarray(grid, jnp.int32), pick, side="right")
    return jax.random.permutation(jax.random.fold_in(key, 2), number_of)[grade].astype(jnp.int32)


def split_up(number_of, total, reach, slope):
    portions = [(1 << 20) // math.isqrt(grade ** slope) + 1 for grade in range(2, number_of + 1)]
    rest, holding = total - reach - (number_of - 1), [1] * (number_of - 1)
    while rest > 0:
        candidates = [i for i in range(number_of - 1) if holding[i] < reach]
        mass, remaining = sum([portions[i] for i in candidates]), rest
        for i in candidates:
            extra = min(reach - holding[i], max(1, remaining * portions[i] // mass), rest)
            holding[i] = holding[i] + extra
            rest = rest - extra
    return np.array([reach] + holding)


def uneven(stream_key, number_of, total, most, slope):
    if number_of == 2:
        one = jax.random.randint(stream_key, (), max(1, total - most), min(most, total - 1) + 1)
        return jnp.stack([one, total - one])
    lengths = jnp.asarray(split_up(number_of, total, most, slope), jnp.int32)
    twos = (number_of - 1) // 2
    donor, taker = lengths[1:1 + 2 * twos:2], lengths[2:2 + 2 * twos:2]
    room = jnp.minimum(donor - 1, most - taker)
    shifted = jax.random.randint(jax.random.fold_in(stream_key, 1), (twos,), 0, 1 << 20) % (room + 1)
    lengths = lengths.at[1:1 + 2 * twos:2].set(donor - shifted).at[2:2 + 2 * twos:2].set(taker + shifted)
    return lengths[jax.random.permutation(jax.random.fold_in(stream_key, 2), number_of)]


def noise(own_key, shape, scale, most, shards=(), held_as=jnp.bfloat16):
    factor_of = level_of(own_key, shape, shards, -0.22, 0.18) if shards else 1.0
    array = jax.random.normal(own_key, shape, jnp.float32) * scale * factor_of
    return jnp.minimum(jnp.maximum(array, -most), most).astype(held_as)


def setup_inputs(seed: int = 0) -> dict:
    splits = jax.random.split(jax.random.key(seed), 16)
    dense = noise(splits[0], (ROWS, DENSE), 1.0, 6.0, ((0, 16), (1, 2)))
    ids = touch_ends(ranked(splits[1], (ROWS, FIELDS), VOCAB, 2), jax.random.fold_in(splits[1], 3), 0, VOCAB - 1).astype(jnp.int32)
    table = noise(splits[2], (FIELDS, VOCAB, EMB), 1.0, 6.0, ((0, 2),), jnp.float32)
    sizes = jax.vmap(lambda own: uneven(own, GROUPS_DEV, ROWS_DEV, MOST, 2))(jax.random.split(splits[3], N_ROWS)).reshape((N_ROWS, GROUPS_DEV)).astype(jnp.int32)
    labels = draw_labels(jax.random.fold_in(splits[15], 71), 0)
    w_expert = noise(splits[5], (IN, NE), IN ** -0.5, 0.25, ((0, 2),))
    b_expert = noise(splits[6], (NE,), 0.5, 3.0, (), jnp.float32)
    w_gate = noise(splits[7], (IN, NG), (4 * IN) ** -0.5, 0.125, ((0, 2),))
    b_gate = noise(splits[8], (NG,), 0.05, 0.3, (), jnp.float32)
    w_inner = noise(splits[9], (EXPERTS, H1, H2), H1 ** -0.5, 0.375)
    b_inner = noise(splits[10], (EXPERTS, H2), 0.5, 3.0, (), jnp.float32)
    w_tower = noise(splits[11], (TASKS, H2, TOWER), H2 ** -0.5, 0.5)
    b_tower = noise(splits[12], (TASKS, TOWER), 0.5, 3.0, (), jnp.float32)
    w_head = noise(splits[13], (TASKS, TOWER), (TOWER // 4) ** -0.5, 1.5)
    b_head = noise(splits[14], (TASKS,), 1.0, 3.0, (), jnp.float32)
    return {"dense": dense, "ids": ids, "table": table, "sizes": sizes, "labels": labels, "w_expert": w_expert, "b_expert": b_expert, "w_gate": w_gate, "b_gate": b_gate, "w_inner": w_inner, "b_inner": b_inner, "w_tower": w_tower, "b_tower": b_tower, "w_head": w_head, "b_head": b_head}


@jax.custom_vjp
def low(v):
    return lax.optimization_barrier(v.astype(jnp.bfloat16)).astype(jnp.float32)

@jax.custom_vjp
def low_back(v):
    return v

def low_keep(v):
    return (low(v), None)

def low_pass(kept, grad):
    return (grad,)

def back_keep(v):
    return (v, None)

def back_low(kept, grad):
    return (low(grad),)
low.defvjp(low_keep, low_pass)
low_back.defvjp(back_keep, back_low)

def group_weight(group_sizes, row_count):
    ends = jnp.cumsum(group_sizes).astype(jnp.int32)
    starts = (ends - group_sizes).astype(jnp.int32)
    places = jnp.arange(row_count, dtype=jnp.int32)[:, None]
    inside = (places >= starts[None, :]) & (places < ends[None, :])
    share = 1.0 / group_sizes.astype(jnp.float32)
    return lax.optimization_barrier(jnp.sum(jnp.where(inside, share[None, :], jnp.zeros_like(share)[None, :]), axis=1))

def forward(table, w_expert, b_expert, w_gate, b_gate, w_inner, b_inner, w_tower, b_tower, w_head, b_head, dense, ids, clicks, weight, loss_scale):
    highest = lax.Precision.HIGHEST
    row_count = dense.shape[0]
    fields_half = FIELDS // N_FIELD
    dense_half = DENSE // N_FIELD
    width_half = IN // N_FIELD
    looked = jax.vmap(lambda table_part, column: table_part[column], in_axes=(0, 1), out_axes=1)(table, ids)
    pieces = []
    for group_index in range(N_FIELD):
        block = looked[:, group_index * fields_half:(group_index + 1) * fields_half]
        pieces.append(block.reshape(row_count, fields_half * EMB))
        pieces.append(dense[:, group_index * dense_half:(group_index + 1) * dense_half])
    features = low(jnp.concatenate(pieces, axis=1))
    first_weights = jnp.concatenate([w_expert, w_gate], axis=1)
    summed = jnp.zeros((row_count, NE + NG), jnp.float32)
    for group_index in range(N_FIELD):
        lower = group_index * width_half
        partial_sum = jnp.dot(features[:, lower:lower + width_half], first_weights[lower:lower + width_half], precision=highest)
        summed = summed + low(partial_sum)
    summed = low_back(summed)
    pre_expert = summed[:, :NE] + b_expert
    gate_logits = (summed[:, NE:] + b_gate).reshape(row_count, TASKS, EXPERTS)
    hidden_act = low(jax.nn.silu(pre_expert)).reshape(row_count, EXPERTS, H1)
    second_pre = low_back(jnp.einsum('rei,eio->reo', hidden_act, w_inner, precision=highest)) + b_inner
    expert_out = jax.nn.silu(second_pre)
    gate_mix = jax.nn.softmax(gate_logits, axis=-1)
    mixed = jnp.einsum('rte,reo->rto', gate_mix, expert_out, precision=highest)
    tower_pre = low_back(jnp.einsum('rto,toh->rth', low(mixed), w_tower, precision=highest)) + b_tower
    tower_out = low(jax.nn.silu(tower_pre))
    logit_out = lax.optimization_barrier(jnp.sum(tower_out * w_head, axis=-1)) + b_head
    log_loss = jax.nn.softplus(logit_out) - clicks * logit_out
    loss_sum = jnp.sum(weight[:, None] * log_loss * loss_scale[None, :])
    return (loss_sum, jax.nn.sigmoid(logit_out))

def reference(dense, ids, table, sizes, labels, w_expert, b_expert, w_gate, b_gate, w_inner, b_inner, w_tower, b_tower, w_head, b_head):
    params = tuple((value.astype(jnp.float32) for value in (table, w_expert, b_expert, w_gate, b_gate, w_inner, b_inner, w_tower, b_tower, w_head, b_head)))
    dense_blocks = dense.astype(jnp.float32).reshape(N_ROWS, ROWS_DEV, DENSE)
    id_blocks = ids.reshape(N_ROWS, ROWS_DEV, FIELDS)
    click_blocks = labels.astype(jnp.float32).reshape(N_ROWS, ROWS_DEV, TASKS)

    def shard_rate(inputs):
        group_sizes, clicks = inputs
        weight = group_weight(group_sizes, ROWS_DEV)
        return lax.optimization_barrier(jnp.sum(weight[:, None] * clicks, axis=0))
    rate_sum = lax.optimization_barrier(jnp.sum(lax.map(shard_rate, (sizes, click_blocks)), axis=0))
    groups_total = jnp.float32(N_ROWS * GROUPS_DEV)
    click_rate = (rate_sum + 1.0) / (groups_total + 2.0)
    entropy = -(click_rate * jnp.log(click_rate) + (1.0 - click_rate) * jnp.log(1.0 - click_rate))
    loss_scale = 1.0 / (groups_total * entropy)

    def step(carry, inputs):
        group_sizes, dense_block, id_block, clicks = inputs
        weight = group_weight(group_sizes, ROWS_DEV)

        def loss_fn(*values):
            return forward(*values, id_block, clicks, weight, loss_scale)
        loss_sum, back, predicted = jax.vjp(loss_fn, *params, dense_block, has_aux=True)
        grads = back(jnp.ones((), jnp.float32))
        totals, loss_acc = carry
        totals = tuple((total + grad for total, grad in zip(totals, grads[:-1])))
        return ((totals, loss_acc + loss_sum), (predicted, grads[-1]))
    start = (tuple((jnp.zeros_like(value) for value in params)), jnp.zeros((), jnp.float32))
    (totals, loss_total), (predicted, d_dense) = lax.scan(step, start, (sizes, dense_blocks, id_blocks, click_blocks))
    predicted = predicted.reshape(ROWS, TASKS)
    d_dense = d_dense.reshape(ROWS, DENSE)
    return (predicted, loss_total, d_dense, totals[0], totals[1], totals[2], totals[3], totals[4], totals[5], totals[6], totals[7], totals[8], totals[9], totals[10])
```

```python
import functools

import jax
import jax.numpy as jnp
from jax import lax
from jax.experimental import pallas as pl
from jax.experimental.pallas import tpu as pltpu
from jax.sharding import PartitionSpec as P

BF = jnp.bfloat16
F32 = jnp.float32
LANES = 128
BLOCK = 256
VMEM_LIMIT = 56 * 1024 * 1024

NN = (((1,), (0,)), ((), ()))
TN = (((0,), (0,)), ((), ()))
NT = (((1,), (1,)), ((), ()))


def dot(a, b, dims=NN):
    return lax.dot_general(a, b, dims, preferred_element_type=F32)


def swap(value, axis, bit):
    size = lax.axis_size(axis)
    return lax.ppermute(value, axis, [(i, i ^ bit) for i in range(size)])


def tile_lanes(column, lanes):
    return jnp.concatenate([column] * (lanes // LANES), axis=1)


def fold_lanes(value):
    total = value[:, :LANES]
    for start in range(LANES, value.shape[1], LANES):
        total = total + value[:, start : start + LANES]
    return total


def weight_kernel(sizes_ref, labels_ref, weight_ref, rate_ref):
    groups, rows = sizes_ref.shape[1], labels_ref.shape[1]
    sizes = jnp.broadcast_to(sizes_ref[...].astype(F32), (groups, groups))
    below = lax.broadcasted_iota(jnp.int32, (groups, groups), 0)
    across = lax.broadcasted_iota(jnp.int32, (groups, groups), 1)
    starts = jnp.sum(jnp.where(across < below, sizes, 0.0), axis=1, keepdims=True)
    own = jnp.sum(jnp.where(across == below, sizes, 0.0), axis=1, keepdims=True)
    ends = starts + own
    share = 1.0 / own
    rate = jnp.zeros((2, LANES), F32)
    for at in range(0, rows, BLOCK):
        place = (lax.broadcasted_iota(jnp.int32, (groups, BLOCK), 1) + at).astype(F32)
        inside = (place >= starts) & (place < ends)
        weight = jnp.sum(jnp.where(inside, share, 0.0), axis=0, keepdims=True)
        weight_ref[:, at : at + BLOCK] = weight
        rate = rate + fold_lanes(weight * labels_ref[:, at : at + BLOCK].astype(F32))
    rate_ref[...] = jnp.broadcast_to(jnp.sum(rate, axis=1, keepdims=True), rate_ref.shape)


def look_up(ids_ref, table_ref, dense_ref, feat_ref):
    fields, emb, vocab = table_ref.shape
    for f in range(fields):
        for at in range(0, feat_ref.shape[1], LANES):
            ids = ids_ref[f : f + 1, at : at + LANES]
            low = jnp.broadcast_to(jnp.bitwise_and(ids, LANES - 1), (emb, LANES))
            high = jnp.broadcast_to(jnp.right_shift(ids, 7), (emb, LANES))
            found = None
            for h in range(vocab // LANES):
                part = jnp.take_along_axis(
                    table_ref[f, :, h * LANES : (h + 1) * LANES],
                    low,
                    axis=1,
                    mode="promise_in_bounds",
                )
                found = part if found is None else jnp.where(high == h, part, found)
            feat_ref[f * emb : (f + 1) * emb, at : at + LANES] = found.astype(BF)
    feat_ref[fields * emb :, :] = dense_ref[...]


def first_kernel(j_ref, ids_ref, dense_ref, table_ref, w_ref, wg_ref, bias_ref, feat_ref, part_ref, gpart_ref):
    lanes = feat_ref.shape[1]
    look_up(ids_ref, table_ref, dense_ref, feat_ref)
    half = feat_ref[...] * jnp.asarray(0.5, BF)
    for at in range(0, w_ref.shape[1], 256):
        acc = dot(w_ref[:, at : at + 256], half, TN)
        part_ref[at : at + 256, :] = (acc + tile_lanes(bias_ref[at : at + 256, :], lanes)).astype(BF)
    gpart_ref[...] = dot(wg_ref[...], half)


def middle_kernel(
    groups_total,
    j_ref,
    rate_ref,
    ids_ref,
    dense_ref,
    table_ref,
    w_ref,
    wg_ref,
    part_ref,
    gpart_ref,
    bg_ref,
    wi_ref,
    bi_ref,
    wt_ref,
    bt_ref,
    wh_ref,
    bh_ref,
    labels_ref,
    weight_ref,
    feat_ref,
    u_ref,
    ds_ref,
    dg_ref,
    pred_ref,
    dwide_ref,
    small_ref,
    h_s,
    eo_s,
    sl_s,
    dwide_s,
):
    step, steps = pl.program_id(0), pl.num_programs(0)
    lanes = feat_ref.shape[1]
    experts, h1, h2 = wi_ref.shape
    tasks, tower = wt_ref.shape[0], wt_ref.shape[1]

    @pl.when(step == 0)
    def _():
        dwide_s[...] = jnp.zeros_like(dwide_s)
        small_ref[...] = jnp.zeros_like(small_ref)

    look_up(ids_ref, table_ref, dense_ref, feat_ref)
    half = feat_ref[...] * jnp.asarray(0.5, BF)

    gate_logits = 2.0 * (gpart_ref[...] + dot(wg_ref[...], half)) + tile_lanes(bg_ref[...], lanes)
    gates = []
    for t in range(tasks):
        logits = gate_logits[t * experts : (t + 1) * experts]
        top = jnp.exp(logits - jnp.max(logits, axis=0, keepdims=True))
        gates.append(top / jnp.sum(top, axis=0, keepdims=True))

    mixed = [jnp.zeros((h2, lanes), F32) for _ in range(tasks)]
    for e in range(experts):
        at = e * h1
        u = dot(w_ref[:, at : at + h1], half, TN) + part_ref[at : at + h1, :].astype(F32)
        u_ref[at : at + h1, :] = u.astype(BF)
        hidden = (u + u * jnp.tanh(u)).astype(BF)
        h_s[at : at + h1, :] = hidden
        u2 = dot(wi_ref[e], hidden, TN) + tile_lanes(bi_ref[e * h2 : (e + 1) * h2, :], lanes)
        t2 = jnp.tanh(u2)
        out = u2 + u2 * t2
        eo_s[e] = out
        sl_s[e] = (1.0 + out) + t2 * (1.0 - out)
        for t in range(tasks):
            mixed[t] = mixed[t] + gates[t][e : e + 1, :] * out

    rate = rate_ref[...]
    click = (rate + 1.0) / (groups_total + 2.0)
    entropy = -(click * jnp.log(click) + (1.0 - click) * jnp.log(1.0 - click))
    scale = tile_lanes(1.0 / (groups_total * entropy), lanes)
    labels = labels_ref[...].astype(F32)
    weight = weight_ref[...]

    preds, d_logits, losses, d_mixed = [], [], [], []
    for t in range(tasks):
        rows = slice(t * tower, (t + 1) * tower)
        low = mixed[t].astype(BF)
        tower_pre = dot(wt_ref[t], low) + tile_lanes(bt_ref[rows, :], lanes)
        sigma = 0.5 + 0.5 * jnp.tanh(0.5 * tower_pre)
        tower_out = (tower_pre * sigma).astype(BF).astype(F32)
        head = tile_lanes(wh_ref[rows, :], lanes)
        logit = jnp.sum(tower_out * head, axis=0, keepdims=True) + tile_lanes(bh_ref[t : t + 1, :], lanes)
        label = labels[t : t + 1]
        pred = jax.nn.sigmoid(logit)
        share = weight * scale[t : t + 1]
        plus = jnp.maximum(logit, 0.0) + jnp.log1p(jnp.exp(-jnp.abs(logit)))
        losses.append(share * (plus - label * logit))
        d_logit = share * (pred - label)
        preds.append(pred)
        d_logits.append(d_logit)
        d_tower = d_logit * head * (sigma * (1.0 + tower_pre * (1.0 - sigma)))
        d_low = d_tower.astype(BF)
        base = experts * h2
        small_ref[base + t * tower : base + (t + 1) * tower, :] += fold_lanes(d_tower)
        base = base + tasks * tower
        small_ref[base + t * tower : base + (t + 1) * tower, :] += fold_lanes(d_logit * tower_out)
        dwide_s[experts * h1 + t * tower : experts * h1 + (t + 1) * tower, :] += dot(d_low, low, NT)
        d_mixed.append(dot(wt_ref[t], d_low, TN))
    pred_ref[...] = jnp.concatenate(preds, axis=0)
    base = experts * h2 + 2 * tasks * tower + tasks * experts
    small_ref[base : base + 8, :] += fold_lanes(
        jnp.concatenate(d_logits + losses + [jnp.zeros((8 - 2 * tasks, lanes), F32)], axis=0)
    )

    halves = [0.5 * gate for gate in gates]
    d_gates = [[] for _ in range(tasks)]
    for e in range(experts):
        out = eo_s[e]
        d_out = None
        for t in range(tasks):
            d_gates[t].append(jnp.sum(d_mixed[t] * out, axis=0, keepdims=True))
            term = halves[t][e : e + 1, :] * d_mixed[t]
            d_out = term if d_out is None else d_out + term
        d_second = d_out * sl_s[e]
        small_ref[e * h2 : (e + 1) * h2, :] += fold_lanes(d_second)
        d_low = d_second.astype(BF)
        ds_ref[e * h2 : (e + 1) * h2, :] = d_low
        dwide_s[e * h1 : (e + 1) * h1, :] += dot(h_s[e * h1 : (e + 1) * h1, :], d_low, NT)

    d_all = []
    for t in range(tasks):
        d_gate = jnp.concatenate(d_gates[t], axis=0)
        d_all.append(gates[t] * (d_gate - jnp.sum(gates[t] * d_gate, axis=0, keepdims=True)))
    d_all = jnp.concatenate(d_all, axis=0)
    base = experts * h2 + 2 * tasks * tower
    small_ref[base : base + tasks * experts, :] += fold_lanes(d_all)
    dg_ref[...] = d_all.astype(BF)

    @pl.when(step == steps - 1)
    def _():
        dwide_ref[...] = dwide_s[...].astype(BF)


def expert_kernel(ds_ref, u_ref, wi_ref, own_ref, oth_ref, dg_ref, dpre_ref, dw_own_ref, dw_oth_ref, db_ref, dwg_ref):
    rows = u_ref.shape[1]
    h1 = u_ref.shape[0]
    bias = jnp.zeros((h1, LANES), F32)
    for at in range(0, rows, BLOCK):
        cols = slice(at, at + BLOCK)
        u = u_ref[:, cols].astype(F32)
        t = jnp.tanh(u)
        hidden = u + u * t
        d_pre = dot(wi_ref[0], ds_ref[:, cols]) * ((1.0 + hidden) + t * (1.0 - hidden))
        bias = bias + fold_lanes(d_pre)
        dpre_ref[:, cols] = d_pre.astype(BF)
    dw_own_ref[...] = dot(dpre_ref[...], own_ref[...], NT).astype(BF)
    dw_oth_ref[...] = dot(dpre_ref[...], oth_ref[...], NT).astype(BF)
    db_ref[...] = jnp.sum(bias.T, axis=0, keepdims=True)

    @pl.when(pl.program_id(0) == 0)
    def _():
        half = own_ref.shape[0]
        dwg_ref[:, :half] = dot(dg_ref[...], own_ref[...], NT)
        dwg_ref[:, half:] = dot(dg_ref[...], oth_ref[...], NT)


def feature_kernel(base_ref, ids_ref, dpre_ref, dg_ref, w_ref, wg_ref, dtab_ref, ddense_ref, acc_s):
    step, steps = pl.program_id(0), pl.num_programs(0)
    fields = ids_ref.shape[0]
    emb = 16
    lanes = ids_ref.shape[1]
    highs = acc_s.shape[1] // emb

    @pl.when(step == 0)
    def _():
        acc_s[...] = jnp.zeros_like(acc_s)

    d_feat = dot(w_ref[...], dpre_ref[...]) + dot(wg_ref[...], dg_ref[...], TN)
    ddense_ref[...] = d_feat[fields * emb :, :].astype(ddense_ref.dtype)
    places = lax.broadcasted_iota(jnp.int32, (LANES, lanes), 0)
    for f in range(fields):
        ids = ids_ref[f : f + 1, :]
        hot = jnp.where(places == jnp.bitwise_and(ids, LANES - 1), 1.0, 0.0).astype(BF)
        high = jnp.broadcast_to(jnp.right_shift(ids, 7), (emb, lanes))
        grad = d_feat[f * emb : (f + 1) * emb, :]
        spread = jnp.concatenate([jnp.where(high == h, grad, 0.0) for h in range(highs)], axis=0)
        acc_s[f] += dot(spread.astype(BF), hot, NT)

    @pl.when(step == steps - 1)
    def _():
        for f in range(fields):
            for h in range(highs):
                for s in range(2):
                    start = h * emb + s * 8
                    dtab_ref[s, h, f * 8 : (f + 1) * 8, :] = acc_s[f, start : start + 8, :].astype(BF)


def params():
    return pltpu.CompilerParams(vmem_limit_bytes=VMEM_LIMIT)


def whole(shape):
    return pl.BlockSpec(shape, lambda i, *_: (0,) * len(shape))


def here(rows):
    return pl.BlockSpec((rows, BLOCK), lambda i, *_: (0, i))


def shifted(rows, count):
    return pl.BlockSpec((rows, BLOCK), lambda i, j: (0, j[0] * count + i))


def sds(shape, dtype):
    return jax.ShapeDtypeStruct(shape, dtype)


def add_low(a, b):
    return (a.astype(F32) + b.astype(F32)).astype(BF)


def pick(value, bit, axis):
    return lax.dynamic_index_in_dim(value, bit, axis, keepdims=False)


def ordered(bit, mine, theirs, axis):
    return jnp.where(
        bit == 0,
        jnp.concatenate([mine, theirs], axis=axis),
        jnp.concatenate([theirs, mine], axis=axis),
    )


def scatter_bits(value, rank, first_bit):
    bit = first_bit
    while value.shape[0] > 1:
        value = value.reshape((value.shape[0] // 2, 2) + value.shape[1:])
        mine = jnp.bitwise_and(jnp.right_shift(rank, bit), 1)
        value = add_low(pick(value, mine, 1), swap(pick(value, 1 - mine, 1), "rows", 1 << bit))
        bit += 1
    return value[0]


def per_device(
    dense, ids, table, sizes, labels, w_expert, b_expert, w_gate, b_gate, w_inner, b_inner, w_tower, b_tower, w_head, b_head
):
    n_rows = lax.axis_size("rows")
    rank, j = lax.axis_index("rows"), lax.axis_index("field")
    core = jnp.bitwise_and(rank, 1)
    rows_all, fields = ids.shape
    rows = rows_all // 2
    blocks = rows // BLOCK
    vocab, emb = table.shape[1], table.shape[2]
    dense_cols = dense.shape[1]
    width, n_expert = w_expert.shape
    experts, h1, h2 = w_inner.shape
    tasks, tower = w_head.shape
    gates = tasks * experts
    row_bits = [1 << k for k in range(n_rows.bit_length() - 1)]

    ids_t, dense_t, labels_t = ids.T, dense.T, labels.T
    table_t = jnp.transpose(table, (0, 2, 1))
    wg_own = w_gate.T
    j_arr = j.reshape(1).astype(jnp.int32)

    away = (1 - j) * rows
    half_w = width // 2
    w_part = lax.dynamic_slice_in_dim(w_expert, core * half_w, half_w, axis=0)
    ids_oth = swap(lax.dynamic_slice_in_dim(ids_t, away, rows, axis=1), "field", 1)
    dense_oth = swap(lax.dynamic_slice_in_dim(dense_t, away, rows, axis=1), "field", 1)
    w_mine = swap(w_part, "field", 1)
    w_oth = ordered(core, w_mine, swap(w_mine, "rows", 1), 0)
    wg_oth = swap(wg_own, "field", 1)
    half_e = emb // 2
    t_mine = swap(lax.dynamic_slice_in_dim(table_t.astype(BF), core * half_e, half_e, axis=1), "field", 1)
    table_oth = ordered(core, t_mine, swap(t_mine, "rows", 1), 1).astype(F32)

    weight, rate = pl.pallas_call(
        weight_kernel,
        out_shape=(sds((1, rows_all), F32), sds((tasks, LANES), F32)),
        compiler_params=params(),
        name="row_weights",
    )(sizes, labels_t)
    for bit in row_bits:
        rate = rate + swap(rate, "rows", bit)

    def lanes_of(value):
        return jnp.broadcast_to(value.reshape(-1, 1).astype(F32), (value.size, LANES))

    feat_own, part, gpart = pl.pallas_call(
        first_kernel,
        grid_spec=pltpu.PrefetchScalarGridSpec(
            num_scalar_prefetch=1,
            grid=(blocks,),
            in_specs=[
                shifted(fields, blocks),
                shifted(dense_cols, blocks),
                whole((fields, emb, vocab)),
                whole((width, n_expert)),
                whole((gates, width)),
                whole((n_expert, LANES)),
            ],
            out_specs=[here(width), here(n_expert), here(gates)],
        ),
        out_shape=(sds((width, rows), BF), sds((n_expert, rows), BF), sds((gates, rows), F32)),
        compiler_params=params(),
        name="own_half",
    )(j_arr, ids_t, dense_t, table_t, w_expert, wg_own, lanes_of(0.5 * b_expert))

    wi_half = w_inner * jnp.asarray(0.5, BF)
    small_rows = experts * h2 + 2 * tasks * tower + gates + 8
    wide_rows = experts * h1 + tasks * tower
    feat_oth, u, d_second, d_gates, pred, d_wide, small = pl.pallas_call(
        functools.partial(middle_kernel, float(sizes.shape[1] * n_rows)),
        grid_spec=pltpu.PrefetchScalarGridSpec(
            num_scalar_prefetch=1,
            grid=(blocks,),
            in_specs=[
                whole((tasks, LANES)),
                here(fields),
                here(dense_cols),
                whole((fields, emb, vocab)),
                whole((width, n_expert)),
                whole((gates, width)),
                here(n_expert),
                here(gates),
                whole((gates, LANES)),
                whole((experts, h1, h2)),
                whole((experts * h2, LANES)),
                whole((tasks, tower, h2)),
                whole((tasks * tower, LANES)),
                whole((tasks * tower, LANES)),
                whole((tasks, LANES)),
                shifted(tasks, blocks),
                shifted(1, blocks),
            ],
            out_specs=[
                here(width),
                here(n_expert),
                here(experts * h2),
                here(gates),
                here(tasks),
                whole((wide_rows, h2)),
                whole((small_rows, LANES)),
            ],
            scratch_shapes=[
                pltpu.VMEM((n_expert, BLOCK), BF),
                pltpu.VMEM((experts, h2, BLOCK), F32),
                pltpu.VMEM((experts, h2, BLOCK), F32),
                pltpu.VMEM((wide_rows, h2), F32),
            ],
        ),
        out_shape=(
            sds((width, rows), BF),
            sds((n_expert, rows), BF),
            sds((experts * h2, rows), BF),
            sds((gates, rows), BF),
            sds((tasks, rows), F32),
            sds((wide_rows, h2), BF),
            sds((small_rows, LANES), F32),
        ),
        compiler_params=params(),
        name="middle",
    )(
        j_arr,
        rate,
        ids_oth,
        dense_oth,
        table_oth,
        w_oth,
        wg_oth,
        part,
        gpart,
        lanes_of(b_gate),
        wi_half,
        lanes_of(0.5 * b_inner),
        jnp.transpose(w_tower, (0, 2, 1)),
        lanes_of(b_tower),
        lanes_of(w_head),
        lanes_of(b_head),
        labels_t,
        weight,
    )

    full = lambda shape: pl.BlockSpec(shape, lambda e: (0,) * len(shape))
    d_pre, dw_own, dw_oth, d_b_expert, d_wg = pl.pallas_call(
        expert_kernel,
        grid=(experts,),
        in_specs=[
            pl.BlockSpec((h2, rows), lambda e: (e, 0)),
            pl.BlockSpec((h1, rows), lambda e: (e, 0)),
            pl.BlockSpec((1, h1, h2), lambda e: (e, 0, 0)),
            full((width, rows)),
            full((width, rows)),
            full((gates, rows)),
        ],
        out_specs=[
            pl.BlockSpec((h1, rows), lambda e: (e, 0)),
            pl.BlockSpec((h1, width), lambda e: (e, 0)),
            pl.BlockSpec((h1, width), lambda e: (e, 0)),
            pl.BlockSpec((1, h1), lambda e: (0, e)),
            full((gates, 2 * width)),
        ],
        out_shape=(
            sds((n_expert, rows), BF),
            sds((n_expert, width), BF),
            sds((n_expert, width), BF),
            sds((1, n_expert), F32),
            sds((gates, 2 * width), F32),
        ),
        compiler_params=params(),
        name="expert_back",
    )(d_second, u, wi_half, feat_own, feat_oth, d_gates)

    def features_back(base, ids_half, w_half, wg_half, dtype, name):
        highs = vocab // LANES
        return pl.pallas_call(
            feature_kernel,
            grid_spec=pltpu.PrefetchScalarGridSpec(
                num_scalar_prefetch=1,
                grid=(blocks,),
                in_specs=[
                    shifted(fields, blocks),
                    here(n_expert),
                    here(gates),
                    whole((width, n_expert)),
                    whole((gates, width)),
                ],
                out_specs=[whole((2, highs, fields * 8, LANES)), here(dense_cols)],
                scratch_shapes=[pltpu.VMEM((fields, highs * emb, LANES), F32)],
            ),
            out_shape=(sds((2, highs, fields * 8, LANES), BF), sds((dense_cols, rows), dtype)),
            compiler_params=params(),
            name=name,
        )(base, ids_half, d_pre, d_gates, w_half, wg_half)

    dt_oth, dd_oth = features_back(jnp.zeros((1,), jnp.int32), ids_oth, w_oth, wg_oth, BF, "features_back_other")
    dt_own, dd_own = features_back(j_arr, ids_t, w_expert, wg_own, F32, "features_back_own")

    def core_then_field(own, oth, axis):
        own = add_low(pick(own, core, axis), swap(pick(own, 1 - core, axis), "rows", 1))
        oth = add_low(pick(oth, core, axis), swap(pick(oth, 1 - core, axis), "rows", 1))
        return add_low(own, swap(oth, "field", 1))

    split = (n_rows // 2, 2, n_expert // n_rows, width)
    d_w = scatter_bits(core_then_field(dw_own.reshape(split), dw_oth.reshape(split), 1), rank, 1)
    d_w_expert = d_w.T.astype(F32)

    d_t = core_then_field(dt_own, dt_oth, 0)
    highs = d_t.shape[0]
    more = n_rows // 2 // highs
    if more > 1:
        d_t = d_t.reshape(highs, fields * 8, more, LANES // more)
        d_t = jnp.transpose(d_t, (0, 2, 1, 3)).reshape(highs * more, fields * 8, LANES // more)
    d_t = scatter_bits(d_t, rank, 1)
    part_w = d_t.shape[1] // 2
    keep = lax.dynamic_slice_in_dim(d_t, core * part_w, part_w, axis=1)
    give = lax.dynamic_slice_in_dim(d_t, (1 - core) * part_w, part_w, axis=1)
    split = (fields, 8, part_w)
    d_table = ordered(core, keep.reshape(split), swap(give, "rows", 1).reshape(split), 1)
    d_table = jnp.transpose(d_table, (0, 2, 1)).astype(F32)

    d_dense = ordered(j, dd_own, swap(dd_oth, "field", 1).astype(F32), 1).T
    predicted = ordered(j, pred, swap(pred, "field", 1), 1).T

    bits = [("rows", 1, core), ("field", 1, j), ("rows", 2, jnp.bitwise_and(jnp.right_shift(rank, 1), 1))]
    wide = d_wide
    for axis, bit, mine in bits:
        wide = wide.reshape(2, wide.shape[0] // 2, h2)
        wide = add_low(pick(wide, mine, 0), swap(pick(wide, 1 - mine, 0), axis, bit))
    for bit in row_bits[2:]:
        wide = add_low(wide, swap(wide, "rows", bit))
    for axis, bit, mine in reversed(bits):
        wide = ordered(mine, wide, swap(wide, axis, bit), 0)
    d_w_inner = wide[: experts * h1].astype(F32).reshape(experts, h1, h2)
    d_w_tower = jnp.transpose(wide[experts * h1 :].astype(F32).reshape(tasks, tower, h2), (0, 2, 1))

    small = jnp.sum(small, axis=1)
    small = small + swap(small, "field", 1)
    for bit in row_bits:
        small = small + swap(small, "rows", bit)
    cut = [experts * h2, tasks * tower, tasks * tower, gates, tasks, tasks]
    pieces, at = [], 0
    for size in cut:
        pieces.append(small[at : at + size])
        at += size
    d_b_inner, d_b_tower, d_w_head, d_b_gate, d_b_head, losses = pieces

    late = jnp.concatenate([d_wg[:, :width].reshape(-1), d_b_expert[0]])
    sent = jnp.concatenate([d_wg[:, width:].reshape(-1), d_b_expert[0]])
    late = late + swap(sent, "field", 1)
    for bit in row_bits:
        late = late + swap(late, "rows", bit)
    d_w_gate = late[: gates * width].reshape(gates, width).T
    d_b_expert = late[gates * width :]

    return (
        predicted,
        jnp.sum(losses),
        d_dense,
        d_table,
        d_w_expert,
        d_b_expert,
        d_w_gate,
        d_b_gate,
        d_w_inner,
        d_b_inner.reshape(experts, h2),
        d_w_tower,
        d_b_tower.reshape(tasks, tower),
        d_w_head.reshape(tasks, tower),
        d_b_head,
    )


def solution(mesh):
    return jax.shard_map(
        per_device,
        mesh=mesh,
        in_specs=(
            P("rows", "field"),
            P("rows", "field"),
            P("field", None, None),
            P("rows", None),
            P("rows", None),
            P("field", None),
            P(),
            P("field", None),
            P(),
            P(),
            P(),
            P(),
            P(),
            P(),
            P(),
        ),
        out_specs=(
            P("rows", None),
            P(),
            P("rows", "field"),
            P("field", "rows", None),
            P("field", "rows"),
            P(),
            P("field", None),
            P(),
            P(),
            P(),
            P(),
            P(),
            P(),
            P(),
        ),
        check_vma=False,
    )
```

```python
import functools

import jax
import jax.numpy as jnp
from jax import lax
from jax.experimental import pallas as pl
from jax.experimental.pallas import tpu as pltpu
from jax.sharding import PartitionSpec as P

BF = jnp.bfloat16
F32 = jnp.float32
LANES = 128

NN = (((1,), (0,)), ((), ()))
TN = (((0,), (0,)), ((), ()))
NT = (((1,), (1,)), ((), ()))


def dot(a, b, dims=NN):
    return lax.dot_general(a, b, dims, preferred_element_type=F32)


def swap(value, axis, bit):
    size = lax.axis_size(axis)
    return lax.ppermute(value, axis, [(i, i ^ bit) for i in range(size)])


def tile_lanes(column, lanes):
    return jnp.concatenate([column] * (lanes // LANES), axis=1)


def fold_lanes(value):
    total = value[:, :LANES]
    for start in range(LANES, value.shape[1], LANES):
        total = total + value[:, start : start + LANES]
    return total


def weight_kernel(sizes_ref, labels_ref, weight_ref, rate_ref):
    groups, rows = sizes_ref.shape[1], labels_ref.shape[1]
    sizes = jnp.broadcast_to(sizes_ref[...].astype(F32), (groups, groups))
    below = lax.broadcasted_iota(jnp.int32, (groups, groups), 0)
    across = lax.broadcasted_iota(jnp.int32, (groups, groups), 1)
    starts = jnp.sum(jnp.where(across < below, sizes, 0.0), axis=1, keepdims=True)
    own = jnp.sum(jnp.where(across == below, sizes, 0.0), axis=1, keepdims=True)
    ends = starts + own
    share = 1.0 / own
    rate = jnp.zeros((2, LANES), F32)
    for at in range(0, rows, 256):
        place = (lax.broadcasted_iota(jnp.int32, (groups, 256), 1) + at).astype(F32)
        inside = (place >= starts) & (place < ends)
        weight = jnp.sum(jnp.where(inside, share, 0.0), axis=0, keepdims=True)
        weight_ref[:, at : at + 256] = weight
        rate = rate + fold_lanes(weight * labels_ref[:, at : at + 256].astype(F32))
    rate_ref[...] = jnp.broadcast_to(jnp.sum(rate, axis=1, keepdims=True), rate_ref.shape)


def look_kernel(j_ref, ids_ref, *refs):
    dense_ref = refs[0] if len(refs) == 3 else None
    table_ref, feat_ref = refs[-2:]
    fields, emb, vocab = table_ref.shape
    rows = feat_ref.shape[1]
    lanes = 256

    def block(i, carry):
        source = pl.ds(pl.multiple_of(j_ref[0] * rows + i * lanes, lanes), lanes)
        target = pl.multiple_of(i * lanes, lanes)
        every = ids_ref[:, source]
        for f in range(fields):
            for at in range(0, lanes, LANES):
                ids = every[f : f + 1, at : at + LANES]
                low = jnp.broadcast_to(jnp.bitwise_and(ids, LANES - 1), (emb, LANES))
                high = jnp.broadcast_to(jnp.right_shift(ids, 7), (emb, LANES))
                found = None
                for h in range(vocab // LANES):
                    piece = table_ref[f, :, h * LANES : (h + 1) * LANES]
                    piece = jnp.take_along_axis(piece, low, axis=1, mode="promise_in_bounds")
                    found = piece if found is None else jnp.where(high == h, piece, found)
                feat_ref[f * emb : (f + 1) * emb, pl.ds(target + at, LANES)] = found.astype(BF)
        if dense_ref is not None:
            feat_ref[fields * emb :, pl.ds(target, lanes)] = dense_ref[:, source]
        return carry

    lax.fori_loop(0, rows // lanes, block, 0)


def partial_kernel(feat_ref, w_ref, wg_ref, bias_ref, part_ref, gpart_ref):
    rows = feat_ref.shape[1]
    lanes = chunk_of(rows, 768)

    def block(i, carry):
        cols = pl.ds(pl.multiple_of(i * lanes, lanes), lanes)
        half = feat_ref[:, cols] * jnp.asarray(0.5, BF)
        for at in range(0, w_ref.shape[1], 256):
            acc = dot(w_ref[:, at : at + 256], half, TN)
            part_ref[at : at + 256, cols] = (acc + tile_lanes(bias_ref[at : at + 256, :], lanes)).astype(BF)
        gpart_ref[:, cols] = dot(wg_ref[...], half)
        return carry

    lax.fori_loop(0, rows // lanes, block, 0)


def middle_kernel(
    groups_total,
    where_ref,
    rate_ref,
    own_ref,
    look_ref,
    dense_ref,
    w_ref,
    wg_ref,
    part_ref,
    gpart_ref,
    bg_ref,
    wi_ref,
    bi_ref,
    wt_ref,
    bt_ref,
    wh_ref,
    bh_ref,
    labels_ref,
    weight_ref,
    slope_ref,
    feat_ref,
    dg_ref,
    pred_ref,
    wide_keep_ref,
    wide_send_ref,
    sums_keep_ref,
    sums_send_ref,
    wide_ref,
    small_ref,
    hidden_ref,
    ds_ref,
    out_s,
    slope_s,
    dwt_s,
):
    rows = feat_ref.shape[1]
    lanes = out_s.shape[2]
    experts, h1, h2 = wi_ref.shape
    tasks, tower = wt_ref.shape[0], wt_ref.shape[1]
    one = jnp.asarray(1.0, BF)
    small_ref[...] = jnp.zeros_like(small_ref)
    dwt_s[...] = jnp.zeros_like(dwt_s)
    feat_ref[: look_ref.shape[0], :] = look_ref[...]
    feat_ref[look_ref.shape[0] :, :] = dense_ref[...]
    rate = rate_ref[...]
    click = (rate + 1.0) / (groups_total + 2.0)
    entropy = -(click * jnp.log(click) + (1.0 - click) * jnp.log(1.0 - click))
    scale = tile_lanes(1.0 / (groups_total * entropy), lanes)

    def block(i, carry):
        cols = pl.ds(pl.multiple_of(i * lanes, lanes), lanes)
        source = pl.ds(pl.multiple_of(where_ref[1] * rows + i * lanes, LANES), lanes)
        half = feat_ref[:, cols] * jnp.asarray(0.5, BF)
        gate_logits = 2.0 * (gpart_ref[:, cols] + dot(wg_ref[...], half)) + tile_lanes(bg_ref[...], lanes)
        gates = []
        for t in range(tasks):
            logits = gate_logits[t * experts : (t + 1) * experts]
            top = jnp.exp(logits - jnp.max(logits, axis=0, keepdims=True))
            gates.append(top / jnp.sum(top, axis=0, keepdims=True))
        mixed = [jnp.zeros((h2, lanes), F32) for _ in range(tasks)]
        for e in range(experts):
            at = e * h1
            u = dot(w_ref[:, at : at + h1], half, TN) + part_ref[at : at + h1, cols].astype(F32)
            t1 = jnp.tanh(u)
            hidden = (u + u * t1).astype(BF)
            hidden_ref[at : at + h1, cols] = hidden
            slope_ref[at : at + h1, cols] = (one + hidden) + t1.astype(BF) * (one - hidden)
            u2 = dot(wi_ref[e], hidden, TN) + tile_lanes(bi_ref[e * h2 : (e + 1) * h2, :], lanes)
            t2 = jnp.tanh(u2)
            out = u2 + u2 * t2
            out_s[e] = out
            slope_s[e] = (1.0 + out) + t2 * (1.0 - out)
            for t in range(tasks):
                mixed[t] = mixed[t] + gates[t][e : e + 1, :] * out
        labels = labels_ref[:, source].astype(F32)
        weight = weight_ref[:, source]
        preds, d_logits, losses, d_mixed = [], [], [], []
        for t in range(tasks):
            mine = slice(t * tower, (t + 1) * tower)
            low = mixed[t].astype(BF)
            tower_pre = dot(wt_ref[t], low) + tile_lanes(bt_ref[mine, :], lanes)
            sigma = 0.5 + 0.5 * jnp.tanh(0.5 * tower_pre)
            tower_out = (tower_pre * sigma).astype(BF).astype(F32)
            head = tile_lanes(wh_ref[mine, :], lanes)
            logit = jnp.sum(tower_out * head, axis=0, keepdims=True) + tile_lanes(bh_ref[t : t + 1, :], lanes)
            label = labels[t : t + 1]
            pred = jax.nn.sigmoid(logit)
            share = weight * scale[t : t + 1]
            plus = jnp.maximum(logit, 0.0) + jnp.log1p(jnp.exp(-jnp.abs(logit)))
            losses.append(share * (plus - label * logit))
            d_logit = share * (pred - label)
            preds.append(pred)
            d_logits.append(d_logit)
            d_tower = d_logit * head * (sigma * (1.0 + tower_pre * (1.0 - sigma)))
            d_low = d_tower.astype(BF)
            base = experts * h2
            small_ref[base + t * tower : base + (t + 1) * tower, :] += fold_lanes(d_tower)
            base = base + tasks * tower
            small_ref[base + t * tower : base + (t + 1) * tower, :] += fold_lanes(d_logit * tower_out)
            dwt_s[mine, :] += dot(d_low, low, NT)
            d_mixed.append(dot(wt_ref[t], d_low, TN))
        pred_ref[:, cols] = jnp.concatenate(preds, axis=0)
        base = experts * h2 + 2 * tasks * tower + tasks * experts
        small_ref[base : base + 8, :] += fold_lanes(
            jnp.concatenate(d_logits + losses + [jnp.zeros((8 - 2 * tasks, lanes), F32)], axis=0)
        )
        halves = [0.5 * gate for gate in gates]
        d_gates = [[] for _ in range(tasks)]
        for e in range(experts):
            out = out_s[e]
            d_out = None
            for t in range(tasks):
                d_gates[t].append(jnp.sum(d_mixed[t] * out, axis=0, keepdims=True))
                term = halves[t][e : e + 1, :] * d_mixed[t]
                d_out = term if d_out is None else d_out + term
            d_second = d_out * slope_s[e]
            small_ref[e * h2 : (e + 1) * h2, :] += fold_lanes(d_second)
            ds_ref[e * h2 : (e + 1) * h2, cols] = d_second.astype(BF)
        d_all = []
        for t in range(tasks):
            d_gate = jnp.concatenate(d_gates[t], axis=0)
            d_all.append(gates[t] * (d_gate - jnp.sum(gates[t] * d_gate, axis=0, keepdims=True)))
        d_all = jnp.concatenate(d_all, axis=0)
        base = experts * h2 + 2 * tasks * tower
        small_ref[base : base + tasks * experts, :] += fold_lanes(d_all)
        dg_ref[:, cols] = d_all.astype(BF)
        return carry

    lax.fori_loop(0, rows // lanes, block, 0)

    part, tail = experts * h1 // 4, tasks * tower // 4
    for e in range(experts):
        d_wi = dot(hidden_ref[e * h1 : (e + 1) * h1, :], ds_ref[e * h2 : (e + 1) * h2, :], NT).astype(BF)
        at = e * h1
        base = at // part * (part + tail) + at % part
        wide_ref[base : base + h1, :] = d_wi
    for q in range(4):
        base = q * (part + tail) + part
        wide_ref[base : base + tail, :] = dwt_s[q * tail : (q + 1) * tail, :].astype(BF)
    core = jnp.bitwise_and(where_ref[0], 1)
    count = 2 * (part + tail)
    wide_keep_ref[...] = wide_ref[pl.ds(pl.multiple_of(core * count, 32), count), :]
    wide_send_ref[...] = wide_ref[pl.ds(pl.multiple_of((1 - core) * count, 32), count), :]

    sums_keep_ref[...] = jnp.zeros_like(sums_keep_ref)
    whole = experts * h2 // LANES + 2 * tasks * tower // LANES
    for g in range(whole):
        sums_keep_ref[g : g + 1, :] = jnp.sum(small_ref[g * LANES : (g + 1) * LANES, :].T, axis=0, keepdims=True)
    left = small_ref.shape[0] - whole * LANES
    sums_keep_ref[whole : whole + 1, :left] = jnp.sum(small_ref[whole * LANES :, :].T, axis=0, keepdims=True)
    step = chunk_of(rows, 768)
    for e in range(experts):
        r1, r2 = slice(e * h1, (e + 1) * h1), slice(e * h2, (e + 1) * h2)
        bias = jnp.zeros((h1, LANES), F32)
        for at in range(0, rows, step):
            cols = slice(at, at + step)
            d_pre = dot(wi_ref[e], ds_ref[r2, cols]) * slope_ref[r1, cols].astype(F32)
            bias = bias + fold_lanes(d_pre)
            slope_ref[r1, cols] = d_pre.astype(BF)
        row = jnp.sum(bias.T, axis=0, keepdims=True)
        for m in range(h1 // LANES):
            at = 16 + e * (h1 // LANES) + m
            sums_keep_ref[at : at + 1, :] = row[:, m * LANES : (m + 1) * LANES]
    sums_send_ref[...] = sums_keep_ref[...]
    for source, target in ((own_ref, sums_keep_ref), (feat_ref, sums_send_ref)):
        d_wg = dot(dg_ref[...], source[...], NT)
        for m in range(d_wg.shape[1] // LANES):
            target[32 + m * 16 : 48 + m * 16, :] = d_wg[:, m * LANES : (m + 1) * LANES]


def first_weight_kernel(where_ref, dpre_ref, own_ref, oth_ref, keep_ref, send_ref, _):
    even = jnp.bitwise_and(where_ref[0], 1) == 0
    for at in range(0, dpre_ref.shape[0], 2 * LANES):
        for side, source in enumerate((own_ref, oth_ref)):
            d_w = dot(source[...], dpre_ref[at : at + 2 * LANES, :], NT)
            first, second = d_w[:, :LANES], d_w[:, LANES:]
            keep_ref[side, at // (2 * LANES)] = jnp.where(even, first, second).astype(BF)
            send_ref[side, at // (2 * LANES)] = jnp.where(even, second, first).astype(BF)


def feature_kernel(part, parts, where_ref, base_ref, ids_ref, dpre_ref, dg_ref, w_ref, wg_ref, *refs):
    fields, emb = ids_ref.shape[0], 16
    rows = dg_ref.shape[1]
    lanes = chunk_of(rows, 1152)
    carried = refs[0] if part > 0 else None
    if part > 0:
        refs = refs[2:]
    if part == parts - 1:
        keep_ref, send_ref, ddense_ref, _, acc_s = refs
    else:
        acc_s, ddense_ref, _ = refs
    highs = acc_s.shape[1] // emb
    acc_s[...] = jnp.zeros_like(acc_s) if carried is None else carried[...]

    def block(i, carry):
        cols = pl.ds(pl.multiple_of(i * lanes, lanes), lanes)
        source = pl.ds(pl.multiple_of(base_ref[0] * rows + i * lanes, LANES), lanes)
        d_feat = dot(w_ref[...], dpre_ref[:, cols]) + dot(wg_ref[...], dg_ref[:, cols], TN)
        ddense_ref[:, cols] = d_feat[fields * emb :, :].astype(ddense_ref.dtype)
        every = ids_ref[:, source]
        low = jnp.bitwise_and(every, LANES - 1)
        every = jnp.right_shift(every, 7)
        places = lax.broadcasted_iota(jnp.int32, (LANES, lanes), 0)
        for f in range(fields):
            hot = jnp.where(places == low[f : f + 1, :], 1.0, 0.0).astype(BF)
            high = jnp.broadcast_to(every[f : f + 1, :], (emb, lanes))
            grad = d_feat[f * emb : (f + 1) * emb, :]
            spread = jnp.concatenate([jnp.where(high == h, grad, 0.0) for h in range(highs)], axis=0)
            acc_s[f] += dot(spread.astype(BF), hot, NT)
        return carry

    steps = rows // lanes
    lax.fori_loop(steps * part // parts, steps * (part + 1) // parts, block, 0)
    if part < parts - 1:
        return
    even = jnp.bitwise_and(where_ref[0], 1) == 0
    left = lax.broadcasted_iota(jnp.int32, (emb, LANES), 1) < LANES // 2
    for p in range((fields + 1) // 2):
        rows_p = slice(p * emb, (p + 1) * emb)
        for h in range(highs):
            a = acc_s[2 * p, h * emb : (h + 1) * emb, :]
            b = acc_s[2 * p + 1, h * emb : (h + 1) * emb, :] if 2 * p + 1 < fields else jnp.zeros_like(a)
            first = jnp.where(left, a, pltpu.roll(b, LANES // 2, 1))
            second = jnp.where(left, pltpu.roll(a, LANES // 2, 1), b)
            keep_ref[h, rows_p, :] = jnp.where(even, first, second).astype(BF)
            send_ref[h, rows_p, :] = jnp.where(even, second, first).astype(BF)


def step_kernel(works, counts, where_ref, *refs):
    def bit(k):
        return jnp.bitwise_and(jnp.right_shift(where_ref[0], k), 1)

    ins = sum(n for n, _ in counts)
    a, b = 0, ins
    for work, (n_in, n_out) in zip(works, counts):
        work(refs[a : a + n_in], refs[b : b + n_out], bit, where_ref)
        a, b = a + n_in, b + n_out


def total(a, b, at):
    return a[at].astype(F32) + b[at].astype(F32)


def work_sum(ins, outs, bit, where):
    outs[0][...] = total(ins[0], ins[1], ...).astype(outs[0].dtype)


def work_sides(ins, outs, bit, where):
    for side in range(2):
        outs[side][...] = total(ins[0], ins[1], side).astype(outs[side].dtype)


def work_rows(ins, outs, bit, where):
    count = outs[0].shape[0]
    for out, half in ((outs[0], where[1]), (outs[1], 1 - where[1])):
        out[...] = total(ins[0], ins[1], pl.ds(pl.multiple_of(half * count, 32), count)).astype(out.dtype)


def work_halve(k):
    def work(ins, outs, bit, where):
        for out, half in ((outs[0], bit(k)), (outs[1], 1 - bit(k))):
            for n in range(out.shape[0]):
                out[n] = total(ins[0], ins[1], 2 * n + half).astype(out.dtype)

    return work


def work_three(ins, outs, bit, where):
    for out, half in ((outs[0], bit(1)), (outs[1], 1 - bit(1))):
        for n in range(out.shape[0]):
            at = 2 * n + half
            out[n] = (total(ins[0], ins[1], at) + ins[2][at].astype(F32)).astype(out.dtype)


def work_two_ways(ins, outs, bit, where):
    half = ins[0].shape[1] // 2
    for side in range(2):
        for n in range(half):
            outs[side][n] = total(ins[0], ins[1], (side, n)).astype(BF)
    for out, which in ((outs[2], bit(1)), (outs[3], 1 - bit(1))):
        for side in range(2):
            for n in range(half // 2):
                out[side, n] = total(ins[0], ins[1], (side, half + 2 * n + which)).astype(BF)


def work_join_halves(ins, outs, bit, where):
    for n in range(2):
        recv, mine = ins[2 * n], ins[2 * n + 1]
        outs[0][n] = total(recv, mine, bit(2)).astype(BF)
        outs[1][n] = total(recv, mine, 1 - bit(2)).astype(BF)


def work_last_bit(ins, outs, bit, where):
    outs[0][...] = total(ins[0], ins[1], bit(3)).astype(BF)
    outs[1][...] = total(ins[0], ins[1], 1 - bit(3)).astype(BF)


def chunk_of(rows, most):
    lanes = LANES
    for size in range(LANES, most + 1, LANES):
        if rows % size == 0:
            lanes = size
    return lanes


def sds(shape, dtype):
    return jax.ShapeDtypeStruct(shape, dtype)


def pinned(shape, dtype):
    return pltpu.VMEM(shape, dtype)


def run(kernel, name, outs, args, us, scalars=0, scratch=(), mib=16, alias=None, after=()):
    vmem, smem = pl.BlockSpec(memory_space=pltpu.VMEM), pl.BlockSpec(memory_space=pltpu.SMEM)
    count = len(args)

    def body(*refs):
        kernel(*refs[:count], *refs[count + len(after) :])

    return pl.pallas_call(
        body,
        in_specs=[smem] * scalars + [vmem] * (count - scalars) + [pl.BlockSpec(memory_space=pl.ANY)] * len(after),
        out_specs=[vmem] * len(outs),
        out_shape=list(outs),
        scratch_shapes=list(scratch),
        input_output_aliases=alias or {},
        compiler_params=pltpu.CompilerParams(vmem_limit_bytes=mib * 1024 * 1024),
        cost_estimate=pl.CostEstimate(flops=int(us * 1.0e9), bytes_accessed=0, transcendentals=0),
        name=name,
    )(*args, *after)


def take_step(name, where, items):
    ins = [value for item in items for value in item[1]]
    outs = [shape for item in items for shape in item[2]]
    counts = [(len(item[1]), len(item[2])) for item in items]
    kernel = functools.partial(step_kernel, [item[0] for item in items], counts)
    got = run(kernel, name, outs, [where] + ins, 1.0, 1, mib=6)
    split, at = [], 0
    for _, count in counts:
        split.append(list(got[at : at + count]) if count > 1 else got[at])
        at += count
    return split


def add_low(a, b):
    return (a.astype(F32) + b.astype(F32)).astype(BF)


def pick(value, bit, axis):
    return lax.dynamic_index_in_dim(value, bit, axis, keepdims=False)


def ordered(bit, mine, theirs, axis):
    return jnp.where(
        bit == 0,
        jnp.concatenate([mine, theirs], axis=axis),
        jnp.concatenate([theirs, mine], axis=axis),
    )


def bit_of(rank, k):
    return jnp.bitwise_and(jnp.right_shift(rank, k), 1)


def keep_half(value, rank, k, axis):
    mine = bit_of(rank, k)
    return add_low(pick(value, mine, axis), swap(pick(value, 1 - mine, axis), "rows", 1 << k))


def keep_bits(value, rank, first, last):
    for k in range(first, last):
        value = value.reshape((value.shape[0] // 2, 2) + value.shape[1:])
        value = keep_half(value, rank, k, 1)
    return value


def per_device(
    dense, ids, table, sizes, labels, w_expert, b_expert, w_gate, b_gate, w_inner, b_inner, w_tower, b_tower, w_head, b_head
):
    n_rows = lax.axis_size("rows")
    n_bits = n_rows.bit_length() - 1
    rank, j = lax.axis_index("rows"), lax.axis_index("field")
    core = bit_of(rank, 0)
    rows_all, fields = ids.shape
    rows = rows_all // 2
    vocab, emb = table.shape[1], table.shape[2]
    dense_cols = dense.shape[1]
    width, n_expert = w_expert.shape
    experts, h1, h2 = w_inner.shape
    tasks, tower = w_head.shape
    gates = tasks * experts

    ids_t, dense_t, labels_t = ids.T, dense.T, labels.T
    table_t = jnp.transpose(table, (0, 2, 1))
    wg_own = w_gate.T
    j_arr = j.reshape(1).astype(jnp.int32)
    zero = jnp.zeros((1,), jnp.int32)
    where = jnp.stack([rank, j]).astype(jnp.int32)
    fast = n_rows * LANES == n_expert and n_rows * LANES == 2 * vocab
    if not fast:
        where = where * jnp.asarray([0, 1], jnp.int32)

    away = (1 - j) * rows
    second = bit_of(rank, 1)
    quarter = 2 * core + second

    def quarter_of(value):
        return pick(value.reshape((4, value.shape[0] // 4) + value.shape[1:]), quarter, 0)

    def joined(value):
        value = ordered(second, value, swap(value, "rows", 2), 0)
        return value, ordered(core, value, swap(value, "rows", 1), 0)

    w_mine = swap(quarter_of(w_expert), "field", 1)
    t_mine = swap(quarter_of(table_t.reshape(fields * emb, vocab)).astype(BF), "field", 1)
    ids_oth = swap(lax.dynamic_slice_in_dim(ids_t, away, rows, axis=1), "field", 1)
    dense_oth = swap(lax.dynamic_slice_in_dim(dense_t, away, rows, axis=1), "field", 1)
    wg_oth = swap(wg_own, "field", 1)
    w_some, w_oth = joined(w_mine)
    t_some, table_oth = joined(t_mine)
    table_oth = table_oth.astype(F32).reshape(fields, emb, vocab)

    weight, rate = run(
        weight_kernel, "row_weights", [sds((1, rows_all), F32), sds((tasks, LANES), F32)], [sizes, labels_t], 1.0
    )
    rates = [rate]
    for k in range(n_bits):
        rates.append(rates[-1] + swap(rates[-1], "rows", 1 << k))
    rate = rates[-1]

    def lanes_of(value):
        return jnp.broadcast_to(value.reshape(-1, 1).astype(F32), (value.size, LANES))

    feat = pinned((width, rows), BF)
    (feat_own,) = run(look_kernel, "look_own", [feat], [j_arr, ids_t, dense_t, table_t], 3.4, 1)
    part, gpart = run(
        partial_kernel,
        "own_share",
        [pinned((n_expert, rows), BF), sds((gates, rows), F32)],
        [feat_own, w_expert, wg_own, lanes_of(0.5 * b_expert)],
        3.2,
        after=[rates[1], w_mine],
    )
    (look_oth,) = run(
        look_kernel,
        "look_other",
        [pinned((fields * emb, rows), BF)],
        [zero, ids_oth, table_oth],
        3.4,
        1,
        after=[w_some, rates[2]],
    )

    wi_half = w_inner * jnp.asarray(0.5, BF)
    wide_rows = experts * h1 + tasks * tower
    small_rows = experts * h2 + 2 * tasks * tower + gates + 8
    lanes = chunk_of(rows, 1152)
    d_pre, feat_oth, d_gates, pred, wide_keep, wide_send, sums_keep, sums_send = run(
        functools.partial(middle_kernel, float(sizes.shape[1] * n_rows)),
        "middle",
        [
            pinned((n_expert, rows), BF),
            feat,
            sds((gates, rows), BF),
            sds((tasks, rows), F32),
            sds((wide_rows // 2, h2), BF),
            sds((wide_rows // 2, h2), BF),
            sds((64, LANES), F32),
            sds((64, LANES), F32),
        ],
        [
            where,
            rate,
            feat_own,
            look_oth,
            dense_oth,
            w_oth,
            wg_oth,
            part,
            gpart,
            lanes_of(b_gate),
            wi_half,
            lanes_of(0.5 * b_inner),
            jnp.transpose(w_tower, (0, 2, 1)),
            lanes_of(b_tower),
            lanes_of(w_head),
            lanes_of(b_head),
            labels_t,
            weight,
        ],
        21.0,
        1,
        [
            pltpu.VMEM((wide_rows, h2), BF),
            pltpu.VMEM((small_rows, LANES), F32),
            pltpu.VMEM((n_expert, rows), BF),
            pltpu.VMEM((experts * h2, rows), BF),
            pltpu.VMEM((experts, h2, lanes), F32),
            pltpu.VMEM((experts, h2, lanes), F32),
            pltpu.VMEM((tasks * tower, h2), F32),
        ],
        mib=36,
        alias={7: 0},
    )

    held = pinned((n_expert, rows), BF)
    blocks = n_expert // LANES // 2
    deep = (fields + 1) // 2 * emb
    highs = vocab // LANES
    flat = sds((wide_rows // 4, h2), BF)
    sums_s = sds((64, LANES), F32)

    def blocks_s(*shape):
        return sds(shape + (width, LANES), BF)

    def planes_s(count):
        return sds((count, deep, LANES), BF)

    def features_back(part, parts, base, ids_half, d_pre, w_half, wg_half, carried, dtype, name, after):
        outs = [sds((dense_cols, rows), dtype), held]
        scratch = [pltpu.VMEM((fields, highs * emb, LANES), F32)]
        if part == parts - 1:
            outs = [planes_s(highs), planes_s(highs)] + outs
        else:
            outs, scratch = [sds((fields, highs * emb, LANES), F32)] + outs, []
        alias = {3: len(outs) - 1}
        if part > 0:
            alias[8] = len(outs) - 2
        return run(
            functools.partial(feature_kernel, part, parts),
            name,
            outs,
            [where, base, ids_half, d_pre, d_gates, w_half, wg_half] + carried,
            6.5 / parts,
            2,
            scratch,
            alias=alias,
            after=after,
        )

    def over_rows(value, bit):
        return swap(value, "rows", bit)

    pred_got = swap(pred, "field", 1)
    wide_got = over_rows(wide_send, 1)
    sums_got = swap(sums_send, "field", 1)
    dw_keep, dw_send, d_pre = run(
        first_weight_kernel,
        "first_weights",
        [blocks_s(2, blocks), blocks_s(2, blocks), held],
        [where, d_pre, feat_own, feat_oth],
        5.5,
        1,
        alias={1: 2},
    )
    predicted = ordered(j, pred, pred_got, 1).T
    if fast:
        dw_got = over_rows(dw_send, 1)
        (wide_keep, wide_send), sums = take_step(
            "step_1",
            where,
            [
                (work_rows, [wide_got, wide_keep], [flat, flat]),
                (work_sum, [sums_got, sums_keep], [sums_s]),
            ],
        )
        wide_got = swap(wide_send, "field", 1)
        sums_got = over_rows(sums, 1)
        after = [sums]
    else:
        after = []
    dt_keep, dt_send, dd_oth, d_pre = features_back(
        0, 1, zero, ids_oth, d_pre, w_oth, wg_oth, [], BF, "features_other", after
    )
    if fast:
        dt_got = over_rows(dt_send, 1)
        (a_keep, a_send, b_keep, b_send), wide, sums = take_step(
            "step_2",
            where,
            [
                (work_two_ways, [dw_got, dw_keep], [blocks_s(4), blocks_s(4), blocks_s(2, 2), blocks_s(2, 2)]),
                (work_sum, [wide_got, wide_keep], [flat]),
                (work_sum, [sums_got, sums], [sums_s]),
            ],
        )
        a_got = swap(a_send, "field", 1)
        b_got = over_rows(b_send, 2)
        wide_got = over_rows(wide, 2)
        sums_got = over_rows(sums, 2)
        after = [sums]
    dd_got = swap(dd_oth, "field", 1)
    acc, dd_own, d_pre = features_back(
        0, 2, j_arr, ids_t, d_pre, w_expert, wg_own, [], F32, "features_own_0", after
    )
    if fast:
        dt_oth, wide, sums = take_step(
            "step_3",
            where,
            [
                (work_sum, [dt_got, dt_keep], [planes_s(highs)]),
                (work_sum, [wide_got, wide], [flat]),
                (work_sum, [sums_got, sums], [sums_s]),
            ],
        )
        dt_far = swap(dt_oth, "field", 1)
        wide_got = over_rows(wide, 4)
        sums_got = over_rows(sums, 4)
        after = [dt_oth]
    do_keep, do_send, dd_own, _ = features_back(
        1, 2, j_arr, ids_t, d_pre, w_expert, wg_own, [acc, dd_own], F32, "features_own_1", after
    )
    d_dense = ordered(j, dd_own, dd_got.astype(F32), 1).T
    if fast:
        do_got = over_rows(do_send, 1)
        (a_keep, a_send), (b_keep, b_send), wide, sums = take_step(
            "step_4",
            where,
            [
                (work_halve(1), [a_got, a_keep], [blocks_s(2), blocks_s(2)]),
                (work_sides, [b_got, b_keep], [blocks_s(2), blocks_s(2)]),
                (work_sum, [wide_got, wide], [flat]),
                (work_sum, [sums_got, sums], [sums_s]),
            ],
        )
        a_got = over_rows(a_send, 2)
        b_got = swap(b_send, "field", 1)
        wide_got = over_rows(wide, 8)
        sums_got = over_rows(sums, 8)
        ((d_keep, d_send),) = take_step(
            "step_5", where, [(work_three, [do_got, do_keep, dt_far], [planes_s(highs // 2), planes_s(highs // 2)])]
        )
        d_got = over_rows(d_send, 2)
        (c_keep, c_send), wide, sums = take_step(
            "step_6",
            where,
            [
                (work_join_halves, [a_got, a_keep, b_got, b_keep], [blocks_s(2), blocks_s(2)]),
                (work_sum, [wide_got, wide], [flat]),
                (work_sum, [sums_got, sums], [sums_s]),
            ],
        )
        c_got = over_rows(c_send, 4)
        wide = ordered(j, wide, swap(wide, "field", 1), 0)
        ((d_keep, d_send),) = take_step(
            "step_7", where, [(work_halve(2), [d_got, d_keep], [planes_s(highs // 4), planes_s(highs // 4)])]
        )
        d_got = over_rows(d_send, 4)
        ((c_keep, c_send),) = take_step(
            "step_8", where, [(work_last_bit, [c_got, c_keep], [blocks_s(), blocks_s()])]
        )
        c_got = over_rows(c_send, 8)
        wide = ordered(core, wide, over_rows(wide, 1), 0)
        ((d_keep, d_send),) = take_step(
            "step_9", where, [(work_halve(3), [d_got, d_keep], [planes_s(1), planes_s(1)])]
        )
        d_got = over_rows(d_send, 8)
        d_w_expert = c_keep.astype(F32) + c_got.astype(F32)
        d_t = d_keep.astype(F32) + d_got.astype(F32)
        d_t = d_t.reshape(deep // emb, emb, 2, LANES // 2)
        d_table = jnp.transpose(d_t, (0, 2, 3, 1)).reshape(deep // emb * 2, LANES // 2, emb)[:fields]
    else:

        def tables(keep, send):
            value = jnp.stack([keep, send], axis=1).reshape(highs, 2, deep // emb, emb, 2, LANES // 2)
            return jnp.transpose(value, (2, 4, 3, 0, 1, 5)).reshape(deep // emb * 2, emb, vocab)[:fields]

        d_t = add_low(tables(do_keep, do_send), swap(tables(dt_keep, dt_send), "field", 1)).astype(F32)
        d_table = jnp.transpose(lax.psum_scatter(d_t, "rows", scatter_dimension=2, tiled=True), (0, 2, 1))
        d_w = jnp.stack([dw_keep, dw_send], axis=2).reshape(2, 2 * blocks, width, LANES)
        d_w = add_low(d_w[0], swap(d_w[1], "field", 1)).astype(F32)
        d_w = jnp.transpose(d_w, (1, 0, 2)).reshape(width, n_expert)
        d_w_expert = lax.psum_scatter(d_w, "rows", scatter_dimension=1, tiled=True)
        wide = jnp.concatenate([wide_keep, wide_send], axis=0)
        wide = add_low(wide, swap(wide, "field", 1))
        sums = sums_keep + sums_got
        for k in range(n_bits):
            wide = add_low(wide, over_rows(wide, 1 << k))
            sums = sums + over_rows(sums, 1 << k)

    wide = wide.astype(F32).reshape(4, wide_rows // 4, h2)
    cut = experts * h1 // 4
    d_w_inner = wide[:, :cut].reshape(experts, h1, h2)
    d_w_tower = jnp.transpose(wide[:, cut:].reshape(tasks, tower, h2), (0, 2, 1))
    d_b_inner = sums[: experts * h2 // LANES].reshape(experts, h2)
    d_b_tower, d_w_head, scalars = sums[8], sums[9], sums[10]
    d_b_gate, d_b_head, losses = scalars[:gates], scalars[gates : gates + tasks], scalars[gates + tasks : gates + 2 * tasks]
    d_b_expert = sums[16:32].reshape(n_expert)
    d_w_gate = jnp.concatenate([sums[32:48], sums[48:64]], axis=1)

    return (
        predicted,
        jnp.sum(losses),
        d_dense,
        d_table,
        d_w_expert,
        d_b_expert,
        d_w_gate.T,
        d_b_gate,
        d_w_inner,
        d_b_inner,
        d_w_tower,
        d_b_tower.reshape(tasks, tower),
        d_w_head.reshape(tasks, tower),
        d_b_head,
    )


def solution(mesh):
    return jax.shard_map(
        per_device,
        mesh=mesh,
        in_specs=(
            P("rows", "field"),
            P("rows", "field"),
            P("field", None, None),
            P("rows", None),
            P("rows", None),
            P("field", None),
            P(),
            P("field", None),
            P(),
            P(),
            P(),
            P(),
            P(),
            P(),
            P(),
        ),
        out_specs=(
            P("rows", None),
            P(),
            P("rows", "field"),
            P("field", "rows", None),
            P("field", "rows"),
            P(),
            P("field", None),
            P(),
            P(),
            P(),
            P(),
            P(),
            P(),
            P(),
        ),
        check_vma=False,
    )
```

```python
import functools

import jax
import jax.numpy as jnp
from jax import lax
from jax.experimental import pallas as pl
from jax.experimental.pallas import tpu as pltpu
from jax.sharding import PartitionSpec as P

BF = jnp.bfloat16
F32 = jnp.float32
LANES = 128
SCALE = 1.0e9
UNP = 2.0
FW, FB, ST = 0.5, 0.5, 0.3
LO = 4.0
RQ = 0.1

NN = (((1,), (0,)), ((), ()))
TN = (((0,), (0,)), ((), ()))
NT = (((1,), (1,)), ((), ()))


def dot(a, b, dims=NN):
    return lax.dot_general(a, b, dims, preferred_element_type=F32)


def swap(value, axis, bit):
    size = lax.axis_size(axis)
    return lax.ppermute(value, axis, [(i, i ^ bit) for i in range(size)])


def columns_of(row):
    return jnp.broadcast_to(row, (LANES, LANES)).T


def tile_lanes(column, lanes):
    return jnp.concatenate([column] * (lanes // LANES), axis=1)


def fold_lanes(value):
    total = value[:, :LANES]
    for start in range(LANES, value.shape[1], LANES):
        total = total + value[:, start : start + LANES]
    return total


def pack_kernel(
    where_ref,
    w_ref,
    table_ref,
    wg_ref,
    ids_ref,
    dense_ref,
    sizes_ref,
    labels_ref,
    first_ref,
    second_ref,
    rows_ref,
    weight_ref,
    rate_ref,
    table_s,
    wg_s,
    ids_s,
    sizes_s,
    labels_s,
    sems,
):
    quarter = jnp.bitwise_and(where_ref[0], 3)
    fields, emb, vocab = table_ref.shape
    lanes = table_s.shape[2]
    dense_cols, rows = dense_ref.shape[0], rows_ref.shape[1]
    some, count = w_ref.shape[0] // 4 - second_ref.shape[0], w_ref.shape[0] // 4
    away = pl.ds(pl.multiple_of((1 - where_ref[1]) * rows, LANES), rows)
    base = pl.multiple_of(quarter * count, 16)
    copies = [
        pltpu.make_async_copy(w_ref.at[pl.ds(base, some), :], first_ref.at[:some, :], sems.at[0]),
        pltpu.make_async_copy(w_ref.at[pl.ds(base + some, count - some), :], second_ref, sems.at[1]),
        pltpu.make_async_copy(
            table_ref.at[:, :, pl.ds(pl.multiple_of(quarter * lanes, LANES), lanes)], table_s, sems.at[2]
        ),
        pltpu.make_async_copy(wg_ref, wg_s, sems.at[3]),
        pltpu.make_async_copy(ids_ref.at[:, away], ids_s, sems.at[4]),
        pltpu.make_async_copy(dense_ref.at[:, away], rows_ref.at[:dense_cols, :], sems.at[5]),
        pltpu.make_async_copy(sizes_ref, sizes_s, sems.at[6]),
        pltpu.make_async_copy(labels_ref, labels_s, sems.at[7]),
    ]
    for copy in copies:
        copy.start()
    for copy in copies:
        copy.wait()
    sizes_ref, labels_ref = sizes_s, labels_s
    for f in range(fields):
        at = some + f % 2 * emb
        first_ref[at : at + emb, f // 2 * lanes : (f // 2 + 1) * lanes] = table_s[f].astype(BF)
    at = some + fields % 2 * emb
    first_ref[at : at + emb, fields // 2 * lanes : (fields // 2 + 1) * lanes] = wg_s[...]
    first_ref[some:, (fields // 2 + 1) * lanes :] = jnp.zeros_like(first_ref[some:, (fields // 2 + 1) * lanes :])
    ids = ids_s[...]
    value = (jnp.bitwise_and(ids, 127) + 128).astype(F32)
    for k in range(3):
        up = float(1 << (1 << k))
        value = value * jnp.where(jnp.bitwise_and(jnp.right_shift(ids, 7 + k), 1) == 1, up, 1.0)
    rows_ref[dense_cols : dense_cols + fields, :] = value.astype(BF)
    rows_ref[dense_cols + fields :, :] = jnp.zeros_like(rows_ref[dense_cols + fields :, :])
    groups, rows = sizes_ref.shape[1], labels_ref.shape[1]
    sizes = jnp.broadcast_to(sizes_ref[...].astype(F32), (groups, groups))
    below = lax.broadcasted_iota(jnp.int32, (groups, groups), 0)
    across = lax.broadcasted_iota(jnp.int32, (groups, groups), 1)
    starts = jnp.sum(jnp.where(across < below, sizes, 0.0), axis=1, keepdims=True)
    own = jnp.sum(jnp.where(across == below, sizes, 0.0), axis=1, keepdims=True)
    ends = starts + own
    share = 1.0 / own
    rate = jnp.zeros((2, LANES), F32)
    for at in range(0, rows, 256):
        place = (lax.broadcasted_iota(jnp.int32, (groups, 256), 1) + at).astype(F32)
        inside = (place >= starts) & (place < ends)
        weight = jnp.sum(jnp.where(inside, share, 0.0), axis=0, keepdims=True)
        weight_ref[:, at : at + 256] = weight
        rate = rate + fold_lanes(weight * labels_ref[:, at : at + 256].astype(F32))
    rate_ref[...] = jnp.broadcast_to(jnp.sum(rate, axis=1, keepdims=True), rate_ref.shape)


def look_up(ids_ref, first, table_ref, feat_ref, rows, dense_ref=None):
    fields, emb, vocab = table_ref.shape
    lanes = 256

    def block(i, carry):
        source = pl.ds(pl.multiple_of(first + i * lanes, lanes), lanes)
        target = pl.multiple_of(i * lanes, lanes)
        every = ids_ref[:, source]
        for f in range(fields):
            for at in range(0, lanes, LANES):
                ids = every[f : f + 1, at : at + LANES]
                low = jnp.broadcast_to(jnp.bitwise_and(ids, LANES - 1), (emb, LANES))
                high = jnp.broadcast_to(jnp.right_shift(ids, 7), (emb, LANES))
                found = None
                for h in range(vocab // LANES):
                    piece = table_ref[f, :, h * LANES : (h + 1) * LANES]
                    piece = jnp.take_along_axis(piece, low, axis=1, mode="promise_in_bounds")
                    found = piece if found is None else jnp.where(high == h, piece, found)
                feat_ref[f * emb : (f + 1) * emb, pl.ds(target + at, LANES)] = found.astype(BF)
        if dense_ref is not None:
            feat_ref[fields * emb :, pl.ds(target, lanes)] = dense_ref[:, source]
        return carry

    lax.fori_loop(0, rows // lanes, block, 0)


def look_own_kernel(
    where_ref, ids_ref, dense_ref, table_ref, w_in, wg_in, bias_in, feat_ref, w_ref, wg_ref, bias_ref, ids_s, table_s, sems
):
    rows = feat_ref.shape[1]
    fields, emb, _ = table_ref.shape
    mine = pl.ds(pl.multiple_of(where_ref[1] * rows, LANES), rows)
    copies = [
        pltpu.make_async_copy(ids_ref.at[:, mine], ids_s, sems.at[0]),
        pltpu.make_async_copy(table_ref, table_s, sems.at[1]),
        pltpu.make_async_copy(dense_ref.at[:, mine], feat_ref.at[fields * emb :, :], sems.at[2]),
        pltpu.make_async_copy(bias_in, bias_ref, sems.at[3]),
        pltpu.make_async_copy(wg_in, wg_ref, sems.at[4]),
        pltpu.make_async_copy(w_in, w_ref, sems.at[5]),
    ]
    for copy in copies:
        copy.start()
    for copy in copies[:2]:
        copy.wait()
    look_up(ids_s, 0, table_s, feat_ref, rows)
    for copy in copies[2:]:
        copy.wait()


def unpack_kernel(rows_ref, ids_ref):
    fields = ids_ref.shape[0]
    dense_cols = rows_ref.shape[0] - 16
    value = rows_ref[dense_cols : dense_cols + fields, :].astype(F32)
    high = jnp.zeros(value.shape, jnp.int32)
    for k in range(2, -1, -1):
        up = float(1 << (1 << k))
        over = value >= 128.0 * up
        value = jnp.where(over, value * (1.0 / up), value)
        high = high + jnp.where(over, 1 << k, 0)
    ids_ref[...] = high * 128 + (value.astype(jnp.int32) - 128)


def look_other_kernel(where_ref, ids_ref, p0_ref, p1_ref, p2_ref, p3_ref, feat_ref, wg_ref, table_s):
    fields, emb, vocab = table_s.shape
    lanes, some = vocab // 4, p0_ref.shape[0] - 2 * emb
    quarter = jnp.bitwise_and(where_ref[0], 3)
    for flip, source in ((0, p0_ref), (2, p1_ref), (1, p2_ref), (3, p3_ref)):
        at = pl.multiple_of(jnp.bitwise_xor(quarter, flip) * lanes, LANES)
        for f in range(fields):
            top = some + f % 2 * emb
            piece = source[top : top + emb, f // 2 * lanes : (f // 2 + 1) * lanes]
            table_s[f, :, pl.ds(at, lanes)] = piece.astype(F32)
    top = some + fields % 2 * emb
    wg_ref[...] = p0_ref[top : top + emb, fields // 2 * lanes : (fields // 2 + 1) * lanes]
    look_up(ids_ref, 0, table_s, feat_ref, feat_ref.shape[1])


def partial_kernel(feat_ref, w_ref, wg_ref, bias_ref, part_ref, gpart_ref, bias_s):
    rows = feat_ref.shape[1]
    for n in range(bias_ref.shape[0]):
        bias_s[n * LANES : (n + 1) * LANES, :] = 0.5 * columns_of(bias_ref[n : n + 1, :])
    lanes = chunk_of(rows, 768)

    def block(i, carry):
        cols = pl.ds(pl.multiple_of(i * lanes, lanes), lanes)
        half = feat_ref[:, cols] * jnp.asarray(0.5, BF)
        for at in range(0, w_ref.shape[1], 256):
            acc = dot(w_ref[:, at : at + 256], half, TN)
            part_ref[at : at + 256, cols] = (acc + tile_lanes(bias_s[at : at + 256, :], lanes)).astype(BF)
        gpart_ref[:, cols] = dot(wg_ref[...], half)
        return carry

    lax.fori_loop(0, rows // lanes, block, 0)


def relay_kernel(*refs):
    pass


def add_kernel(a_ref, b_ref, out_ref):
    out_ref[...] = a_ref[...] + b_ref[...]


def middle_kernel(
    groups_total,
    where_ref,
    rate_ref,
    own_ref,
    look_ref,
    rows_ref,
    p0_ref,
    p1_ref,
    p2_ref,
    p3_ref,
    q0_ref,
    q1_ref,
    q2_ref,
    q3_ref,
    wg_ref,
    part_ref,
    gpart_ref,
    bg_raw,
    wi_raw,
    bi_raw,
    wt_ref,
    bt_raw,
    wh_raw,
    bh_raw,
    labels_ref,
    weight_ref,
    slope_ref,
    feat_ref,
    dg_ref,
    w_ref,
    pred_ref,
    mix_keep_ref,
    mix_send_ref,
    pred_out_ref,
    bg_ref,
    wi_ref,
    bi_ref,
    bt_ref,
    wh_ref,
    bh_ref,
    wide_ref,
    sums_s,
    small_ref,
    hidden_ref,
    ds_ref,
    out_s,
    slope_s,
    dwt_s,
):
    rows = feat_ref.shape[1]
    lanes = out_s.shape[2]
    experts, h1, h2 = wi_raw.shape
    tasks, tower = wt_ref.shape[0], wt_ref.shape[1]
    one = jnp.asarray(1.0, BF)
    wi_ref[...] = wi_raw[...] * jnp.asarray(0.5, BF)
    for n in range(bi_raw.shape[0]):
        bi_ref[n * LANES : (n + 1) * LANES, :] = 0.5 * columns_of(bi_raw[n : n + 1, :])
    bt_ref[...] = columns_of(jnp.concatenate([bt_raw[t : t + 1, :] for t in range(tasks)], axis=1))
    wh_ref[...] = columns_of(jnp.concatenate([wh_raw[...][t : t + 1, :].astype(F32) for t in range(tasks)], axis=1))
    bg_ref[...] = small_column(bg_raw)
    bh_ref[...] = small_column(bh_raw)
    small_ref[...] = jnp.zeros_like(small_ref)
    dwt_s[...] = jnp.zeros_like(dwt_s)
    feat_ref[: look_ref.shape[0], :] = look_ref[...]
    feat_ref[look_ref.shape[0] :, :] = rows_ref[: feat_ref.shape[0] - look_ref.shape[0], :]
    quarter = jnp.bitwise_and(where_ref[0], 3)
    count = w_ref.shape[0] // 4
    some = count - q0_ref.shape[0]
    for flip, upper, lower in ((0, p0_ref, q0_ref), (2, p1_ref, q1_ref), (1, p2_ref, q2_ref), (3, p3_ref, q3_ref)):
        at = pl.multiple_of(jnp.bitwise_xor(quarter, flip) * count, 16)
        w_ref[pl.ds(at, some), :] = upper[:some, :]
        w_ref[pl.ds(at + some, count - some), :] = lower[...]
    rate = rate_ref[...]
    click = (rate + 1.0) / (groups_total + 2.0)
    entropy = -(click * jnp.log(click) + (1.0 - click) * jnp.log(1.0 - click))
    scale = tile_lanes(1.0 / (groups_total * entropy), lanes)

    def block(i, carry):
        cols = pl.ds(pl.multiple_of(i * lanes, lanes), lanes)
        source = pl.ds(pl.multiple_of(where_ref[1] * rows + i * lanes, LANES), lanes)
        half = feat_ref[:, cols] * jnp.asarray(0.5, BF)
        gate_logits = 2.0 * (gpart_ref[:, cols] + dot(wg_ref[...], half)) + tile_lanes(bg_ref[...], lanes)
        gates = []
        for t in range(tasks):
            logits = gate_logits[t * experts : (t + 1) * experts]
            top = jnp.exp(logits - jnp.max(logits, axis=0, keepdims=True))
            gates.append(top / jnp.sum(top, axis=0, keepdims=True))
        mixed = [jnp.zeros((h2, lanes), F32) for _ in range(tasks)]
        for e in range(experts):
            at = e * h1
            u = dot(w_ref[:, at : at + h1], half, TN) + part_ref[at : at + h1, cols].astype(F32)
            t1 = jnp.tanh(u)
            hidden = (u + u * t1).astype(BF)
            hidden_ref[at : at + h1, cols] = hidden
            slope_ref[at : at + h1, cols] = (one + hidden) + t1.astype(BF) * (one - hidden)
            u2 = dot(wi_ref[e], hidden, TN) + tile_lanes(bi_ref[e * h2 : (e + 1) * h2, :], lanes)
            t2 = jnp.tanh(u2)
            out = u2 + u2 * t2
            out_s[e] = out
            slope_s[e] = (1.0 + out) + t2 * (1.0 - out)
            for t in range(tasks):
                mixed[t] = mixed[t] + gates[t][e : e + 1, :] * out
        labels = labels_ref[:, source].astype(F32)
        weight = weight_ref[:, source]
        preds, d_logits, losses, d_mixed = [], [], [], []
        for t in range(tasks):
            mine = slice(t * tower, (t + 1) * tower)
            low = mixed[t].astype(BF)
            tower_pre = dot(wt_ref[t], low) + tile_lanes(bt_ref[mine, :], lanes)
            sigma = 0.5 + 0.5 * jnp.tanh(0.5 * tower_pre)
            tower_out = (tower_pre * sigma).astype(BF).astype(F32)
            head = tile_lanes(wh_ref[mine, :], lanes)
            logit = jnp.sum(tower_out * head, axis=0, keepdims=True) + tile_lanes(bh_ref[t : t + 1, :], lanes)
            label = labels[t : t + 1]
            pred = jax.nn.sigmoid(logit)
            share = weight * scale[t : t + 1]
            plus = jnp.maximum(logit, 0.0) + jnp.log1p(jnp.exp(-jnp.abs(logit)))
            losses.append(share * (plus - label * logit))
            d_logit = share * (pred - label)
            preds.append(pred)
            d_logits.append(d_logit)
            d_tower = d_logit * head * (sigma * (1.0 + tower_pre * (1.0 - sigma)))
            d_low = d_tower.astype(BF)
            base = experts * h2
            small_ref[base + t * tower : base + (t + 1) * tower, :] += fold_lanes(d_tower)
            base = base + tasks * tower
            small_ref[base + t * tower : base + (t + 1) * tower, :] += fold_lanes(d_logit * tower_out)
            dwt_s[mine, :] += dot(d_low, low, NT)
            d_mixed.append(dot(wt_ref[t], d_low, TN))
        pred_ref[:, cols] = jnp.concatenate(preds, axis=0)
        base = experts * h2 + 2 * tasks * tower + tasks * experts
        small_ref[base : base + 8, :] += fold_lanes(
            jnp.concatenate(d_logits + losses + [jnp.zeros((8 - 2 * tasks, lanes), F32)], axis=0)
        )
        halves = [0.5 * gate for gate in gates]
        d_gates = [[] for _ in range(tasks)]
        for e in range(experts):
            out = out_s[e]
            d_out = None
            for t in range(tasks):
                d_gates[t].append(jnp.sum(d_mixed[t] * out, axis=0, keepdims=True))
                term = halves[t][e : e + 1, :] * d_mixed[t]
                d_out = term if d_out is None else d_out + term
            d_second = d_out * slope_s[e]
            small_ref[e * h2 : (e + 1) * h2, :] += fold_lanes(d_second)
            ds_ref[e * h2 : (e + 1) * h2, cols] = d_second.astype(BF)
        d_all = []
        for t in range(tasks):
            d_gate = jnp.concatenate(d_gates[t], axis=0)
            d_all.append(gates[t] * (d_gate - jnp.sum(gates[t] * d_gate, axis=0, keepdims=True)))
        d_all = jnp.concatenate(d_all, axis=0)
        base = experts * h2 + 2 * tasks * tower
        small_ref[base : base + tasks * experts, :] += fold_lanes(d_all)
        dg_ref[:, cols] = d_all.astype(BF)
        return carry

    lax.fori_loop(0, rows // lanes, block, 0)

    part, tail = experts * h1 // 4, tasks * tower // 4
    for e in range(experts):
        d_wi = dot(hidden_ref[e * h1 : (e + 1) * h1, :], ds_ref[e * h2 : (e + 1) * h2, :], NT).astype(BF)
        at = e * h1
        base = at // part * (part + tail) + at % part
        wide_ref[base : base + h1, :] = d_wi
    for q in range(4):
        base = q * (part + tail) + part
        wide_ref[base : base + tail, :] = dwt_s[q * tail : (q + 1) * tail, :].astype(BF)
    core = jnp.bitwise_and(where_ref[0], 1)
    count = 2 * (part + tail)
    mix_keep_ref[:count, :] = wide_ref[pl.ds(pl.multiple_of(core * count, 32), count), :]
    mix_send_ref[:count, :] = wide_ref[pl.ds(pl.multiple_of((1 - core) * count, 32), count), :]

    sums_s[...] = jnp.zeros_like(sums_s)
    whole = experts * h2 // LANES + 2 * tasks * tower // LANES
    for g in range(whole):
        sums_s[g : g + 1, :] = jnp.sum(small_ref[g * LANES : (g + 1) * LANES, :].T, axis=0, keepdims=True)
    left = small_ref.shape[0] - whole * LANES
    sums_s[whole : whole + 1, :left] = jnp.sum(small_ref[whole * LANES :, :].T, axis=0, keepdims=True)
    step = chunk_of(rows, 768)
    for e in range(experts):
        r1, r2 = slice(e * h1, (e + 1) * h1), slice(e * h2, (e + 1) * h2)
        bias = jnp.zeros((h1, LANES), F32)
        for at in range(0, rows, step):
            cols = slice(at, at + step)
            d_pre = dot(wi_ref[e], ds_ref[r2, cols]) * slope_ref[r1, cols].astype(F32)
            bias = bias + fold_lanes(d_pre)
            slope_ref[r1, cols] = d_pre.astype(BF)
        row = jnp.sum(bias.T, axis=0, keepdims=True)
        for m in range(h1 // LANES):
            at = 16 + e * (h1 // LANES) + m
            sums_s[at : at + 1, :] = row[:, m * LANES : (m + 1) * LANES]
    for side, source in enumerate((own_ref, feat_ref)):
        d_wg = dot(dg_ref[...], source[...], NT)
        for m in range(d_wg.shape[1] // LANES):
            at = 32 + (2 * side + m) * 16
            sums_s[at : at + 16, :] = d_wg[:, m * LANES : (m + 1) * LANES]
    put_split(mix_keep_ref, count, sums_s[...])
    put_split(mix_send_ref, count, sums_s[...])
    pred = pred_ref[...]
    for m in range(rows // LANES):
        piece = pred[:, m * LANES : (m + 1) * LANES]
        high = piece.astype(BF)
        low = (piece - high.astype(F32)).astype(BF)
        split = jnp.concatenate([high.astype(F32), low.astype(F32)], axis=0)
        pred_out_ref[4 * m : 4 * m + 4, :] = split.astype(BF)
    pred_out_ref[4 * (rows // LANES) :, :] = jnp.zeros_like(pred_out_ref[4 * (rows // LANES) :, :])


def small_column(raw):
    count = raw.shape[1]
    same = lax.broadcasted_iota(jnp.int32, (count, count), 0) == lax.broadcasted_iota(jnp.int32, (count, count), 1)
    column = jnp.sum(jnp.where(same, jnp.broadcast_to(raw[...], (count, count)), 0.0), axis=1, keepdims=True)
    return jnp.broadcast_to(column, (count, LANES))


def put_split(target, at, value):
    count = value.shape[0]
    high = value.astype(BF)
    target[at : at + count, :] = high
    target[at + count : at + 2 * count, :] = (value - high.astype(F32)).astype(BF)


def get_split(source, at, count):
    return source[at : at + count, :].astype(F32) + source[at + count : at + 2 * count, :].astype(F32)


def weight_gradients(where_ref, dpre_ref, first, own_ref, oth_ref, keep_ref, send_ref):
    even = jnp.bitwise_and(where_ref[0], 1) == 0
    for n in range(keep_ref.shape[1]):
        at = first + n * 2 * LANES
        for side, source in enumerate((own_ref, oth_ref)):
            d_w = dot(source[...], dpre_ref[at : at + 2 * LANES, :], NT)
            one, two = d_w[:, :LANES], d_w[:, LANES:]
            keep_ref[side, n] = jnp.where(even, one, two).astype(BF)
            send_ref[side, n] = jnp.where(even, two, one).astype(BF)


def first_weight_kernel(where_ref, dpre_ref, own_ref, oth_ref, keep_ref, send_ref, _):
    weight_gradients(where_ref, dpre_ref, 0, own_ref, oth_ref, keep_ref, send_ref)


def feature_kernel(part, parts, where_ref, ids_ref, dpre_ref, dg_ref, w_ref, wg_ref, *refs):
    fields, emb = ids_ref.shape[0], 16
    rows = dg_ref.shape[1]
    lanes = chunk_of(rows, 1152)
    carried = refs[0] if part > 0 else None
    first = where_ref[1] * rows if ids_ref.shape[1] > rows else 0
    if part > 0:
        refs = refs[2:]
    if part == parts - 1:
        keep_ref, send_ref, ddense_ref, _, acc_s = refs
    else:
        acc_s, ddense_ref, _ = refs
    highs = acc_s.shape[1] // emb
    acc_s[...] = jnp.zeros_like(acc_s) if carried is None else carried[...]

    def block(i, carry):
        cols = pl.ds(pl.multiple_of(i * lanes, lanes), lanes)
        source = pl.ds(pl.multiple_of(first + i * lanes, LANES), lanes)
        d_feat = dot(w_ref[...], dpre_ref[:, cols]) + dot(wg_ref[...], dg_ref[:, cols], TN)
        ddense_ref[:, cols] = d_feat[fields * emb :, :].astype(ddense_ref.dtype)
        every = ids_ref[:, source]
        low = jnp.bitwise_and(every, LANES - 1)
        every = jnp.right_shift(every, 7)
        places = lax.broadcasted_iota(jnp.int32, (LANES, lanes), 0)
        for f in range(fields):
            hot = jnp.where(places == low[f : f + 1, :], 1.0, 0.0).astype(BF)
            high = jnp.broadcast_to(every[f : f + 1, :], (emb, lanes))
            grad = d_feat[f * emb : (f + 1) * emb, :]
            spread = jnp.concatenate([jnp.where(high == h, grad, 0.0) for h in range(highs)], axis=0)
            acc_s[f] += dot(spread.astype(BF), hot, NT)
        return carry

    steps = rows // lanes
    lax.fori_loop(steps * part // parts, steps * (part + 1) // parts, block, 0)
    if part < parts - 1:
        return
    even = jnp.bitwise_and(where_ref[0], 1) == 0
    left = lax.broadcasted_iota(jnp.int32, (emb, LANES), 1) < LANES // 2
    for p in range((fields + 1) // 2):
        rows_p = slice(p * emb, (p + 1) * emb)
        for h in range(highs):
            a = acc_s[2 * p, h * emb : (h + 1) * emb, :]
            b = acc_s[2 * p + 1, h * emb : (h + 1) * emb, :] if 2 * p + 1 < fields else jnp.zeros_like(a)
            first = jnp.where(left, a, pltpu.roll(b, LANES // 2, 1))
            second = jnp.where(left, pltpu.roll(a, LANES // 2, 1), b)
            keep_ref[h, rows_p, :] = jnp.where(even, first, second).astype(BF)
            send_ref[h, rows_p, :] = jnp.where(even, second, first).astype(BF)


def step_kernel(works, counts, where_ref, *refs):
    def bit(k):
        return jnp.bitwise_and(jnp.right_shift(where_ref[0], k), 1)

    ins = sum(n for n, _ in counts)
    a, b = 0, ins
    for work, (n_in, n_out) in zip(works, counts):
        work(refs[a : a + n_in], refs[b : b + n_out], bit, where_ref)
        a, b = a + n_in, b + n_out


def total(a, b, at):
    return a[at].astype(F32) + b[at].astype(F32)


def work_sum(ins, outs, bit, where):
    outs[0][...] = total(ins[0], ins[1], ...).astype(outs[0].dtype)


def work_sides(ins, outs, bit, where):
    for side in range(2):
        outs[side][...] = total(ins[0], ins[1], side).astype(outs[side].dtype)


def work_mix_core(ins, outs, bit, where):
    got, mine = ins
    keep, send = outs
    count = keep.shape[0] - 128
    sums = get_split(got, 2 * count, 96) + get_split(mine, 2 * count, 96)
    for out, half in ((keep, where[1]), (send, 1 - where[1])):
        out[:count, :] = total(got, mine, pl.ds(pl.multiple_of(half * count, 32), count)).astype(BF)
    put_split(keep, count, jnp.concatenate([sums[:32], sums[32:64]], axis=0))
    put_split(send, count, jnp.concatenate([sums[:32], sums[64:96]], axis=0))


def work_pred(ins, outs, bit, where):
    rows = outs[0].shape[1] // 2
    for side, source in ((where[1], ins[0]), (1 - where[1], ins[1])):
        for m in range(rows // LANES):
            value = source[4 * m : 4 * m + 2, :].astype(F32) + source[4 * m + 2 : 4 * m + 4, :].astype(F32)
            outs[0][:, pl.ds(pl.multiple_of(side * rows + m * LANES, LANES), LANES)] = value


def work_mix(ins, outs, bit, where):
    count = ins[0].shape[0] - 128
    outs[0][:count, :] = total(ins[0], ins[1], slice(0, count)).astype(BF)
    put_split(outs[0], count, get_split(ins[0], count, 64) + get_split(ins[1], count, 64))


def work_mix_last(ins, outs, bit, where):
    quarter, inner, tower, head, gate, ends, loss, first, weights = outs
    count = ins[0].shape[0] - 128
    quarter[...] = total(ins[0], ins[1], slice(0, count)).astype(BF)
    sums = get_split(ins[0], count, 64) + get_split(ins[1], count, 64)
    inner[...] = sums[:8]
    half = tower.shape[1]
    for n in range(2):
        tower[n : n + 1, :] = sums[8:9, n * half : (n + 1) * half]
        head[n : n + 1, :] = sums[9:10, n * half : (n + 1) * half]
    gates = gate.shape[1]
    gate[...] = sums[10:11, :gates]
    ends[...] = sums[10:11, gates : gates + 2]
    loss[...] = sums[10:11, gates + 2 : gates + 3] + sums[10:11, gates + 3 : gates + 4]
    first[...] = sums[16:32]
    weights[:, :LANES] = sums[32:48]
    weights[:, LANES:] = sums[48:64]


def work_wide(ins, outs, bit, where):
    here = bit(0) * 2 + where[1]
    cut = outs[0].shape[1]
    for n, source in enumerate(ins):
        at = (here, jnp.bitwise_xor(here, 1), jnp.bitwise_xor(here, 2), jnp.bitwise_xor(here, 3))[n]
        outs[0][at] = source[:cut, :].astype(F32)
        outs[1][at] = source[cut:, :].astype(F32)


def work_dense(ins, outs, bit, where):
    mine, theirs = ins
    rows = mine.shape[1]
    outs[0][:, pl.ds(pl.multiple_of(where[1] * rows, LANES), rows)] = mine[...]
    outs[0][:, pl.ds(pl.multiple_of((1 - where[1]) * rows, LANES), rows)] = theirs[...].astype(F32)


def work_table(ins, outs, bit, where):
    value = total(ins[0], ins[1], 0)
    emb, half = outs[0].shape[1:]
    for f in range(outs[0].shape[0]):
        piece = value[f // 2 * emb : (f // 2 + 1) * emb]
        if f % 2:
            piece = pltpu.roll(piece, half, 1)
        outs[0][f] = piece[:, :half]


def work_add(ins, outs, bit, where):
    outs[0][...] = total(ins[0], ins[1], ...)


def work_pass(ins, outs, bit, where):
    outs[0][...] = ins[0][...]


def work_halve(k):
    def work(ins, outs, bit, where):
        for out, half in ((outs[0], bit(k)), (outs[1], 1 - bit(k))):
            for n in range(out.shape[0]):
                out[n] = total(ins[0], ins[1], 2 * n + half).astype(out.dtype)

    return work


def work_two_ways(ins, outs, bit, where):
    half = ins[0].shape[1] // 2
    for side in range(2):
        for n in range(half):
            outs[side][n] = total(ins[0], ins[1], (side, n)).astype(BF)
    for out, which in ((outs[2], bit(1)), (outs[3], 1 - bit(1))):
        for side in range(2):
            for n in range(half // 2):
                out[side, n] = total(ins[0], ins[1], (side, half + 2 * n + which)).astype(BF)


def work_halve_top(ins, outs, bit, where):
    count = outs[0].shape[0]
    for out, half in ((outs[0], bit(2)), (outs[1], 1 - bit(2))):
        for n in range(count):
            out[n] = total(ins[0], ins[1], half * count + n).astype(BF)


def work_choose(ins, outs, bit, where):
    one, second = total(ins[0], ins[1], 0), total(ins[2], ins[3], 0)
    mine = bit(3) == 0
    outs[0][...] = jnp.where(mine, one, second).astype(BF)
    outs[1][...] = jnp.where(mine, second, one).astype(BF)


def chunk_of(rows, most):
    lanes = LANES
    for size in range(LANES, most + 1, LANES):
        if rows % size == 0:
            lanes = size
    return lanes


def sds(shape, dtype):
    return jax.ShapeDtypeStruct(shape, dtype)


def pinned(shape, dtype):
    return pltpu.VMEM(shape, dtype)


def run(kernel, name, outs, args, us, scalars=0, scratch=(), mib=16, alias=None, after=(), loose=False):
    vmem, smem = pl.BlockSpec(memory_space=pltpu.VMEM), pl.BlockSpec(memory_space=pltpu.SMEM)
    free = pl.BlockSpec(memory_space=pltpu.HBM if loose else pl.ANY)
    count = len(args)

    def body(*refs):
        kernel(*refs[:count], *refs[count + len(after) :])

    return pl.pallas_call(
        body,
        in_specs=[smem] * scalars + [free if loose else vmem] * (count - scalars) + [free] * len(after),
        out_specs=[vmem] * len(outs),
        out_shape=list(outs),
        scratch_shapes=list(scratch),
        input_output_aliases=alias or {},
        compiler_params=pltpu.CompilerParams(vmem_limit_bytes=mib * 1024 * 1024),
        cost_estimate=pl.CostEstimate(flops=int(us * SCALE), bytes_accessed=0, transcendentals=0),
        name=name,
    )(*args, *after)


def take_step(name, where, items, after=()):
    ins = [value for item in items for value in item[1]]
    outs = [shape for item in items for shape in item[2]]
    counts = [(len(item[1]), len(item[2])) for item in items]
    kernel = functools.partial(step_kernel, [item[0] for item in items], counts)
    got = run(kernel, name, outs, [where] + ins, ST, 1, mib=6, after=after)
    split, at = [], 0
    for _, count in counts:
        split.append(list(got[at : at + count]) if count > 1 else got[at])
        at += count
    return split


def relay(values, us, after=()):
    free = pl.BlockSpec(memory_space=pl.ANY)
    return pl.pallas_call(
        relay_kernel,
        in_specs=[free] * (len(values) + len(after)),
        out_specs=[free] * len(values),
        out_shape=[sds(value.shape, value.dtype) for value in values],
        input_output_aliases={n: n for n in range(len(values))},
        compiler_params=pltpu.CompilerParams(vmem_limit_bytes=1 << 20),
        cost_estimate=pl.CostEstimate(flops=int(us * SCALE), bytes_accessed=0, transcendentals=0),
        name="relay",
    )(*values, *after)


def add_low(a, b):
    return (a.astype(F32) + b.astype(F32)).astype(BF)


def ordered(bit, mine, theirs, axis):
    return jnp.where(
        bit == 0,
        jnp.concatenate([mine, theirs], axis=axis),
        jnp.concatenate([theirs, mine], axis=axis),
    )


def bit_of(rank, k):
    return jnp.bitwise_and(jnp.right_shift(rank, k), 1)


def per_device(
    dense, ids, table, sizes, labels, w_expert, b_expert, w_gate, b_gate, w_inner, b_inner, w_tower, b_tower, w_head, b_head
):
    n_rows = lax.axis_size("rows")
    n_bits = n_rows.bit_length() - 1
    rank, j = lax.axis_index("rows"), lax.axis_index("field")
    core = bit_of(rank, 0)
    rows_all, fields = ids.shape
    rows = rows_all // 2
    vocab, emb = table.shape[1], table.shape[2]
    dense_cols = dense.shape[1]
    width, n_expert = w_expert.shape
    experts, h1, h2 = w_inner.shape
    tasks, tower = w_head.shape
    gates = tasks * experts

    ids_t, dense_t, labels_t = ids.T, dense.T, labels.T
    table_t = jnp.transpose(table, (0, 2, 1))
    wg_own = w_gate.T
    where = jnp.stack([rank, j]).astype(jnp.int32)
    fast = n_rows * LANES == n_expert and n_rows * LANES == 2 * vocab

    def over_rows(value, bit):
        return swap(value, "rows", bit)

    def over_field(value):
        return swap(value, "field", 1)

    some = width // 16
    first, second, rows_away, weight, rate = run(
        pack_kernel,
        "pack",
        [
            sds((some + 2 * emb, n_expert), BF),
            sds((width // 4 - some, n_expert), BF),
            sds((dense_cols + 16, rows), BF),
            sds((1, rows_all), F32),
            sds((tasks, LANES), F32),
        ],
        [where, w_expert, table_t, wg_own, ids_t, dense_t, sizes, labels_t],
        2.0,
        1,
        [
            pltpu.VMEM((fields, emb, vocab // 4), F32),
            pltpu.VMEM(wg_own.shape, BF),
            pltpu.VMEM((fields, rows), jnp.int32),
            pltpu.VMEM(sizes.shape, jnp.int32),
            pltpu.VMEM(labels_t.shape, jnp.int32),
            pltpu.SemaphoreType.DMA((8,)),
        ],
        mib=60,
        loose=True,
    )
    p0, q0, rows_oth = over_field(first), over_field(second), over_field(rows_away)
    feat = pinned((width, rows), BF)
    rate_s = sds((tasks, LANES), F32)

    def click_sum(rate, k, after):
        return run(add_kernel, "click_sum", [rate_s], [rate, over_rows(rate, 1 << k)], 0.3, after=after, mib=2)[0]

    rate = click_sum(rate, 0, [])
    bias = b_expert.reshape(-1, LANES)
    feat_own, w_own, wg_here, bias = run(
        look_own_kernel,
        "look_own",
        [feat, pinned((width, n_expert), BF), pinned((gates, width), BF), pinned(bias.shape, F32)],
        [where, ids_t, dense_t, table_t, w_expert, wg_own, bias],
        0.3,
        1,
        [
            pltpu.VMEM((fields, rows), jnp.int32),
            pltpu.VMEM((fields, emb, vocab), F32),
            pltpu.SemaphoreType.DMA((6,)),
        ],
        mib=58,
        loose=True,
        after=[rate],
    )
    rate = click_sum(rate, 1, [feat_own])
    (p0,) = relay([p0], 0.1, [rate])
    (q0,) = relay([q0], 0.1, [rate])
    p1 = over_rows(p0, 2)
    p2, p3 = over_rows(p0, 1), over_rows(p1, 1)
    part, gpart = run(
        partial_kernel,
        "own_share",
        [pinned((n_expert, rows), BF), sds((gates, rows), F32)],
        [feat_own, w_own, wg_here, bias],
        0.3,
        0,
        [pltpu.VMEM((n_expert, LANES), F32)],
        mib=20,
        after=[p0],
    )
    rate = click_sum(rate, 2, [gpart])
    q1 = over_rows(q0, 2)
    q2, q3 = over_rows(q0, 1), over_rows(q1, 1)
    q2, q3 = relay([q2, q3], RQ)
    (ids_oth,) = run(unpack_kernel, "unpack", [sds((fields, rows), jnp.int32)], [rows_oth], UNP, mib=4)
    look_oth, wg_oth = run(
        look_other_kernel,
        "look_other",
        [pinned((fields * emb, rows), BF), sds((gates, width), BF)],
        [where, ids_oth, p0, p1, p2, p3],
        LO,
        1,
        [pltpu.VMEM((fields, emb, vocab), F32)],
            )

    for k in range(3, n_bits):
        rate = click_sum(rate, k, [look_oth])
    wide_rows = experts * h1 + tasks * tower
    small_rows = experts * h2 + 2 * tasks * tower + gates + 8
    mix_rows = wide_rows // 2 + 192
    blocks = n_expert // LANES // 2
    lanes = chunk_of(rows, 1152)
    mix_rows = wide_rows // 2 + 192
    blocks = n_expert // LANES // 2
    d_pre, feat_oth, d_gates, w_oth, _, mix_keep, mix_send, pred = run(
        functools.partial(middle_kernel, float(sizes.shape[1] * n_rows)),
        "middle",
        [
            pinned((n_expert, rows), BF),
            feat,
            sds((gates, rows), BF),
            sds((width, n_expert), BF),
            sds((tasks, rows), F32),
            sds((mix_rows, h2), BF),
            sds((mix_rows, h2), BF),
            sds((4 * (rows // LANES) + 8, LANES), BF),
        ],
        [
            where,
            rate,
            feat_own,
            look_oth,
            rows_oth,
            p0,
            p1,
            p2,
            p3,
            q0,
            q1,
            q2,
            q3,
            wg_oth,
            part,
            gpart,
            b_gate.reshape(1, -1),
            w_inner,
            b_inner,
            jnp.transpose(w_tower, (0, 2, 1)),
            b_tower,
            w_head,
            b_head.reshape(1, -1),
            labels_t,
            weight,
        ],
        23.0,
        1,
        [
            pltpu.VMEM((gates, LANES), F32),
            pltpu.VMEM((experts, h1, h2), BF),
            pltpu.VMEM((experts * h2, LANES), F32),
            pltpu.VMEM((tasks * tower, LANES), F32),
            pltpu.VMEM((tasks * tower, LANES), F32),
            pltpu.VMEM((tasks, LANES), F32),
            pltpu.VMEM((wide_rows, h2), BF),
            pltpu.VMEM((96, LANES), F32),
            pltpu.VMEM((small_rows, LANES), F32),
            pltpu.VMEM((n_expert, rows), BF),
            pltpu.VMEM((experts * h2, rows), BF),
            pltpu.VMEM((experts, h2, lanes), F32),
            pltpu.VMEM((experts, h2, lanes), F32),
            pltpu.VMEM((tasks * tower, h2), F32),
        ],
        mib=36,
        alias={14: 0},
    )

    held = pinned((n_expert, rows), BF)
    deep = (fields + 1) // 2 * emb
    highs = vocab // LANES
    quarter_rows = wide_rows // 4
    mix_s = sds((quarter_rows + 128, h2), BF)

    def blocks_s(*shape):
        return sds(shape + (width, LANES), BF)

    def planes_s(count):
        return sds((count, deep, LANES), BF)

    def features_back(part, parts, ids_half, d_pre, w_half, wg_half, carried, dtype, name, after):
        outs = [sds((dense_cols, rows), dtype), held]
        scratch = [pltpu.VMEM((fields, highs * emb, LANES), F32)]
        if part == parts - 1:
            outs = [planes_s(highs), planes_s(highs)] + outs
        else:
            outs, scratch = [sds((fields, highs * emb, LANES), F32)] + outs, []
        alias = {2: len(outs) - 1}
        if part > 0:
            alias[7] = len(outs) - 2
        return run(
            functools.partial(feature_kernel, part, parts),
            name,
            outs,
            [where, ids_half, d_pre, d_gates, w_half, wg_half] + carried,
            FB / parts,
            1,
            scratch,
            alias=alias,
            after=after,
        )

    mix_got = over_rows(mix_send, 1)
    ((mix, mix_send),) = take_step("step_0", where, [(work_mix_core, [mix_got, mix_keep], [mix_s] * 2)])
    mix_got, pred_got = over_field(mix_send), over_field(pred)
    dw_keep, dw_send, d_pre = run(
        first_weight_kernel,
        "first_weights",
        [blocks_s(2, blocks), blocks_s(2, blocks), held],
        [where, d_pre, feat_own, feat_oth],
        FW,
        1,
        alias={1: 2},
        after=[mix],
    )
    (mix,) = take_step("step_1", where, [(work_mix, [mix_got, mix], [mix_s])], [dw_keep])
    if fast:
        (dw_send,) = relay([dw_send], 0.0, [mix])
        dw_got = over_rows(dw_send, 1)
    mix_got = over_rows(mix, 2)
    dt_keep, dt_send, dd_oth, d_pre = features_back(
        0, 1, ids_oth, d_pre, w_oth, wg_oth, [], BF, "features_other", [mix]
    )
    mix_work = (work_mix, [mix_got, mix], [mix_s])
    if fast:
        dt_got = over_rows(dt_send, 1)
        (a_keep, a_send, b_keep, b_send), mix = take_step(
            "step_2",
            where,
            [
                (work_two_ways, [dw_got, dw_keep], [blocks_s(4), blocks_s(4), blocks_s(2, 2), blocks_s(2, 2)]),
                mix_work,
            ],
            [dt_keep],
        )
        a_got = over_field(a_send)
        b_got = over_rows(b_send, 2)
        mix_got = over_rows(mix, 8)
    else:
        (mix,) = take_step("step_2", where, [mix_work], [dt_keep])
    acc, dd_own, d_pre = features_back(0, 2, ids_t, d_pre, w_own, wg_own, [], F32, "features_own_0", [mix])
    if fast:
        (dt_oth,) = take_step("step_3", where, [(work_sum, [dt_got, dt_keep], [planes_s(highs)])], [acc])
        dt_far = over_field(dt_oth)
        after = [dt_oth]
    else:
        after = []
    do_keep, do_send, dd_own, _ = features_back(
        1, 2, ids_t, d_pre, w_own, wg_own, [acc, dd_own], F32, "features_own_1", after
    )
    dense_s = sds((dense_cols, rows_all), F32)
    pred_work = (work_pred, [pred, pred_got], [sds((tasks, rows_all), F32)])
    if fast:
        do_got = over_rows(do_send, 1)
        (a_keep, a_send), (b_keep, b_send), mix, dd_oth, predicted = take_step(
            "step_4",
            where,
            [
                (work_halve_top, [a_got, a_keep], [blocks_s(2)] * 2),
                (work_sides, [b_got, b_keep], [blocks_s(2)] * 2),
                (work_mix, [mix_got, mix], [mix_s]),
                (work_pass, [dd_oth], [sds(dd_oth.shape, BF)]),
                pred_work,
            ],
            [do_keep],
        )
        a_got = over_rows(a_send, 4)
        b_got = over_field(b_send)
        mix_got = over_rows(mix, 4)
        dd_got = over_field(dd_oth)
        (do_keep,) = take_step("step_5", where, [(work_sum, [dt_far, do_keep], [planes_s(highs)])], [mix])
        ((d_keep, d_send),) = take_step(
            "step_5b", where, [(work_halve(1), [do_got, do_keep], [planes_s(highs // 2)] * 2)]
        )
        d_got = over_rows(d_send, 2)
        (a_keep, a_send), (b_keep, b_send), finals, (d_keep, d_send) = take_step(
            "step_6",
            where,
            [
                (work_halve(1), [a_got, a_keep], [blocks_s(1)] * 2),
                (work_halve(2), [b_got, b_keep], [blocks_s(1)] * 2),
                (
                    work_mix_last,
                    [mix_got, mix],
                    [
                        sds((quarter_rows, h2), BF),
                        sds((experts, h2), F32),
                        sds((tasks, tower), F32),
                        sds((tasks, tower), F32),
                        sds((1, gates), F32),
                        sds((1, tasks), F32),
                        sds((1, 1), F32),
                        sds((n_expert // LANES, LANES), F32),
                        sds((gates, width), F32),
                    ],
                ),
                (work_halve(2), [d_got, d_keep], [planes_s(highs // 4)] * 2),
            ],
        )
        a_got, b_got = over_rows(a_send, 2), over_rows(b_send, 4)
        d_got = over_rows(d_send, 4)
        (c_keep, c_send), (d_keep, d_send) = take_step(
            "step_7",
            where,
            [
                (work_choose, [a_got, a_keep, b_got, b_keep], [blocks_s()] * 2),
                (work_halve(3), [d_got, d_keep], [planes_s(1)] * 2),
            ],
        )
        d_got = over_rows(d_send, 8)
        c_got = over_rows(c_send, 8)
        wide, d_b_inner, d_b_tower, d_w_head, d_b_gate, d_b_head, loss, d_b_expert, d_w_gate = finals
        wide_f, wide_c = over_field(wide), over_rows(wide, 1)
        wide_fc = lax.ppermute(wide, ("rows", "field"), [(i, i ^ 3) for i in range(2 * n_rows)])
        d_table, d_w_expert, (d_w_inner, d_w_tower), d_dense = take_step(
            "step_9",
            where,
            [
                (work_table, [d_got, d_keep], [sds((fields, emb, vocab // n_rows), F32)]),
                (work_add, [c_got, c_keep], [sds((width, LANES), F32)]),
                (
                    work_wide,
                    [wide, wide_f, wide_c, wide_fc],
                    [sds((4, experts * h1 // 4, h2), F32), sds((4, tasks * tower // 4, h2), F32)],
                ),
                (work_dense, [dd_own, dd_got], [dense_s]),
            ],
        )
        d_table = jnp.transpose(d_table, (0, 2, 1))
        d_w_inner = d_w_inner.reshape(experts, h1, h2)
        d_w_tower = jnp.transpose(d_w_tower.reshape(tasks, tower, h2), (0, 2, 1))
    else:

        def by_core(keep, send, axis):
            return jnp.where(core == 0, jnp.stack([keep, send], axis), jnp.stack([send, keep], axis))

        def tables(keep, send):
            value = by_core(keep, send, 1).reshape(highs, 2, deep // emb, emb, 2, LANES // 2)
            return jnp.transpose(value, (2, 4, 3, 0, 1, 5)).reshape(deep // emb * 2, emb, vocab)[:fields]

        d_t = add_low(tables(do_keep, do_send), over_field(tables(dt_keep, dt_send))).astype(F32)
        d_table = jnp.transpose(lax.psum_scatter(d_t, "rows", scatter_dimension=2, tiled=True), (0, 2, 1))
        d_w = by_core(dw_keep, dw_send, 2).reshape(2, 2 * blocks, width, LANES)
        d_w = add_low(d_w[0], over_field(d_w[1])).astype(F32)
        d_w = jnp.transpose(d_w, (1, 0, 2)).reshape(width, n_expert)
        d_w_expert = lax.psum_scatter(d_w, "rows", scatter_dimension=1, tiled=True)
        sums = get_split(mix, quarter_rows, 64)
        wide = mix[:quarter_rows]
        for k in range(2, n_bits):
            wide = add_low(wide, over_rows(wide, 1 << k))
            sums = sums + over_rows(sums, 1 << k)
        wide = ordered(j, wide, over_field(wide), 0)
        wide = ordered(core, wide, over_rows(wide, 1), 0).astype(F32).reshape(4, quarter_rows, h2)
        cut = experts * h1 // 4
        d_w_inner = wide[:, :cut].reshape(experts, h1, h2)
        d_w_tower = jnp.transpose(wide[:, cut:].reshape(tasks, tower, h2), (0, 2, 1))
        d_b_inner, d_b_tower, d_w_head = sums[:8], sums[8], sums[9]
        d_b_gate, d_b_head = sums[10, :gates], sums[10, gates : gates + tasks]
        loss = jnp.sum(sums[10, gates + tasks : gates + 2 * tasks])
        d_b_expert = sums[16:32]
        d_w_gate = jnp.concatenate([sums[32:48], sums[48:64]], axis=1)
        d_dense, predicted = take_step(
            "rest", where, [(work_dense, [dd_own, over_field(dd_oth)], [dense_s]), pred_work]
        )

    return (
        predicted.T,
        loss.reshape(()),
        d_dense.T,
        d_table,
        d_w_expert,
        d_b_expert.reshape(n_expert),
        d_w_gate.T,
        d_b_gate.reshape(gates),
        d_w_inner,
        d_b_inner.reshape(experts, h2),
        d_w_tower,
        d_b_tower.reshape(tasks, tower),
        d_w_head.reshape(tasks, tower),
        d_b_head.reshape(tasks),
    )


def solution(mesh):
    return jax.shard_map(
        per_device,
        mesh=mesh,
        in_specs=(
            P("rows", "field"),
            P("rows", "field"),
            P("field", None, None),
            P("rows", None),
            P("rows", None),
            P("field", None),
            P(),
            P("field", None),
            P(),
            P(),
            P(),
            P(),
            P(),
            P(),
            P(),
        ),
        out_specs=(
            P("rows", None),
            P(),
            P("rows", "field"),
            P("field", "rows", None),
            P("field", "rows"),
            P(),
            P("field", None),
            P(),
            P(),
            P(),
            P(),
            P(),
            P(),
            P(),
        ),
        check_vma=False,
    )
```

```python
import functools

import jax
import jax.numpy as jnp
from jax import lax
from jax.experimental import pallas as pl
from jax.experimental.pallas import tpu as pltpu
from jax.sharding import PartitionSpec as P

BF = jnp.bfloat16
F32 = jnp.float32
LANES = 128
SCALE = 1.0e9
UNP = 2.0
FW, FB, ST = 0.5, 0.5, 0.3
LO = 4.0
RQ = 0.1

NN = (((1,), (0,)), ((), ()))
TN = (((0,), (0,)), ((), ()))
NT = (((1,), (1,)), ((), ()))


def dot(a, b, dims=NN):
    return lax.dot_general(a, b, dims, preferred_element_type=F32)


def swap(value, axis, bit):
    size = lax.axis_size(axis)
    return lax.ppermute(value, axis, [(i, i ^ bit) for i in range(size)])


def columns_of(row):
    return jnp.broadcast_to(row, (LANES, LANES)).T


def tile_lanes(column, lanes):
    return jnp.concatenate([column] * (lanes // LANES), axis=1)


def fold_lanes(value):
    total = value[:, :LANES]
    for start in range(LANES, value.shape[1], LANES):
        total = total + value[:, start : start + LANES]
    return total


def pack_kernel(
    where_ref,
    w_ref,
    table_ref,
    wg_ref,
    ids_ref,
    dense_ref,
    sizes_ref,
    labels_ref,
    first_ref,
    second_ref,
    rows_ref,
    weight_ref,
    rate_ref,
    table_s,
    wg_s,
    ids_s,
    sizes_s,
    labels_s,
    sems,
):
    quarter = jnp.bitwise_and(where_ref[0], 3)
    fields, emb, vocab = table_ref.shape
    lanes = table_s.shape[2]
    dense_cols, rows = dense_ref.shape[0], rows_ref.shape[1]
    some, count = w_ref.shape[0] // 4 - second_ref.shape[0], w_ref.shape[0] // 4
    away = pl.ds(pl.multiple_of((1 - where_ref[1]) * rows, LANES), rows)
    base = pl.multiple_of(quarter * count, 16)
    copies = [
        pltpu.make_async_copy(w_ref.at[pl.ds(base, some), :], first_ref.at[:some, :], sems.at[0]),
        pltpu.make_async_copy(w_ref.at[pl.ds(base + some, count - some), :], second_ref, sems.at[1]),
        pltpu.make_async_copy(
            table_ref.at[:, :, pl.ds(pl.multiple_of(quarter * lanes, LANES), lanes)], table_s, sems.at[2]
        ),
        pltpu.make_async_copy(wg_ref, wg_s, sems.at[3]),
        pltpu.make_async_copy(ids_ref.at[:, away], ids_s, sems.at[4]),
        pltpu.make_async_copy(dense_ref.at[:, away], rows_ref.at[:dense_cols, :], sems.at[5]),
        pltpu.make_async_copy(sizes_ref, sizes_s, sems.at[6]),
        pltpu.make_async_copy(labels_ref, labels_s, sems.at[7]),
    ]
    for copy in copies:
        copy.start()
    for copy in copies:
        copy.wait()
    sizes_ref, labels_ref = sizes_s, labels_s
    for f in range(fields):
        at = some + f % 2 * emb
        first_ref[at : at + emb, f // 2 * lanes : (f // 2 + 1) * lanes] = table_s[f].astype(BF)
    at = some + fields % 2 * emb
    first_ref[at : at + emb, fields // 2 * lanes : (fields // 2 + 1) * lanes] = wg_s[...]
    first_ref[some:, (fields // 2 + 1) * lanes :] = jnp.zeros_like(first_ref[some:, (fields // 2 + 1) * lanes :])
    ids = ids_s[...]
    value = (jnp.bitwise_and(ids, 127) + 128).astype(F32)
    for k in range(3):
        up = float(1 << (1 << k))
        value = value * jnp.where(jnp.bitwise_and(jnp.right_shift(ids, 7 + k), 1) == 1, up, 1.0)
    rows_ref[dense_cols : dense_cols + fields, :] = value.astype(BF)
    rows_ref[dense_cols + fields :, :] = jnp.zeros_like(rows_ref[dense_cols + fields :, :])
    groups, rows = sizes_ref.shape[1], labels_ref.shape[1]
    sizes = jnp.broadcast_to(sizes_ref[...].astype(F32), (groups, groups))
    below = lax.broadcasted_iota(jnp.int32, (groups, groups), 0)
    across = lax.broadcasted_iota(jnp.int32, (groups, groups), 1)
    starts = jnp.sum(jnp.where(across < below, sizes, 0.0), axis=1, keepdims=True)
    own = jnp.sum(jnp.where(across == below, sizes, 0.0), axis=1, keepdims=True)
    ends = starts + own
    share = 1.0 / own
    rate = jnp.zeros((2, LANES), F32)
    for at in range(0, rows, 256):
        place = (lax.broadcasted_iota(jnp.int32, (groups, 256), 1) + at).astype(F32)
        inside = (place >= starts) & (place < ends)
        weight = jnp.sum(jnp.where(inside, share, 0.0), axis=0, keepdims=True)
        weight_ref[:, at : at + 256] = weight
        rate = rate + fold_lanes(weight * labels_ref[:, at : at + 256].astype(F32))
    rate_ref[...] = jnp.broadcast_to(jnp.sum(rate, axis=1, keepdims=True), rate_ref.shape)


def look_up(ids_ref, first, table_ref, feat_ref, rows, dense_ref=None):
    fields, emb, vocab = table_ref.shape
    lanes = 256

    def block(i, carry):
        source = pl.ds(pl.multiple_of(first + i * lanes, lanes), lanes)
        target = pl.multiple_of(i * lanes, lanes)
        every = ids_ref[:, source]
        for f in range(fields):
            for at in range(0, lanes, LANES):
                ids = every[f : f + 1, at : at + LANES]
                low = jnp.broadcast_to(jnp.bitwise_and(ids, LANES - 1), (emb, LANES))
                high = jnp.broadcast_to(jnp.right_shift(ids, 7), (emb, LANES))
                found = None
                for h in range(vocab // LANES):
                    piece = table_ref[f, :, h * LANES : (h + 1) * LANES]
                    piece = jnp.take_along_axis(piece, low, axis=1, mode="promise_in_bounds")
                    found = piece if found is None else jnp.where(high == h, piece, found)
                feat_ref[f * emb : (f + 1) * emb, pl.ds(target + at, LANES)] = found.astype(BF)
        if dense_ref is not None:
            feat_ref[fields * emb :, pl.ds(target, lanes)] = dense_ref[:, source]
        return carry

    lax.fori_loop(0, rows // lanes, block, 0)


def look_own_kernel(
    where_ref, ids_ref, dense_ref, table_ref, w_in, wg_in, bias_in, feat_ref, w_ref, wg_ref, bias_ref, ids_s, table_s, sems
):
    rows = feat_ref.shape[1]
    fields, emb, _ = table_ref.shape
    mine = pl.ds(pl.multiple_of(where_ref[1] * rows, LANES), rows)
    copies = [
        pltpu.make_async_copy(ids_ref.at[:, mine], ids_s, sems.at[0]),
        pltpu.make_async_copy(table_ref, table_s, sems.at[1]),
        pltpu.make_async_copy(dense_ref.at[:, mine], feat_ref.at[fields * emb :, :], sems.at[2]),
        pltpu.make_async_copy(bias_in, bias_ref, sems.at[3]),
        pltpu.make_async_copy(wg_in, wg_ref, sems.at[4]),
        pltpu.make_async_copy(w_in, w_ref, sems.at[5]),
    ]
    for copy in copies:
        copy.start()
    for copy in copies[:2]:
        copy.wait()
    look_up(ids_s, 0, table_s, feat_ref, rows)
    for copy in copies[2:]:
        copy.wait()


def unpack_kernel(rows_ref, ids_ref):
    fields = ids_ref.shape[0]
    dense_cols = rows_ref.shape[0] - 16
    value = rows_ref[dense_cols : dense_cols + fields, :].astype(F32)
    high = jnp.zeros(value.shape, jnp.int32)
    for k in range(2, -1, -1):
        up = float(1 << (1 << k))
        over = value >= 128.0 * up
        value = jnp.where(over, value * (1.0 / up), value)
        high = high + jnp.where(over, 1 << k, 0)
    ids_ref[...] = high * 128 + (value.astype(jnp.int32) - 128)


def look_other_kernel(where_ref, ids_ref, p0_ref, p1_ref, p2_ref, p3_ref, feat_ref, wg_ref, table_s):
    fields, emb, vocab = table_s.shape
    lanes, some = vocab // 4, p0_ref.shape[0] - 2 * emb
    quarter = jnp.bitwise_and(where_ref[0], 3)
    for flip, source in ((0, p0_ref), (2, p1_ref), (1, p2_ref), (3, p3_ref)):
        at = pl.multiple_of(jnp.bitwise_xor(quarter, flip) * lanes, LANES)
        for f in range(fields):
            top = some + f % 2 * emb
            piece = source[top : top + emb, f // 2 * lanes : (f // 2 + 1) * lanes]
            table_s[f, :, pl.ds(at, lanes)] = piece.astype(F32)
    top = some + fields % 2 * emb
    wg_ref[...] = p0_ref[top : top + emb, fields // 2 * lanes : (fields // 2 + 1) * lanes]
    look_up(ids_ref, 0, table_s, feat_ref, feat_ref.shape[1])


def partial_kernel(feat_ref, w_ref, wg_ref, bias_ref, part_ref, gpart_ref, bias_s):
    rows = feat_ref.shape[1]
    for n in range(bias_ref.shape[0]):
        bias_s[n * LANES : (n + 1) * LANES, :] = 0.5 * columns_of(bias_ref[n : n + 1, :])
    lanes = chunk_of(rows, 768)

    def block(i, carry):
        cols = pl.ds(pl.multiple_of(i * lanes, lanes), lanes)
        half = feat_ref[:, cols] * jnp.asarray(0.5, BF)
        for at in range(0, w_ref.shape[1], 256):
            acc = dot(w_ref[:, at : at + 256], half, TN)
            part_ref[at : at + 256, cols] = (acc + tile_lanes(bias_s[at : at + 256, :], lanes)).astype(BF)
        gpart_ref[:, cols] = dot(wg_ref[...], half)
        return carry

    lax.fori_loop(0, rows // lanes, block, 0)


def relay_kernel(*refs):
    pass


def add_kernel(a_ref, b_ref, out_ref):
    out_ref[...] = a_ref[...] + b_ref[...]


def middle_kernel(
    groups_total,
    where_ref,
    rate_ref,
    own_ref,
    look_ref,
    rows_ref,
    p0_ref,
    p1_ref,
    p2_ref,
    p3_ref,
    q0_ref,
    q1_ref,
    q2_ref,
    q3_ref,
    wg_ref,
    part_ref,
    gpart_ref,
    bg_raw,
    wi_raw,
    bi_raw,
    wt_ref,
    bt_raw,
    wh_raw,
    bh_raw,
    labels_ref,
    weight_ref,
    slope_ref,
    feat_ref,
    dg_ref,
    w_ref,
    pred_ref,
    mix_keep_ref,
    mix_send_ref,
    pred_out_ref,
    bg_ref,
    wi_ref,
    bi_ref,
    bt_ref,
    wh_ref,
    bh_ref,
    wide_ref,
    sums_s,
    small_ref,
    hidden_ref,
    ds_ref,
    out_s,
    slope_s,
    dwt_s,
):
    rows = feat_ref.shape[1]
    lanes = out_s.shape[2]
    experts, h1, h2 = wi_raw.shape
    tasks, tower = wt_ref.shape[0], wt_ref.shape[1]
    one = jnp.asarray(1.0, BF)
    wi_ref[...] = wi_raw[...] * jnp.asarray(0.5, BF)
    for n in range(bi_raw.shape[0]):
        bi_ref[n * LANES : (n + 1) * LANES, :] = 0.5 * columns_of(bi_raw[n : n + 1, :])
    bt_ref[...] = columns_of(jnp.concatenate([bt_raw[t : t + 1, :] for t in range(tasks)], axis=1))
    wh_ref[...] = columns_of(jnp.concatenate([wh_raw[...][t : t + 1, :].astype(F32) for t in range(tasks)], axis=1))
    bg_ref[...] = small_column(bg_raw)
    bh_ref[...] = small_column(bh_raw)
    small_ref[...] = jnp.zeros_like(small_ref)
    dwt_s[...] = jnp.zeros_like(dwt_s)
    feat_ref[: look_ref.shape[0], :] = look_ref[...]
    feat_ref[look_ref.shape[0] :, :] = rows_ref[: feat_ref.shape[0] - look_ref.shape[0], :]
    quarter = jnp.bitwise_and(where_ref[0], 3)
    count = w_ref.shape[0] // 4
    some = count - q0_ref.shape[0]
    for flip, upper, lower in ((0, p0_ref, q0_ref), (2, p1_ref, q1_ref), (1, p2_ref, q2_ref), (3, p3_ref, q3_ref)):
        at = pl.multiple_of(jnp.bitwise_xor(quarter, flip) * count, 16)
        w_ref[pl.ds(at, some), :] = upper[:some, :]
        w_ref[pl.ds(at + some, count - some), :] = lower[...]
    rate = rate_ref[...]
    click = (rate + 1.0) / (groups_total + 2.0)
    entropy = -(click * jnp.log(click) + (1.0 - click) * jnp.log(1.0 - click))
    scale = tile_lanes(1.0 / (groups_total * entropy), lanes)

    def block(i, carry):
        cols = pl.ds(pl.multiple_of(i * lanes, lanes), lanes)
        source = pl.ds(pl.multiple_of(where_ref[1] * rows + i * lanes, LANES), lanes)
        half = feat_ref[:, cols] * jnp.asarray(0.5, BF)
        gate_logits = 2.0 * (gpart_ref[:, cols] + dot(wg_ref[...], half)) + tile_lanes(bg_ref[...], lanes)
        gates = []
        for t in range(tasks):
            logits = gate_logits[t * experts : (t + 1) * experts]
            top = jnp.exp(logits - jnp.max(logits, axis=0, keepdims=True))
            gates.append(top / jnp.sum(top, axis=0, keepdims=True))
        mixed = [jnp.zeros((h2, lanes), BF) for _ in range(tasks)]
        for e in range(experts):
            at = e * h1
            u = dot(w_ref[:, at : at + h1], half, TN).astype(BF) + part_ref[at : at + h1, cols]
            t1 = jnp.tanh(u)
            hidden = u + u * t1
            hidden_ref[at : at + h1, cols] = hidden
            slope_ref[at : at + h1, cols] = (one + hidden) + t1 * (one - hidden)
            u2 = dot(wi_ref[e], hidden, TN) + tile_lanes(bi_ref[e * h2 : (e + 1) * h2, :], lanes)
            t2 = jnp.tanh(u2)
            out = u2 + u2 * t2
            out = out.astype(BF)
            t2 = t2.astype(BF)
            out_s[e] = out
            slope_s[e] = (one + out) + t2 * (one - out)
            for t in range(tasks):
                mixed[t] = mixed[t] + gates[t][e : e + 1, :].astype(BF) * out
        labels = labels_ref[:, source].astype(F32)
        weight = weight_ref[:, source]
        preds, d_logits, losses, d_mixed = [], [], [], []
        for t in range(tasks):
            mine = slice(t * tower, (t + 1) * tower)
            low = mixed[t]
            tower_pre = dot(wt_ref[t], low) + tile_lanes(bt_ref[mine, :], lanes)
            sigma = 0.5 + 0.5 * jnp.tanh(0.5 * tower_pre)
            tower_out = (tower_pre * sigma).astype(BF).astype(F32)
            head = tile_lanes(wh_ref[mine, :], lanes)
            logit = jnp.sum(tower_out * head, axis=0, keepdims=True) + tile_lanes(bh_ref[t : t + 1, :], lanes)
            label = labels[t : t + 1]
            pred = jax.nn.sigmoid(logit)
            share = weight * scale[t : t + 1]
            plus = jnp.maximum(logit, 0.0) + jnp.log1p(jnp.exp(-jnp.abs(logit)))
            losses.append(share * (plus - label * logit))
            d_logit = share * (pred - label)
            preds.append(pred)
            d_logits.append(d_logit)
            d_tower = d_logit * head * (sigma * (1.0 + tower_pre * (1.0 - sigma)))
            d_low = d_tower.astype(BF)
            base = experts * h2
            small_ref[base + t * tower : base + (t + 1) * tower, :] += fold_lanes(d_tower)
            base = base + tasks * tower
            small_ref[base + t * tower : base + (t + 1) * tower, :] += fold_lanes(d_logit * tower_out)
            dwt_s[mine, :] += dot(d_low, low, NT)
            d_mixed.append(dot(wt_ref[t], d_low, TN))
        pred_ref[:, cols] = jnp.concatenate(preds, axis=0)
        base = experts * h2 + 2 * tasks * tower + tasks * experts
        small_ref[base : base + 8, :] += fold_lanes(
            jnp.concatenate(d_logits + losses + [jnp.zeros((8 - 2 * tasks, lanes), F32)], axis=0)
        )
        halves = [(0.5 * gate).astype(BF) for gate in gates]
        d_lows = [value.astype(BF) for value in d_mixed]
        d_gates = [[] for _ in range(tasks)]
        for e in range(experts):
            out = out_s[e].astype(F32)
            d_out = None
            for t in range(tasks):
                d_gates[t].append(jnp.sum(d_mixed[t] * out, axis=0, keepdims=True))
                term = halves[t][e : e + 1, :] * d_lows[t]
                d_out = term if d_out is None else d_out + term
            d_second = d_out * slope_s[e]
            small_ref[e * h2 : (e + 1) * h2, :] += fold_lanes(d_second.astype(F32))
            ds_ref[e * h2 : (e + 1) * h2, cols] = d_second
        d_all = []
        for t in range(tasks):
            d_gate = jnp.concatenate(d_gates[t], axis=0)
            d_all.append(gates[t] * (d_gate - jnp.sum(gates[t] * d_gate, axis=0, keepdims=True)))
        d_all = jnp.concatenate(d_all, axis=0)
        base = experts * h2 + 2 * tasks * tower
        small_ref[base : base + tasks * experts, :] += fold_lanes(d_all)
        dg_ref[:, cols] = d_all.astype(BF)
        return carry

    lax.fori_loop(0, rows // lanes, block, 0)

    part, tail = experts * h1 // 4, tasks * tower // 4
    for e in range(experts):
        d_wi = dot(hidden_ref[e * h1 : (e + 1) * h1, :], ds_ref[e * h2 : (e + 1) * h2, :], NT).astype(BF)
        at = e * h1
        base = at // part * (part + tail) + at % part
        wide_ref[base : base + h1, :] = d_wi
    for q in range(4):
        base = q * (part + tail) + part
        wide_ref[base : base + tail, :] = dwt_s[q * tail : (q + 1) * tail, :].astype(BF)
    core = jnp.bitwise_and(where_ref[0], 1)
    count = 2 * (part + tail)
    mix_keep_ref[:count, :] = wide_ref[pl.ds(pl.multiple_of(core * count, 32), count), :]
    mix_send_ref[:count, :] = wide_ref[pl.ds(pl.multiple_of((1 - core) * count, 32), count), :]

    sums_s[...] = jnp.zeros_like(sums_s)
    whole = experts * h2 // LANES + 2 * tasks * tower // LANES
    for g in range(whole):
        sums_s[g : g + 1, :] = jnp.sum(small_ref[g * LANES : (g + 1) * LANES, :].T, axis=0, keepdims=True)
    left = small_ref.shape[0] - whole * LANES
    sums_s[whole : whole + 1, :left] = jnp.sum(small_ref[whole * LANES :, :].T, axis=0, keepdims=True)
    step = chunk_of(rows, 768)
    for e in range(experts):
        r1, r2 = slice(e * h1, (e + 1) * h1), slice(e * h2, (e + 1) * h2)
        bias = jnp.zeros((h1, LANES), F32)
        for at in range(0, rows, step):
            cols = slice(at, at + step)
            d_pre = dot(wi_ref[e], ds_ref[r2, cols]) * slope_ref[r1, cols].astype(F32)
            bias = bias + fold_lanes(d_pre)
            slope_ref[r1, cols] = d_pre.astype(BF)
        row = jnp.sum(bias.T, axis=0, keepdims=True)
        for m in range(h1 // LANES):
            at = 16 + e * (h1 // LANES) + m
            sums_s[at : at + 1, :] = row[:, m * LANES : (m + 1) * LANES]
    for side, source in enumerate((own_ref, feat_ref)):
        d_wg = dot(dg_ref[...], source[...], NT)
        for m in range(d_wg.shape[1] // LANES):
            at = 32 + (2 * side + m) * 16
            sums_s[at : at + 16, :] = d_wg[:, m * LANES : (m + 1) * LANES]
    put_split(mix_keep_ref, count, sums_s[...])
    put_split(mix_send_ref, count, sums_s[...])
    pred = pred_ref[...]
    for m in range(rows // LANES):
        piece = pred[:, m * LANES : (m + 1) * LANES]
        high = piece.astype(BF)
        low = (piece - high.astype(F32)).astype(BF)
        split = jnp.concatenate([high.astype(F32), low.astype(F32)], axis=0)
        pred_out_ref[4 * m : 4 * m + 4, :] = split.astype(BF)
    pred_out_ref[4 * (rows // LANES) :, :] = jnp.zeros_like(pred_out_ref[4 * (rows // LANES) :, :])


def small_column(raw):
    count = raw.shape[1]
    same = lax.broadcasted_iota(jnp.int32, (count, count), 0) == lax.broadcasted_iota(jnp.int32, (count, count), 1)
    column = jnp.sum(jnp.where(same, jnp.broadcast_to(raw[...], (count, count)), 0.0), axis=1, keepdims=True)
    return jnp.broadcast_to(column, (count, LANES))


def put_split(target, at, value):
    count = value.shape[0]
    high = value.astype(BF)
    target[at : at + count, :] = high
    target[at + count : at + 2 * count, :] = (value - high.astype(F32)).astype(BF)


def get_split(source, at, count):
    return source[at : at + count, :].astype(F32) + source[at + count : at + 2 * count, :].astype(F32)


def weight_gradients(where_ref, dpre_ref, first, own_ref, oth_ref, keep_ref, send_ref):
    even = jnp.bitwise_and(where_ref[0], 1) == 0
    for n in range(keep_ref.shape[1]):
        at = first + n * 2 * LANES
        for side, source in enumerate((own_ref, oth_ref)):
            d_w = dot(source[...], dpre_ref[at : at + 2 * LANES, :], NT)
            one, two = d_w[:, :LANES], d_w[:, LANES:]
            keep_ref[side, n] = jnp.where(even, one, two).astype(BF)
            send_ref[side, n] = jnp.where(even, two, one).astype(BF)


def first_weight_kernel(where_ref, dpre_ref, own_ref, oth_ref, keep_ref, send_ref, _):
    weight_gradients(where_ref, dpre_ref, 0, own_ref, oth_ref, keep_ref, send_ref)


def feature_kernel(part, parts, where_ref, ids_ref, dpre_ref, dg_ref, w_ref, wg_ref, *refs):
    fields, emb = ids_ref.shape[0], 16
    rows = dg_ref.shape[1]
    lanes = chunk_of(rows, 2304 if parts == 1 else 1152)
    carried = refs[0] if part > 0 else None
    first = where_ref[1] * rows if ids_ref.shape[1] > rows else 0
    if part > 0:
        refs = refs[2:]
    if part == parts - 1:
        keep_ref, send_ref, send2_ref, ddense_ref, _, acc_s = refs
    else:
        acc_s, ddense_ref, _ = refs
    highs = acc_s.shape[1] // emb
    acc_s[...] = jnp.zeros_like(acc_s) if carried is None else carried[...]

    def block(i, carry):
        cols = pl.ds(pl.multiple_of(i * lanes, lanes), lanes)
        source = pl.ds(pl.multiple_of(first + i * lanes, LANES), lanes)
        d_feat = dot(w_ref[...], dpre_ref[:, cols]) + dot(wg_ref[...], dg_ref[:, cols], TN)
        ddense_ref[:, cols] = d_feat[fields * emb :, :].astype(ddense_ref.dtype)
        every = ids_ref[:, source]
        low = jnp.bitwise_and(every, LANES - 1)
        every = jnp.right_shift(every, 7)
        places = lax.broadcasted_iota(jnp.int32, (LANES, lanes), 0)
        for f in range(fields):
            hot = jnp.where(places == low[f : f + 1, :], 1.0, 0.0).astype(BF)
            high = jnp.broadcast_to(every[f : f + 1, :], (emb, lanes))
            grad = d_feat[f * emb : (f + 1) * emb, :]
            spread = jnp.concatenate([jnp.where(high == h, grad, 0.0) for h in range(highs)], axis=0)
            acc_s[f] += dot(spread.astype(BF), hot, NT)
        return carry

    steps = rows // lanes
    lax.fori_loop(steps * part // parts, steps * (part + 1) // parts, block, 0)
    if part < parts - 1:
        return
    even = jnp.bitwise_and(where_ref[0], 1) == 0
    left = lax.broadcasted_iota(jnp.int32, (emb, LANES), 1) < LANES // 2
    for p in range((fields + 1) // 2):
        rows_p = slice(p * emb, (p + 1) * emb)
        for h in range(highs):
            a = acc_s[2 * p, h * emb : (h + 1) * emb, :]
            b = acc_s[2 * p + 1, h * emb : (h + 1) * emb, :] if 2 * p + 1 < fields else jnp.zeros_like(a)
            first = jnp.where(left, a, pltpu.roll(b, LANES // 2, 1))
            second = jnp.where(left, pltpu.roll(a, LANES // 2, 1), b)
            keep_ref[h, rows_p, :] = jnp.where(even, first, second).astype(BF)
            out_ref, place = (send_ref, h) if h < highs // 2 else (send2_ref, h - highs // 2)
            out_ref[place, rows_p, :] = jnp.where(even, second, first).astype(BF)


def step_kernel(works, counts, where_ref, *refs):
    def bit(k):
        return jnp.bitwise_and(jnp.right_shift(where_ref[0], k), 1)

    ins = sum(n for n, _ in counts)
    a, b = 0, ins
    for work, (n_in, n_out) in zip(works, counts):
        work(refs[a : a + n_in], refs[b : b + n_out], bit, where_ref)
        a, b = a + n_in, b + n_out


def total(a, b, at, at_a=None):
    return a[at if at_a is None else at_a].astype(F32) + b[at].astype(F32)


def work_sum(ins, outs, bit, where):
    outs[0][...] = total(ins[0], ins[1], ...).astype(outs[0].dtype)


def work_sides(ins, outs, bit, where):
    for side in range(2):
        outs[side][...] = total(ins[0], ins[1], side).astype(outs[side].dtype)


def work_mix_core(ins, outs, bit, where):
    got, mine, pred = ins
    keep, send = outs
    count = keep.shape[0] - 128
    send[count + 128 :, :] = pred[...]
    sums = get_split(got, 2 * count, 96) + get_split(mine, 2 * count, 96)
    for out, half in ((keep, where[1]), (send, 1 - where[1])):
        out[:count, :] = total(got, mine, pl.ds(pl.multiple_of(half * count, 32), count)).astype(BF)
    put_split(keep, count, jnp.concatenate([sums[:32], sums[32:64]], axis=0))
    put_split(send, count, jnp.concatenate([sums[:32], sums[64:96]], axis=0))


def work_pred(ins, outs, bit, where):
    rows = outs[0].shape[1] // 2
    for side, source in ((where[1], ins[0]), (1 - where[1], ins[1])):
        base = source.shape[0] - ins[0].shape[0]
        for m in range(rows // LANES):
            at = base + 4 * m
            value = source[at : at + 2, :].astype(F32) + source[at + 2 : at + 4, :].astype(F32)
            outs[0][:, pl.ds(pl.multiple_of(side * rows + m * LANES, LANES), LANES)] = value


def work_mix(ins, outs, bit, where):
    count = outs[0].shape[0] - 128
    outs[0][:count, :] = total(ins[0], ins[1], slice(0, count)).astype(BF)
    put_split(outs[0], count, get_split(ins[0], count, 64) + get_split(ins[1], count, 64))


def work_mix_last(ins, outs, bit, where):
    quarter, inner, tower, head, gate, ends, loss, first, weights = outs
    count = ins[0].shape[0] - 128
    quarter[...] = total(ins[0], ins[1], slice(0, count)).astype(BF)
    sums = get_split(ins[0], count, 64) + get_split(ins[1], count, 64)
    inner[...] = sums[:8]
    half = tower.shape[1]
    for n in range(2):
        tower[n : n + 1, :] = sums[8:9, n * half : (n + 1) * half]
        head[n : n + 1, :] = sums[9:10, n * half : (n + 1) * half]
    gates = gate.shape[1]
    gate[...] = sums[10:11, :gates]
    ends[...] = sums[10:11, gates : gates + 2]
    loss[...] = sums[10:11, gates + 2 : gates + 3] + sums[10:11, gates + 3 : gates + 4]
    first[...] = sums[16:32]
    weights[:, :LANES] = sums[32:48]
    weights[:, LANES:] = sums[48:64]


def work_wide(ins, outs, bit, where):
    here = bit(0) * 2 + where[1]
    cut = outs[0].shape[1]
    for n, source in enumerate(ins):
        at = (here, jnp.bitwise_xor(here, 1), jnp.bitwise_xor(here, 2), jnp.bitwise_xor(here, 3))[n]
        outs[0][at] = source[:cut, :].astype(F32)
        outs[1][at] = source[cut:, :].astype(F32)


def work_dense(ins, outs, bit, where):
    mine, theirs = ins
    rows = mine.shape[1]
    outs[0][:, pl.ds(pl.multiple_of(where[1] * rows, LANES), rows)] = mine[...]
    outs[0][:, pl.ds(pl.multiple_of((1 - where[1]) * rows, LANES), rows)] = theirs[...].astype(F32)


def work_table(ins, outs, bit, where):
    value = total(ins[0], ins[1], 0)
    emb, half = outs[0].shape[1:]
    for f in range(outs[0].shape[0]):
        piece = value[f // 2 * emb : (f // 2 + 1) * emb]
        if f % 2:
            piece = pltpu.roll(piece, half, 1)
        outs[0][f] = piece[:, :half]


def work_add(ins, outs, bit, where):
    outs[0][...] = total(ins[0], ins[1], ...)


def work_pass(ins, outs, bit, where):
    outs[0][...] = ins[0][...]


def work_planes(ins, outs, bit, where):
    half = ins[0].shape[0]
    for n in range(2):
        outs[0][n * half : (n + 1) * half] = total(ins[n], ins[2], slice(n * half, (n + 1) * half), slice(None)).astype(BF)


def work_planes_halve(ins, outs, bit, where):
    count = outs[0].shape[0]
    for out, half in ((outs[0], bit(1)), (outs[1], 1 - bit(1))):
        for n in range(count):
            got, base = (ins[0], 0) if n < count // 2 else (ins[1], ins[0].shape[0])
            at = 2 * n + half
            out[n] = total(got, ins[2], at, at - base).astype(BF)


def work_halve(k):
    def work(ins, outs, bit, where):
        for out, half in ((outs[0], bit(k)), (outs[1], 1 - bit(k))):
            for n in range(out.shape[0]):
                out[n] = total(ins[0], ins[1], 2 * n + half).astype(out.dtype)

    return work


def work_two_ways(ins, outs, bit, where):
    half = ins[0].shape[1] // 2
    for side in range(2):
        for n in range(half):
            outs[side][n] = total(ins[0], ins[1], (side, n)).astype(BF)
    for out, which in ((outs[2], bit(1)), (outs[3], 1 - bit(1))):
        for side in range(2):
            for n in range(half // 2):
                out[side, n] = total(ins[0], ins[1], (side, half + 2 * n + which)).astype(BF)


def work_ends(ins, outs, bit, where):
    here = bit(3) * 2 + bit(2)
    for n, out in enumerate(outs):
        there = jnp.bitwise_xor(here, n)
        low = jnp.bitwise_and(there, 1)
        one, two = total(ins[0], ins[1], low), total(ins[2], ins[3], low)
        count = one.shape[0]
        out[:count, :] = jnp.where(there < 2, one, two).astype(BF)
        out[count:, :] = total(ins[4], ins[5], there).astype(BF)


def work_ends_last(ins, outs, bit, where):
    value = ins[0][...].astype(F32)
    for source in ins[1:]:
        value = value + source[...].astype(F32)
    count = outs[0].shape[0]
    outs[0][...] = value[:count]
    emb, half = outs[1].shape[1:]
    for f in range(outs[1].shape[0]):
        piece = value[count + f // 2 * emb : count + (f // 2 + 1) * emb]
        if f % 2:
            piece = pltpu.roll(piece, half, 1)
        outs[1][f] = piece[:, :half]


def chunk_of(rows, most):
    lanes = LANES
    for size in range(LANES, most + 1, LANES):
        if rows % size == 0:
            lanes = size
    return lanes


def sds(shape, dtype):
    return jax.ShapeDtypeStruct(shape, dtype)


def pinned(shape, dtype):
    return pltpu.VMEM(shape, dtype)


def run(kernel, name, outs, args, us, scalars=0, scratch=(), mib=16, alias=None, after=(), loose=False):
    vmem, smem = pl.BlockSpec(memory_space=pltpu.VMEM), pl.BlockSpec(memory_space=pltpu.SMEM)
    free = pl.BlockSpec(memory_space=pltpu.HBM if loose else pl.ANY)
    count = len(args)

    def body(*refs):
        kernel(*refs[:count], *refs[count + len(after) :])

    return pl.pallas_call(
        body,
        in_specs=[smem] * scalars + [free if loose else vmem] * (count - scalars) + [free] * len(after),
        out_specs=[vmem] * len(outs),
        out_shape=list(outs),
        scratch_shapes=list(scratch),
        input_output_aliases=alias or {},
        compiler_params=pltpu.CompilerParams(vmem_limit_bytes=mib * 1024 * 1024),
        cost_estimate=pl.CostEstimate(flops=int(us * SCALE), bytes_accessed=0, transcendentals=0),
        name=name,
    )(*args, *after)


def take_step(name, where, items, after=()):
    ins = [value for item in items for value in item[1]]
    outs = [shape for item in items for shape in item[2]]
    counts = [(len(item[1]), len(item[2])) for item in items]
    kernel = functools.partial(step_kernel, [item[0] for item in items], counts)
    got = run(kernel, name, outs, [where] + ins, ST, 1, mib=6, after=after)
    split, at = [], 0
    for _, count in counts:
        split.append(list(got[at : at + count]) if count > 1 else got[at])
        at += count
    return split


def relay(values, us, after=()):
    free = pl.BlockSpec(memory_space=pl.ANY)
    return pl.pallas_call(
        relay_kernel,
        in_specs=[free] * (len(values) + len(after)),
        out_specs=[free] * len(values),
        out_shape=[sds(value.shape, value.dtype) for value in values],
        input_output_aliases={n: n for n in range(len(values))},
        compiler_params=pltpu.CompilerParams(vmem_limit_bytes=1 << 20),
        cost_estimate=pl.CostEstimate(flops=int(us * SCALE), bytes_accessed=0, transcendentals=0),
        name="relay",
    )(*values, *after)


def add_low(a, b):
    return (a.astype(F32) + b.astype(F32)).astype(BF)


def ordered(bit, mine, theirs, axis):
    return jnp.where(
        bit == 0,
        jnp.concatenate([mine, theirs], axis=axis),
        jnp.concatenate([theirs, mine], axis=axis),
    )


def bit_of(rank, k):
    return jnp.bitwise_and(jnp.right_shift(rank, k), 1)


def per_device(
    dense, ids, table, sizes, labels, w_expert, b_expert, w_gate, b_gate, w_inner, b_inner, w_tower, b_tower, w_head, b_head
):
    n_rows = lax.axis_size("rows")
    n_bits = n_rows.bit_length() - 1
    rank, j = lax.axis_index("rows"), lax.axis_index("field")
    core = bit_of(rank, 0)
    rows_all, fields = ids.shape
    rows = rows_all // 2
    vocab, emb = table.shape[1], table.shape[2]
    dense_cols = dense.shape[1]
    width, n_expert = w_expert.shape
    experts, h1, h2 = w_inner.shape
    tasks, tower = w_head.shape
    gates = tasks * experts

    ids_t, dense_t, labels_t = ids.T, dense.T, labels.T
    table_t = jnp.transpose(table, (0, 2, 1))
    wg_own = w_gate.T
    where = jnp.stack([rank, j]).astype(jnp.int32)
    fast = n_rows * LANES == n_expert and n_rows * LANES == 2 * vocab

    def over_rows(value, bit):
        return swap(value, "rows", bit)

    def over_field(value):
        return swap(value, "field", 1)

    some = width // 16
    first, second, rows_away, weight, rate = run(
        pack_kernel,
        "pack",
        [
            sds((some + 2 * emb, n_expert), BF),
            sds((width // 4 - some, n_expert), BF),
            sds((dense_cols + 16, rows), BF),
            sds((1, rows_all), F32),
            sds((tasks, LANES), F32),
        ],
        [where, w_expert, table_t, wg_own, ids_t, dense_t, sizes, labels_t],
        2.0,
        1,
        [
            pltpu.VMEM((fields, emb, vocab // 4), F32),
            pltpu.VMEM(wg_own.shape, BF),
            pltpu.VMEM((fields, rows), jnp.int32),
            pltpu.VMEM(sizes.shape, jnp.int32),
            pltpu.VMEM(labels_t.shape, jnp.int32),
            pltpu.SemaphoreType.DMA((8,)),
        ],
        mib=60,
        loose=True,
    )
    p0, q0, rows_oth = over_field(first), over_field(second), over_field(rows_away)
    feat = pinned((width, rows), BF)
    rate_s = sds((tasks, LANES), F32)

    def click_sum(rate, k, after):
        return run(add_kernel, "click_sum", [rate_s], [rate, over_rows(rate, 1 << k)], 0.3, after=after, mib=2)[0]

    rate = click_sum(rate, 0, [])
    bias = b_expert.reshape(-1, LANES)
    feat_own, w_own, wg_here, bias = run(
        look_own_kernel,
        "look_own",
        [feat, pinned((width, n_expert), BF), pinned((gates, width), BF), pinned(bias.shape, F32)],
        [where, ids_t, dense_t, table_t, w_expert, wg_own, bias],
        0.3,
        1,
        [
            pltpu.VMEM((fields, rows), jnp.int32),
            pltpu.VMEM((fields, emb, vocab), F32),
            pltpu.SemaphoreType.DMA((6,)),
        ],
        mib=58,
        loose=True,
        after=[rate],
    )
    rate = click_sum(rate, 1, [feat_own])
    (p0,) = relay([p0], 0.1, [rate])
    (q0,) = relay([q0], 0.1, [rate])
    p1 = over_rows(p0, 2)
    p2, p3 = over_rows(p0, 1), over_rows(p1, 1)
    part, gpart = run(
        partial_kernel,
        "own_share",
        [pinned((n_expert, rows), BF), sds((gates, rows), F32)],
        [feat_own, w_own, wg_here, bias],
        0.3,
        0,
        [pltpu.VMEM((n_expert, LANES), F32)],
        mib=20,
        after=[p0],
    )
    rate = click_sum(rate, 2, [gpart])
    q1 = over_rows(q0, 2)
    q2, q3 = over_rows(q0, 1), over_rows(q1, 1)
    q2, q3 = relay([q2, q3], RQ)
    (ids_oth,) = run(unpack_kernel, "unpack", [sds((fields, rows), jnp.int32)], [rows_oth], UNP, mib=4)
    look_oth, wg_oth = run(
        look_other_kernel,
        "look_other",
        [pinned((fields * emb, rows), BF), sds((gates, width), BF)],
        [where, ids_oth, p0, p1, p2, p3],
        LO,
        1,
        [pltpu.VMEM((fields, emb, vocab), F32)],
            )

    for k in range(3, n_bits):
        rate = click_sum(rate, k, [look_oth])
    wide_rows = experts * h1 + tasks * tower
    small_rows = experts * h2 + 2 * tasks * tower + gates + 8
    mix_rows = wide_rows // 2 + 192
    blocks = n_expert // LANES // 2
    lanes = chunk_of(rows, 2304)
    mix_rows = wide_rows // 2 + 192
    blocks = n_expert // LANES // 2
    d_pre, feat_oth, d_gates, w_oth, _, mix_keep, mix_send, pred = run(
        functools.partial(middle_kernel, float(sizes.shape[1] * n_rows)),
        "middle",
        [
            pinned((n_expert, rows), BF),
            feat,
            sds((gates, rows), BF),
            sds((width, n_expert), BF),
            sds((tasks, rows), F32),
            sds((mix_rows, h2), BF),
            sds((mix_rows, h2), BF),
            sds((4 * (rows // LANES) + 8, LANES), BF),
        ],
        [
            where,
            rate,
            feat_own,
            look_oth,
            rows_oth,
            p0,
            p1,
            p2,
            p3,
            q0,
            q1,
            q2,
            q3,
            wg_oth,
            part,
            gpart,
            b_gate.reshape(1, -1),
            w_inner,
            b_inner,
            jnp.transpose(w_tower, (0, 2, 1)),
            b_tower,
            w_head,
            b_head.reshape(1, -1),
            labels_t,
            weight,
        ],
        23.0,
        1,
        [
            pltpu.VMEM((gates, LANES), F32),
            pltpu.VMEM((experts, h1, h2), BF),
            pltpu.VMEM((experts * h2, LANES), F32),
            pltpu.VMEM((tasks * tower, LANES), F32),
            pltpu.VMEM((tasks * tower, LANES), F32),
            pltpu.VMEM((tasks, LANES), F32),
            pltpu.VMEM((wide_rows, h2), BF),
            pltpu.VMEM((96, LANES), F32),
            pltpu.VMEM((small_rows, LANES), F32),
            pltpu.VMEM((n_expert, rows), BF),
            pltpu.VMEM((experts * h2, rows), BF),
            pltpu.VMEM((experts, h2, lanes), BF),
            pltpu.VMEM((experts, h2, lanes), BF),
            pltpu.VMEM((tasks * tower, h2), F32),
        ],
        mib=36,
        alias={14: 0},
    )

    held = pinned((n_expert, rows), BF)
    deep = (fields + 1) // 2 * emb
    highs = vocab // LANES
    quarter_rows = wide_rows // 4
    mix_s = sds((quarter_rows + 128, h2), BF)
    mix_long = sds((quarter_rows + 128 + pred.shape[0], h2), BF)

    def blocks_s(*shape):
        return sds(shape + (width, LANES), BF)

    def planes_s(count):
        return sds((count, deep, LANES), BF)

    def features_back(part, parts, ids_half, d_pre, w_half, wg_half, carried, dtype, name, after):
        outs = [sds((dense_cols, rows), dtype), held]
        scratch = [pltpu.VMEM((fields, highs * emb, LANES), F32)]
        if part == parts - 1:
            outs = [planes_s(highs), planes_s(highs // 2), planes_s(highs // 2)] + outs
        else:
            outs, scratch = [sds((fields, highs * emb, LANES), F32)] + outs, []
        alias = {2: len(outs) - 1}
        if part > 0:
            alias[7] = len(outs) - 2
        return run(
            functools.partial(feature_kernel, part, parts),
            name,
            outs,
            [where, ids_half, d_pre, d_gates, w_half, wg_half] + carried,
            FB / parts,
            1,
            scratch,
            alias=alias,
            after=after,
        )

    mix_got = over_rows(mix_send, 1)
    ((mix, mix_send),) = take_step("step_0", where, [(work_mix_core, [mix_got, mix_keep, pred], [mix_s, mix_long])])
    mix_got = over_field(mix_send)
    dw_keep, dw_send, d_pre = run(
        first_weight_kernel,
        "first_weights",
        [blocks_s(2, blocks), blocks_s(2, blocks), held],
        [where, d_pre, feat_own, feat_oth],
        FW,
        1,
        alias={1: 2},
        after=[mix],
    )
    predicted_s = sds((tasks, rows_all), F32)
    pred_work = (work_pred, [pred, mix_got], [predicted_s])
    (mix,) = take_step("step_1", where, [(work_mix, [mix_got, mix], [mix_s])], [dw_keep])
    if fast:
        (dw_send,) = relay([dw_send], 0.0, [mix])
        dw_got = over_rows(dw_send, 1)
    mix_got = over_rows(mix, 2)
    dt_keep, *dt_send, dd_oth, d_pre = features_back(
        0, 1, ids_oth, d_pre, w_oth, wg_oth, [], BF, "features_other", [mix]
    )
    mix_work = (work_mix, [mix_got, mix], [mix_s])
    if fast:
        dt_got = [over_rows(value, 1) for value in dt_send]
        (a_keep, a_send, b_keep, b_send), mix = take_step(
            "step_2",
            where,
            [
                (work_two_ways, [dw_got, dw_keep], [blocks_s(4), blocks_s(4), blocks_s(2, 2), blocks_s(2, 2)]),
                mix_work,
            ],
            [dt_keep],
        )
        a_got = over_field(a_send)
        b_got = over_rows(b_send, 2)
        mix_got = over_rows(mix, 4)
    else:
        (mix,) = take_step("step_2", where, [mix_work], [dt_keep])
    acc, dd_own, d_pre = features_back(0, 2, ids_t, d_pre, w_own, wg_own, [], F32, "features_own_0", [mix])
    if fast:
        dt_oth, mix = take_step(
            "step_3",
            where,
            [(work_planes, dt_got + [dt_keep], [planes_s(highs)]), (work_mix, [mix_got, mix], [mix_s])],
            [acc],
        )
        mix_got = over_rows(mix, 8)
        dt_far = over_field(dt_oth)
        after = [dt_oth]
    else:
        after = []
    do_keep, *do_send, dd_own, _ = features_back(
        1, 2, ids_t, d_pre, w_own, wg_own, [acc, dd_own], F32, "features_own_1", after
    )
    dense_s = sds((dense_cols, rows_all), F32)
    if fast:
        do_got = [over_rows(value, 1) for value in do_send]
        (a_keep, a_send), (b_keep, b_send) = take_step(
            "step_4",
            where,
            [
                (work_halve(1), [a_got, a_keep], [blocks_s(2)] * 2),
                (work_sides, [b_got, b_keep], [blocks_s(2)] * 2),
            ],
            [do_keep],
        )
        a_got = over_rows(a_send, 2)
        b_got = over_field(b_send)
        (do_keep,) = take_step("step_5", where, [(work_sum, [dt_far, do_keep], [planes_s(highs)])], [a_keep])
        (d_keep, d_send), dd_oth = take_step(
            "step_5b",
            where,
            [
                (work_planes_halve, do_got + [do_keep], [planes_s(highs // 2)] * 2),
                (work_pass, [dd_oth], [sds(dd_oth.shape, BF)]),
            ],
        )
        dd_got = over_field(dd_oth)
        d_got = over_rows(d_send, 2)
        ends_s = sds((width + deep, h2), BF)
        finals, predicted = take_step(
            "step_5c",
            where,
            [
                (
                    work_mix_last,
                    [mix_got, mix],
                    [
                        sds((quarter_rows, h2), BF),
                        sds((experts, h2), F32),
                        sds((tasks, tower), F32),
                        sds((tasks, tower), F32),
                        sds((1, gates), F32),
                        sds((1, tasks), F32),
                        sds((1, 1), F32),
                        sds((n_expert // LANES, LANES), F32),
                        sds((gates, width), F32),
                    ],
                ),
                pred_work,
            ],
            [d_keep],
        )
        (e_keep, e_low, e_high, e_both), = take_step(
            "step_6",
            where,
            [
                (work_ends, [a_got, a_keep, b_got, b_keep, d_got, d_keep], [ends_s] * 4),
            ],
            finals[:1],
        )
        e_got = [over_rows(value, bit) for value, bit in ((e_low, 4), (e_high, 8), (e_both, 12))]
        wide, d_b_inner, d_b_tower, d_w_head, d_b_gate, d_b_head, loss, d_b_expert, d_w_gate = finals
        wide_f, wide_c = over_field(wide), over_rows(wide, 1)
        wide_fc = lax.ppermute(wide, ("rows", "field"), [(i, i ^ 3) for i in range(2 * n_rows)])
        (d_w_expert, d_table), (d_w_inner, d_w_tower), d_dense = take_step(
            "step_8",
            where,
            [
                (
                    work_ends_last,
                    [e_keep] + e_got,
                    [sds((width, LANES), F32), sds((fields, emb, vocab // n_rows), F32)],
                ),
                (
                    work_wide,
                    [wide, wide_f, wide_c, wide_fc],
                    [sds((4, experts * h1 // 4, h2), F32), sds((4, tasks * tower // 4, h2), F32)],
                ),
                (work_dense, [dd_own, dd_got], [dense_s]),
            ],
        )
        d_table = jnp.transpose(d_table, (0, 2, 1))
        d_w_inner = d_w_inner.reshape(experts, h1, h2)
        d_w_tower = jnp.transpose(d_w_tower.reshape(tasks, tower, h2), (0, 2, 1))
    else:

        def by_core(keep, send, axis):
            return jnp.where(core == 0, jnp.stack([keep, send], axis), jnp.stack([send, keep], axis))

        def tables(keep, send):
            value = by_core(keep, send, 1).reshape(highs, 2, deep // emb, emb, 2, LANES // 2)
            return jnp.transpose(value, (2, 4, 3, 0, 1, 5)).reshape(deep // emb * 2, emb, vocab)[:fields]

        do_send, dt_send = jnp.concatenate(do_send), jnp.concatenate(dt_send)
        d_t = add_low(tables(do_keep, do_send), over_field(tables(dt_keep, dt_send))).astype(F32)
        d_table = jnp.transpose(lax.psum_scatter(d_t, "rows", scatter_dimension=2, tiled=True), (0, 2, 1))
        d_w = by_core(dw_keep, dw_send, 2).reshape(2, 2 * blocks, width, LANES)
        d_w = add_low(d_w[0], over_field(d_w[1])).astype(F32)
        d_w = jnp.transpose(d_w, (1, 0, 2)).reshape(width, n_expert)
        d_w_expert = lax.psum_scatter(d_w, "rows", scatter_dimension=1, tiled=True)
        sums = get_split(mix, quarter_rows, 64)
        wide = mix[:quarter_rows]
        for k in range(2, n_bits):
            wide = add_low(wide, over_rows(wide, 1 << k))
            sums = sums + over_rows(sums, 1 << k)
        wide = ordered(j, wide, over_field(wide), 0)
        wide = ordered(core, wide, over_rows(wide, 1), 0).astype(F32).reshape(4, quarter_rows, h2)
        cut = experts * h1 // 4
        d_w_inner = wide[:, :cut].reshape(experts, h1, h2)
        d_w_tower = jnp.transpose(wide[:, cut:].reshape(tasks, tower, h2), (0, 2, 1))
        d_b_inner, d_b_tower, d_w_head = sums[:8], sums[8], sums[9]
        d_b_gate, d_b_head = sums[10, :gates], sums[10, gates : gates + tasks]
        loss = jnp.sum(sums[10, gates + tasks : gates + 2 * tasks])
        d_b_expert = sums[16:32]
        d_w_gate = jnp.concatenate([sums[32:48], sums[48:64]], axis=1)
        d_dense, predicted = take_step(
            "rest", where, [(work_dense, [dd_own, over_field(dd_oth)], [dense_s]), pred_work]
        )

    return (
        predicted.T,
        loss.reshape(()),
        d_dense.T,
        d_table,
        d_w_expert,
        d_b_expert.reshape(n_expert),
        d_w_gate.T,
        d_b_gate.reshape(gates),
        d_w_inner,
        d_b_inner.reshape(experts, h2),
        d_w_tower,
        d_b_tower.reshape(tasks, tower),
        d_w_head.reshape(tasks, tower),
        d_b_head.reshape(tasks),
    )


def solution(mesh):
    return jax.shard_map(
        per_device,
        mesh=mesh,
        in_specs=(
            P("rows", "field"),
            P("rows", "field"),
            P("field", None, None),
            P("rows", None),
            P("rows", None),
            P("field", None),
            P(),
            P("field", None),
            P(),
            P(),
            P(),
            P(),
            P(),
            P(),
            P(),
        ),
        out_specs=(
            P("rows", None),
            P(),
            P("rows", "field"),
            P("field", "rows", None),
            P("field", "rows"),
            P(),
            P("field", None),
            P(),
            P(),
            P(),
            P(),
            P(),
            P(),
            P(),
        ),
        check_vma=False,
    )
```

```python
import functools

import jax
import jax.numpy as jnp
from jax import lax
from jax.experimental import pallas as pl
from jax.experimental.pallas import tpu as pltpu
from jax.sharding import PartitionSpec as P

BF = jnp.bfloat16
F32 = jnp.float32
LANES = 128
SCALE = 1.0e9
UNP = 2.0
FW, FB, ST = 0.5, 0.5, 0.3
LO = 4.0
RQ = 0.1

NN = (((1,), (0,)), ((), ()))
TN = (((0,), (0,)), ((), ()))
NT = (((1,), (1,)), ((), ()))


def dot(a, b, dims=NN):
    return lax.dot_general(a, b, dims, preferred_element_type=F32)


def swap(value, axis, bit):
    size = lax.axis_size(axis)
    return lax.ppermute(value, axis, [(i, i ^ bit) for i in range(size)])


def columns_of(row):
    return jnp.broadcast_to(row, (LANES, LANES)).T


def tile_lanes(column, lanes):
    return jnp.concatenate([column] * (lanes // LANES), axis=1)


def fold_lanes(value):
    total = value[:, :LANES]
    for start in range(LANES, value.shape[1], LANES):
        total = total + value[:, start : start + LANES]
    return total


def pack_kernel(
    where_ref,
    w_ref,
    table_ref,
    wg_ref,
    ids_ref,
    dense_ref,
    sizes_ref,
    labels_ref,
    first_ref,
    second_ref,
    rows_ref,
    weight_ref,
    rate_ref,
    table_s,
    wg_s,
    ids_s,
    sizes_s,
    labels_s,
    sems,
):
    quarter = jnp.bitwise_and(where_ref[0], 3)
    fields, emb, vocab = table_ref.shape
    lanes = table_s.shape[2]
    dense_cols, rows = dense_ref.shape[0], rows_ref.shape[1]
    some, count = w_ref.shape[0] // 4 - second_ref.shape[0], w_ref.shape[0] // 4
    away = pl.ds(pl.multiple_of((1 - where_ref[1]) * rows, LANES), rows)
    base = pl.multiple_of(quarter * count, 16)
    copies = [
        pltpu.make_async_copy(w_ref.at[pl.ds(base, some), :], first_ref.at[:some, :], sems.at[0]),
        pltpu.make_async_copy(w_ref.at[pl.ds(base + some, count - some), :], second_ref, sems.at[1]),
        pltpu.make_async_copy(
            table_ref.at[:, :, pl.ds(pl.multiple_of(quarter * lanes, LANES), lanes)], table_s, sems.at[2]
        ),
        pltpu.make_async_copy(wg_ref, wg_s, sems.at[3]),
        pltpu.make_async_copy(ids_ref.at[:, away], ids_s, sems.at[4]),
        pltpu.make_async_copy(dense_ref.at[:, away], rows_ref.at[:dense_cols, :], sems.at[5]),
        pltpu.make_async_copy(sizes_ref, sizes_s, sems.at[6]),
        pltpu.make_async_copy(labels_ref, labels_s, sems.at[7]),
    ]
    for copy in copies:
        copy.start()
    for copy in copies:
        copy.wait()
    sizes_ref, labels_ref = sizes_s, labels_s
    for f in range(fields):
        at = some + f % 2 * emb
        first_ref[at : at + emb, f // 2 * lanes : (f // 2 + 1) * lanes] = table_s[f].astype(BF)
    at = some + fields % 2 * emb
    first_ref[at : at + emb, fields // 2 * lanes : (fields // 2 + 1) * lanes] = wg_s[...]
    first_ref[some:, (fields // 2 + 1) * lanes :] = jnp.zeros_like(first_ref[some:, (fields // 2 + 1) * lanes :])
    ids = ids_s[...]
    value = (jnp.bitwise_and(ids, 127) + 128).astype(F32)
    for k in range(3):
        up = float(1 << (1 << k))
        value = value * jnp.where(jnp.bitwise_and(jnp.right_shift(ids, 7 + k), 1) == 1, up, 1.0)
    rows_ref[dense_cols : dense_cols + fields, :] = value.astype(BF)
    rows_ref[dense_cols + fields :, :] = jnp.zeros_like(rows_ref[dense_cols + fields :, :])
    groups, rows = sizes_ref.shape[1], labels_ref.shape[1]
    sizes = jnp.broadcast_to(sizes_ref[...].astype(F32), (groups, groups))
    below = lax.broadcasted_iota(jnp.int32, (groups, groups), 0)
    across = lax.broadcasted_iota(jnp.int32, (groups, groups), 1)
    starts = jnp.sum(jnp.where(across < below, sizes, 0.0), axis=1, keepdims=True)
    own = jnp.sum(jnp.where(across == below, sizes, 0.0), axis=1, keepdims=True)
    ends = starts + own
    share = 1.0 / own
    rate = jnp.zeros((2, LANES), F32)
    for at in range(0, rows, 256):
        place = (lax.broadcasted_iota(jnp.int32, (groups, 256), 1) + at).astype(F32)
        inside = (place >= starts) & (place < ends)
        weight = jnp.sum(jnp.where(inside, share, 0.0), axis=0, keepdims=True)
        weight_ref[:, at : at + 256] = weight
        rate = rate + fold_lanes(weight * labels_ref[:, at : at + 256].astype(F32))
    rate_ref[...] = jnp.broadcast_to(jnp.sum(rate, axis=1, keepdims=True), rate_ref.shape)


def look_up(ids_ref, first, table_ref, feat_ref, rows, dense_ref=None):
    fields, emb, vocab = table_ref.shape
    lanes = 256

    def block(i, carry):
        source = pl.ds(pl.multiple_of(first + i * lanes, lanes), lanes)
        target = pl.multiple_of(i * lanes, lanes)
        every = ids_ref[:, source]
        for f in range(fields):
            for at in range(0, lanes, LANES):
                ids = every[f : f + 1, at : at + LANES]
                low = jnp.broadcast_to(jnp.bitwise_and(ids, LANES - 1), (emb, LANES))
                high = jnp.broadcast_to(jnp.right_shift(ids, 7), (emb, LANES))
                found = None
                for h in range(vocab // LANES):
                    piece = table_ref[f, :, h * LANES : (h + 1) * LANES]
                    piece = jnp.take_along_axis(piece, low, axis=1, mode="promise_in_bounds")
                    found = piece if found is None else jnp.where(high == h, piece, found)
                feat_ref[f * emb : (f + 1) * emb, pl.ds(target + at, LANES)] = found.astype(BF)
        if dense_ref is not None:
            feat_ref[fields * emb :, pl.ds(target, lanes)] = dense_ref[:, source]
        return carry

    lax.fori_loop(0, rows // lanes, block, 0)


def look_own_kernel(
    where_ref, ids_ref, dense_ref, table_ref, w_in, wg_in, bias_in, feat_ref, w_ref, wg_ref, bias_ref, ids_s, table_s, sems
):
    rows = feat_ref.shape[1]
    fields, emb, _ = table_ref.shape
    mine = pl.ds(pl.multiple_of(where_ref[1] * rows, LANES), rows)
    copies = [
        pltpu.make_async_copy(ids_ref.at[:, mine], ids_s, sems.at[0]),
        pltpu.make_async_copy(table_ref, table_s, sems.at[1]),
        pltpu.make_async_copy(dense_ref.at[:, mine], feat_ref.at[fields * emb :, :], sems.at[2]),
        pltpu.make_async_copy(bias_in, bias_ref, sems.at[3]),
        pltpu.make_async_copy(wg_in, wg_ref, sems.at[4]),
        pltpu.make_async_copy(w_in, w_ref, sems.at[5]),
    ]
    for copy in copies:
        copy.start()
    for copy in copies[:2]:
        copy.wait()
    look_up(ids_s, 0, table_s, feat_ref, rows)
    for copy in copies[2:]:
        copy.wait()


def unpack_kernel(rows_ref, ids_ref):
    fields = ids_ref.shape[0]
    dense_cols = rows_ref.shape[0] - 16
    value = rows_ref[dense_cols : dense_cols + fields, :].astype(F32)
    high = jnp.zeros(value.shape, jnp.int32)
    for k in range(2, -1, -1):
        up = float(1 << (1 << k))
        over = value >= 128.0 * up
        value = jnp.where(over, value * (1.0 / up), value)
        high = high + jnp.where(over, 1 << k, 0)
    ids_ref[...] = high * 128 + (value.astype(jnp.int32) - 128)


def look_other_kernel(where_ref, ids_ref, p0_ref, p1_ref, p2_ref, p3_ref, feat_ref, wg_ref, table_s):
    fields, emb, vocab = table_s.shape
    lanes, some = vocab // 4, p0_ref.shape[0] - 2 * emb
    quarter = jnp.bitwise_and(where_ref[0], 3)
    for flip, source in ((0, p0_ref), (2, p1_ref), (1, p2_ref), (3, p3_ref)):
        at = pl.multiple_of(jnp.bitwise_xor(quarter, flip) * lanes, LANES)
        for f in range(fields):
            top = some + f % 2 * emb
            piece = source[top : top + emb, f // 2 * lanes : (f // 2 + 1) * lanes]
            table_s[f, :, pl.ds(at, lanes)] = piece.astype(F32)
    top = some + fields % 2 * emb
    wg_ref[...] = p0_ref[top : top + emb, fields // 2 * lanes : (fields // 2 + 1) * lanes]
    look_up(ids_ref, 0, table_s, feat_ref, feat_ref.shape[1])


def partial_kernel(feat_ref, w_ref, wg_ref, bias_ref, part_ref, gpart_ref, bias_s):
    rows = feat_ref.shape[1]
    for n in range(bias_ref.shape[0]):
        bias_s[n * LANES : (n + 1) * LANES, :] = 0.5 * columns_of(bias_ref[n : n + 1, :])
    lanes = chunk_of(rows, 768)

    def block(i, carry):
        cols = pl.ds(pl.multiple_of(i * lanes, lanes), lanes)
        half = feat_ref[:, cols] * jnp.asarray(0.5, BF)
        for at in range(0, w_ref.shape[1], 256):
            acc = dot(w_ref[:, at : at + 256], half, TN)
            part_ref[at : at + 256, cols] = (acc + tile_lanes(bias_s[at : at + 256, :], lanes)).astype(BF)
        gpart_ref[:, cols] = dot(wg_ref[...], half)
        return carry

    lax.fori_loop(0, rows // lanes, block, 0)


def relay_kernel(*refs):
    pass


def add_kernel(a_ref, b_ref, out_ref):
    out_ref[...] = a_ref[...] + b_ref[...]


def middle_kernel(
    groups_total,
    where_ref,
    rate_ref,
    own_ref,
    look_ref,
    rows_ref,
    p0_ref,
    p1_ref,
    p2_ref,
    p3_ref,
    q0_ref,
    q1_ref,
    q2_ref,
    q3_ref,
    wg_ref,
    part_ref,
    gpart_ref,
    bg_raw,
    wi_raw,
    bi_raw,
    wt_ref,
    bt_raw,
    wh_raw,
    bh_raw,
    labels_ref,
    weight_ref,
    slope_ref,
    feat_ref,
    dg_ref,
    w_ref,
    pred_ref,
    mix_keep_ref,
    mix_send_ref,
    pred_out_ref,
    bg_ref,
    wi_ref,
    bi_ref,
    bt_ref,
    wh_ref,
    bh_ref,
    wide_ref,
    sums_s,
    small_ref,
    hidden_ref,
    ds_ref,
    out_s,
    slope_s,
    dwt_s,
):
    rows = feat_ref.shape[1]
    lanes = out_s.shape[2]
    experts, h1, h2 = wi_raw.shape
    tasks, tower = wt_ref.shape[0], wt_ref.shape[1]
    one = jnp.asarray(1.0, BF)
    wi_ref[...] = wi_raw[...] * jnp.asarray(0.5, BF)
    for n in range(bi_raw.shape[0]):
        bi_ref[n * LANES : (n + 1) * LANES, :] = (0.5 * columns_of(bi_raw[n : n + 1, :])).astype(BF)
    bt_ref[...] = columns_of(jnp.concatenate([bt_raw[t : t + 1, :] for t in range(tasks)], axis=1))
    wh_ref[...] = columns_of(jnp.concatenate([wh_raw[...][t : t + 1, :].astype(F32) for t in range(tasks)], axis=1))
    bg_ref[...] = small_column(bg_raw)
    bh_ref[...] = small_column(bh_raw)
    small_ref[...] = jnp.zeros_like(small_ref)
    dwt_s[...] = jnp.zeros_like(dwt_s)
    feat_ref[: look_ref.shape[0], :] = look_ref[...]
    feat_ref[look_ref.shape[0] :, :] = rows_ref[: feat_ref.shape[0] - look_ref.shape[0], :]
    quarter = jnp.bitwise_and(where_ref[0], 3)
    count = w_ref.shape[0] // 4
    some = count - q0_ref.shape[0]
    for flip, upper, lower in ((0, p0_ref, q0_ref), (2, p1_ref, q1_ref), (1, p2_ref, q2_ref), (3, p3_ref, q3_ref)):
        at = pl.multiple_of(jnp.bitwise_xor(quarter, flip) * count, 16)
        w_ref[pl.ds(at, some), :] = upper[:some, :]
        w_ref[pl.ds(at + some, count - some), :] = lower[...]
    rate = rate_ref[...]
    click = (rate + 1.0) / (groups_total + 2.0)
    entropy = -(click * jnp.log(click) + (1.0 - click) * jnp.log(1.0 - click))
    scale = tile_lanes(1.0 / (groups_total * entropy), lanes)

    def block(i, carry):
        cols = pl.ds(pl.multiple_of(i * lanes, lanes), lanes)
        source = pl.ds(pl.multiple_of(where_ref[1] * rows + i * lanes, LANES), lanes)
        half = feat_ref[:, cols] * jnp.asarray(0.5, BF)
        gate_logits = 2.0 * (gpart_ref[:, cols] + dot(wg_ref[...], half)) + tile_lanes(bg_ref[...], lanes)
        gates = []
        for t in range(tasks):
            logits = gate_logits[t * experts : (t + 1) * experts]
            top = jnp.exp(logits - jnp.max(logits, axis=0, keepdims=True))
            gates.append(top / jnp.sum(top, axis=0, keepdims=True))
        mixed = [jnp.zeros((h2, lanes), BF) for _ in range(tasks)]
        for e in range(experts):
            at = e * h1
            u = dot(w_ref[:, at : at + h1], half, TN).astype(BF) + part_ref[at : at + h1, cols]
            t1 = jnp.tanh(u)
            hidden = u + u * t1
            hidden_ref[at : at + h1, cols] = hidden
            slope_ref[at : at + h1, cols] = (one + hidden) + t1 * (one - hidden)
            u2 = dot(wi_ref[e], hidden, TN).astype(BF) + tile_lanes(bi_ref[e * h2 : (e + 1) * h2, :], lanes)
            t2 = jnp.tanh(u2)
            out = u2 + u2 * t2
            out_s[e] = out
            slope_s[e] = (one + out) + t2 * (one - out)
            for t in range(tasks):
                mixed[t] = mixed[t] + gates[t][e : e + 1, :].astype(BF) * out
        labels = labels_ref[:, source].astype(F32)
        weight = weight_ref[:, source]
        preds, d_logits, losses, d_mixed = [], [], [], []
        for t in range(tasks):
            mine = slice(t * tower, (t + 1) * tower)
            low = mixed[t]
            tower_pre = dot(wt_ref[t], low) + tile_lanes(bt_ref[mine, :], lanes)
            sigma = 0.5 + 0.5 * jnp.tanh(0.5 * tower_pre)
            tower_out = (tower_pre * sigma).astype(BF).astype(F32)
            head = tile_lanes(wh_ref[mine, :], lanes)
            logit = jnp.sum(tower_out * head, axis=0, keepdims=True) + tile_lanes(bh_ref[t : t + 1, :], lanes)
            label = labels[t : t + 1]
            pred = jax.nn.sigmoid(logit)
            share = weight * scale[t : t + 1]
            plus = jnp.maximum(logit, 0.0) + jnp.log1p(jnp.exp(-jnp.abs(logit)))
            losses.append(share * (plus - label * logit))
            d_logit = share * (pred - label)
            preds.append(pred)
            d_logits.append(d_logit)
            d_tower = d_logit * head * (sigma * (1.0 + tower_pre * (1.0 - sigma)))
            d_low = d_tower.astype(BF)
            base = experts * h2
            small_ref[base + t * tower : base + (t + 1) * tower, :] += fold_lanes(d_tower)
            base = base + tasks * tower
            small_ref[base + t * tower : base + (t + 1) * tower, :] += fold_lanes(d_logit * tower_out)
            dwt_s[mine, :] += dot(d_low, low, NT)
            d_mixed.append(dot(wt_ref[t], d_low, TN))
        pred_ref[:, cols] = jnp.concatenate(preds, axis=0)
        base = experts * h2 + 2 * tasks * tower + tasks * experts
        small_ref[base : base + 8, :] += fold_lanes(
            jnp.concatenate(d_logits + losses + [jnp.zeros((8 - 2 * tasks, lanes), F32)], axis=0)
        )
        halves = [(0.5 * gate).astype(BF) for gate in gates]
        d_lows = [value.astype(BF) for value in d_mixed]
        d_gates = [[] for _ in range(tasks)]
        for e in range(experts):
            out = out_s[e]
            d_out = None
            for t in range(tasks):
                product = d_lows[t] * out
                product = (product[: h2 // 2] + product[h2 // 2 :]).astype(F32)
                d_gates[t].append(jnp.sum(product, axis=0, keepdims=True))
                term = halves[t][e : e + 1, :] * d_lows[t]
                d_out = term if d_out is None else d_out + term
            d_second = d_out * slope_s[e]
            small_ref[e * h2 : (e + 1) * h2, :] += fold_lanes(d_second.astype(F32))
            ds_ref[e * h2 : (e + 1) * h2, cols] = d_second
        d_all = []
        for t in range(tasks):
            d_gate = jnp.concatenate(d_gates[t], axis=0)
            d_all.append(gates[t] * (d_gate - jnp.sum(gates[t] * d_gate, axis=0, keepdims=True)))
        d_all = jnp.concatenate(d_all, axis=0)
        base = experts * h2 + 2 * tasks * tower
        small_ref[base : base + tasks * experts, :] += fold_lanes(d_all)
        dg_ref[:, cols] = d_all.astype(BF)
        return carry

    lax.fori_loop(0, rows // lanes, block, 0)

    part, tail = experts * h1 // 4, tasks * tower // 4
    for e in range(experts):
        d_wi = dot(hidden_ref[e * h1 : (e + 1) * h1, :], ds_ref[e * h2 : (e + 1) * h2, :], NT).astype(BF)
        at = e * h1
        base = at // part * (part + tail) + at % part
        wide_ref[base : base + h1, :] = d_wi
    for q in range(4):
        base = q * (part + tail) + part
        wide_ref[base : base + tail, :] = dwt_s[q * tail : (q + 1) * tail, :].astype(BF)
    core = jnp.bitwise_and(where_ref[0], 1)
    count = 2 * (part + tail)
    mix_keep_ref[:count, :] = wide_ref[pl.ds(pl.multiple_of(core * count, 32), count), :]
    mix_send_ref[:count, :] = wide_ref[pl.ds(pl.multiple_of((1 - core) * count, 32), count), :]

    sums_s[...] = jnp.zeros_like(sums_s)
    whole = experts * h2 // LANES + 2 * tasks * tower // LANES
    for g in range(whole):
        sums_s[g : g + 1, :] = jnp.sum(small_ref[g * LANES : (g + 1) * LANES, :].T, axis=0, keepdims=True)
    left = small_ref.shape[0] - whole * LANES
    sums_s[whole : whole + 1, :left] = jnp.sum(small_ref[whole * LANES :, :].T, axis=0, keepdims=True)
    step = chunk_of(rows, 768)
    for e in range(experts):
        r1, r2 = slice(e * h1, (e + 1) * h1), slice(e * h2, (e + 1) * h2)
        bias = jnp.zeros((h1, LANES), F32)
        for at in range(0, rows, step):
            cols = slice(at, at + step)
            d_pre = dot(wi_ref[e], ds_ref[r2, cols]) * slope_ref[r1, cols].astype(F32)
            bias = bias + fold_lanes(d_pre)
            slope_ref[r1, cols] = d_pre.astype(BF)
        row = jnp.sum(bias.T, axis=0, keepdims=True)
        for m in range(h1 // LANES):
            at = 16 + e * (h1 // LANES) + m
            sums_s[at : at + 1, :] = row[:, m * LANES : (m + 1) * LANES]
    for side, source in enumerate((own_ref, feat_ref)):
        d_wg = dot(dg_ref[...], source[...], NT)
        for m in range(d_wg.shape[1] // LANES):
            at = 32 + (2 * side + m) * 16
            sums_s[at : at + 16, :] = d_wg[:, m * LANES : (m + 1) * LANES]
    put_split(mix_keep_ref, count, sums_s[...])
    put_split(mix_send_ref, count, sums_s[...])
    pred = pred_ref[...]
    for m in range(rows // LANES):
        piece = pred[:, m * LANES : (m + 1) * LANES]
        high = piece.astype(BF)
        low = (piece - high.astype(F32)).astype(BF)
        split = jnp.concatenate([high.astype(F32), low.astype(F32)], axis=0)
        pred_out_ref[4 * m : 4 * m + 4, :] = split.astype(BF)
    pred_out_ref[4 * (rows // LANES) :, :] = jnp.zeros_like(pred_out_ref[4 * (rows // LANES) :, :])


def small_column(raw):
    count = raw.shape[1]
    same = lax.broadcasted_iota(jnp.int32, (count, count), 0) == lax.broadcasted_iota(jnp.int32, (count, count), 1)
    column = jnp.sum(jnp.where(same, jnp.broadcast_to(raw[...], (count, count)), 0.0), axis=1, keepdims=True)
    return jnp.broadcast_to(column, (count, LANES))


def put_split(target, at, value):
    count = value.shape[0]
    high = value.astype(BF)
    target[at : at + count, :] = high
    target[at + count : at + 2 * count, :] = (value - high.astype(F32)).astype(BF)


def get_split(source, at, count):
    return source[at : at + count, :].astype(F32) + source[at + count : at + 2 * count, :].astype(F32)


def weight_gradients(where_ref, dpre_ref, first, own_ref, oth_ref, keep_ref, send_ref):
    even = jnp.bitwise_and(where_ref[0], 1) == 0
    for n in range(keep_ref.shape[1]):
        at = first + n * 2 * LANES
        for side, source in enumerate((own_ref, oth_ref)):
            d_w = dot(source[...], dpre_ref[at : at + 2 * LANES, :], NT)
            one, two = d_w[:, :LANES], d_w[:, LANES:]
            keep_ref[side, n] = jnp.where(even, one, two).astype(BF)
            send_ref[side, n] = jnp.where(even, two, one).astype(BF)


def first_weight_kernel(where_ref, dpre_ref, own_ref, oth_ref, keep_ref, send_ref, _):
    weight_gradients(where_ref, dpre_ref, 0, own_ref, oth_ref, keep_ref, send_ref)


def feature_kernel(part, parts, where_ref, ids_ref, dpre_ref, dg_ref, w_ref, wg_ref, *refs):
    fields, emb = ids_ref.shape[0], 16
    rows = dg_ref.shape[1]
    lanes = chunk_of(rows, 2304 if parts == 1 else 1152)
    carried = refs[0] if part > 0 else None
    first = where_ref[1] * rows if ids_ref.shape[1] > rows else 0
    if part > 0:
        refs = refs[2:]
    if part == parts - 1:
        keep_ref, send_ref, send2_ref, ddense_ref, _, acc_s = refs
    else:
        acc_s, ddense_ref, _ = refs
    highs = acc_s.shape[1] // emb
    acc_s[...] = jnp.zeros_like(acc_s) if carried is None else carried[...]

    def block(i, carry):
        cols = pl.ds(pl.multiple_of(i * lanes, lanes), lanes)
        source = pl.ds(pl.multiple_of(first + i * lanes, LANES), lanes)
        d_feat = dot(w_ref[...], dpre_ref[:, cols]) + dot(wg_ref[...], dg_ref[:, cols], TN)
        ddense_ref[:, cols] = d_feat[fields * emb :, :].astype(ddense_ref.dtype)
        every = ids_ref[:, source]
        low = jnp.bitwise_and(every, LANES - 1)
        every = jnp.right_shift(every, 7)
        places = lax.broadcasted_iota(jnp.int32, (LANES, lanes), 0)
        for f in range(fields):
            hot = jnp.where(places == low[f : f + 1, :], 1.0, 0.0).astype(BF)
            high = jnp.broadcast_to(every[f : f + 1, :], (emb, lanes))
            grad = d_feat[f * emb : (f + 1) * emb, :]
            spread = jnp.concatenate([jnp.where(high == h, grad, 0.0) for h in range(highs)], axis=0)
            acc_s[f] += dot(spread.astype(BF), hot, NT)
        return carry

    steps = rows // lanes
    lax.fori_loop(steps * part // parts, steps * (part + 1) // parts, block, 0)
    if part < parts - 1:
        return
    even = jnp.bitwise_and(where_ref[0], 1) == 0
    left = lax.broadcasted_iota(jnp.int32, (emb, LANES), 1) < LANES // 2
    for p in range((fields + 1) // 2):
        rows_p = slice(p * emb, (p + 1) * emb)
        for h in range(highs):
            a = acc_s[2 * p, h * emb : (h + 1) * emb, :]
            b = acc_s[2 * p + 1, h * emb : (h + 1) * emb, :] if 2 * p + 1 < fields else jnp.zeros_like(a)
            first = jnp.where(left, a, pltpu.roll(b, LANES // 2, 1))
            second = jnp.where(left, pltpu.roll(a, LANES // 2, 1), b)
            keep_ref[h, rows_p, :] = jnp.where(even, first, second).astype(BF)
            out_ref, place = (send_ref, h) if h < highs // 2 else (send2_ref, h - highs // 2)
            out_ref[place, rows_p, :] = jnp.where(even, second, first).astype(BF)


def step_kernel(works, counts, where_ref, *refs):
    def bit(k):
        return jnp.bitwise_and(jnp.right_shift(where_ref[0], k), 1)

    ins = sum(n for n, _ in counts)
    a, b = 0, ins
    for work, (n_in, n_out) in zip(works, counts):
        work(refs[a : a + n_in], refs[b : b + n_out], bit, where_ref)
        a, b = a + n_in, b + n_out


def total(a, b, at, at_a=None):
    return a[at if at_a is None else at_a].astype(F32) + b[at].astype(F32)


def work_sum(ins, outs, bit, where):
    outs[0][...] = total(ins[0], ins[1], ...).astype(outs[0].dtype)


def work_sides(ins, outs, bit, where):
    for side in range(2):
        outs[side][...] = total(ins[0], ins[1], side).astype(outs[side].dtype)


def work_mix_core(ins, outs, bit, where):
    got, mine, pred = ins
    keep, send = outs
    count = keep.shape[0] - 128
    send[count + 128 :, :] = pred[...]
    sums = get_split(got, 2 * count, 96) + get_split(mine, 2 * count, 96)
    for out, half in ((keep, where[1]), (send, 1 - where[1])):
        out[:count, :] = total(got, mine, pl.ds(pl.multiple_of(half * count, 32), count)).astype(BF)
    put_split(keep, count, jnp.concatenate([sums[:32], sums[32:64]], axis=0))
    put_split(send, count, jnp.concatenate([sums[:32], sums[64:96]], axis=0))


def work_pred(ins, outs, bit, where):
    rows = outs[0].shape[1] // 2
    for side, source in ((where[1], ins[0]), (1 - where[1], ins[1])):
        base = source.shape[0] - ins[0].shape[0]
        for m in range(rows // LANES):
            at = base + 4 * m
            value = source[at : at + 2, :].astype(F32) + source[at + 2 : at + 4, :].astype(F32)
            outs[0][:, pl.ds(pl.multiple_of(side * rows + m * LANES, LANES), LANES)] = value


def work_mix(ins, outs, bit, where):
    count = outs[0].shape[0] - 128
    outs[0][:count, :] = total(ins[0], ins[1], slice(0, count)).astype(BF)
    put_split(outs[0], count, get_split(ins[0], count, 64) + get_split(ins[1], count, 64))


def work_mix_last(ins, outs, bit, where):
    quarter, inner, tower, head, gate, ends, loss, first, weights = outs
    count = ins[0].shape[0] - 128
    quarter[...] = total(ins[0], ins[1], slice(0, count)).astype(BF)
    sums = get_split(ins[0], count, 64) + get_split(ins[1], count, 64)
    inner[...] = sums[:8]
    half = tower.shape[1]
    for n in range(2):
        tower[n : n + 1, :] = sums[8:9, n * half : (n + 1) * half]
        head[n : n + 1, :] = sums[9:10, n * half : (n + 1) * half]
    gates = gate.shape[1]
    gate[...] = sums[10:11, :gates]
    ends[...] = sums[10:11, gates : gates + 2]
    loss[...] = sums[10:11, gates + 2 : gates + 3] + sums[10:11, gates + 3 : gates + 4]
    first[...] = sums[16:32]
    weights[:, :LANES] = sums[32:48]
    weights[:, LANES:] = sums[48:64]


def work_wide(ins, outs, bit, where):
    here = bit(0) * 2 + where[1]
    cut = outs[0].shape[1]
    for n, source in enumerate(ins):
        at = (here, jnp.bitwise_xor(here, 1), jnp.bitwise_xor(here, 2), jnp.bitwise_xor(here, 3))[n]
        outs[0][at] = source[:cut, :].astype(F32)
        outs[1][at] = source[cut:, :].astype(F32)


def work_dense(ins, outs, bit, where):
    mine, theirs = ins
    rows = mine.shape[1]
    outs[0][:, pl.ds(pl.multiple_of(where[1] * rows, LANES), rows)] = mine[...]
    outs[0][:, pl.ds(pl.multiple_of((1 - where[1]) * rows, LANES), rows)] = theirs[...].astype(F32)


def work_table(ins, outs, bit, where):
    value = total(ins[0], ins[1], 0)
    emb, half = outs[0].shape[1:]
    for f in range(outs[0].shape[0]):
        piece = value[f // 2 * emb : (f // 2 + 1) * emb]
        if f % 2:
            piece = pltpu.roll(piece, half, 1)
        outs[0][f] = piece[:, :half]


def work_add(ins, outs, bit, where):
    outs[0][...] = total(ins[0], ins[1], ...)


def work_pass(ins, outs, bit, where):
    outs[0][...] = ins[0][...]


def work_planes(ins, outs, bit, where):
    half = ins[0].shape[0]
    for n in range(2):
        outs[0][n * half : (n + 1) * half] = total(ins[n], ins[2], slice(n * half, (n + 1) * half), slice(None)).astype(BF)


def work_planes_halve(ins, outs, bit, where):
    count = outs[0].shape[0]
    for out, half in ((outs[0], bit(1)), (outs[1], 1 - bit(1))):
        for n in range(count):
            got, base = (ins[0], 0) if n < count // 2 else (ins[1], ins[0].shape[0])
            at = 2 * n + half
            out[n] = total(got, ins[2], at, at - base).astype(BF)


def work_halve(k):
    def work(ins, outs, bit, where):
        for out, half in ((outs[0], bit(k)), (outs[1], 1 - bit(k))):
            for n in range(out.shape[0]):
                out[n] = total(ins[0], ins[1], 2 * n + half).astype(out.dtype)

    return work


def work_two_ways(ins, outs, bit, where):
    half = ins[0].shape[1] // 2
    for side in range(2):
        for n in range(half):
            outs[side][n] = total(ins[0], ins[1], (side, n)).astype(BF)
    for out, which in ((outs[2], bit(1)), (outs[3], 1 - bit(1))):
        for side in range(2):
            for n in range(half // 2):
                out[side, n] = total(ins[0], ins[1], (side, half + 2 * n + which)).astype(BF)


def work_ends(ins, outs, bit, where):
    here = bit(3) * 2 + bit(2)
    for n, out in enumerate(outs):
        there = jnp.bitwise_xor(here, n)
        low = jnp.bitwise_and(there, 1)
        one, two = total(ins[0], ins[1], low), total(ins[2], ins[3], low)
        count = one.shape[0]
        out[:count, :] = jnp.where(there < 2, one, two).astype(BF)
        out[count:, :] = total(ins[4], ins[5], there).astype(BF)


def work_ends_last(ins, outs, bit, where):
    value = ins[0][...].astype(F32)
    for source in ins[1:]:
        value = value + source[...].astype(F32)
    count = outs[0].shape[0]
    outs[0][...] = value[:count]
    emb, half = outs[1].shape[1:]
    for f in range(outs[1].shape[0]):
        piece = value[count + f // 2 * emb : count + (f // 2 + 1) * emb]
        if f % 2:
            piece = pltpu.roll(piece, half, 1)
        outs[1][f] = piece[:, :half]


def chunk_of(rows, most):
    lanes = LANES
    for size in range(LANES, most + 1, LANES):
        if rows % size == 0:
            lanes = size
    return lanes


def sds(shape, dtype):
    return jax.ShapeDtypeStruct(shape, dtype)


def pinned(shape, dtype):
    return pltpu.VMEM(shape, dtype)


def run(kernel, name, outs, args, us, scalars=0, scratch=(), mib=16, alias=None, after=(), loose=False):
    vmem, smem = pl.BlockSpec(memory_space=pltpu.VMEM), pl.BlockSpec(memory_space=pltpu.SMEM)
    free = pl.BlockSpec(memory_space=pltpu.HBM if loose else pl.ANY)
    count = len(args)

    def body(*refs):
        kernel(*refs[:count], *refs[count + len(after) :])

    return pl.pallas_call(
        body,
        in_specs=[smem] * scalars + [free if loose else vmem] * (count - scalars) + [free] * len(after),
        out_specs=[vmem] * len(outs),
        out_shape=list(outs),
        scratch_shapes=list(scratch),
        input_output_aliases=alias or {},
        compiler_params=pltpu.CompilerParams(vmem_limit_bytes=mib * 1024 * 1024),
        cost_estimate=pl.CostEstimate(flops=int(us * SCALE), bytes_accessed=0, transcendentals=0),
        name=name,
    )(*args, *after)


def take_step(name, where, items, after=()):
    ins = [value for item in items for value in item[1]]
    outs = [shape for item in items for shape in item[2]]
    counts = [(len(item[1]), len(item[2])) for item in items]
    kernel = functools.partial(step_kernel, [item[0] for item in items], counts)
    got = run(kernel, name, outs, [where] + ins, ST, 1, mib=6, after=after)
    split, at = [], 0
    for _, count in counts:
        split.append(list(got[at : at + count]) if count > 1 else got[at])
        at += count
    return split


def relay(values, us, after=()):
    free = pl.BlockSpec(memory_space=pl.ANY)
    return pl.pallas_call(
        relay_kernel,
        in_specs=[free] * (len(values) + len(after)),
        out_specs=[free] * len(values),
        out_shape=[sds(value.shape, value.dtype) for value in values],
        input_output_aliases={n: n for n in range(len(values))},
        compiler_params=pltpu.CompilerParams(vmem_limit_bytes=1 << 20),
        cost_estimate=pl.CostEstimate(flops=int(us * SCALE), bytes_accessed=0, transcendentals=0),
        name="relay",
    )(*values, *after)


def add_low(a, b):
    return (a.astype(F32) + b.astype(F32)).astype(BF)


def ordered(bit, mine, theirs, axis):
    return jnp.where(
        bit == 0,
        jnp.concatenate([mine, theirs], axis=axis),
        jnp.concatenate([theirs, mine], axis=axis),
    )


def bit_of(rank, k):
    return jnp.bitwise_and(jnp.right_shift(rank, k), 1)


def per_device(
    dense, ids, table, sizes, labels, w_expert, b_expert, w_gate, b_gate, w_inner, b_inner, w_tower, b_tower, w_head, b_head
):
    n_rows = lax.axis_size("rows")
    n_bits = n_rows.bit_length() - 1
    rank, j = lax.axis_index("rows"), lax.axis_index("field")
    core = bit_of(rank, 0)
    rows_all, fields = ids.shape
    rows = rows_all // 2
    vocab, emb = table.shape[1], table.shape[2]
    dense_cols = dense.shape[1]
    width, n_expert = w_expert.shape
    experts, h1, h2 = w_inner.shape
    tasks, tower = w_head.shape
    gates = tasks * experts

    ids_t, dense_t, labels_t = ids.T, dense.T, labels.T
    table_t = jnp.transpose(table, (0, 2, 1))
    wg_own = w_gate.T
    where = jnp.stack([rank, j]).astype(jnp.int32)
    fast = n_rows * LANES == n_expert and n_rows * LANES == 2 * vocab

    def over_rows(value, bit):
        return swap(value, "rows", bit)

    def over_field(value):
        return swap(value, "field", 1)

    some = width // 16
    first, second, rows_away, weight, rate = run(
        pack_kernel,
        "pack",
        [
            sds((some + 2 * emb, n_expert), BF),
            sds((width // 4 - some, n_expert), BF),
            sds((dense_cols + 16, rows), BF),
            sds((1, rows_all), F32),
            sds((tasks, LANES), F32),
        ],
        [where, w_expert, table_t, wg_own, ids_t, dense_t, sizes, labels_t],
        2.0,
        1,
        [
            pltpu.VMEM((fields, emb, vocab // 4), F32),
            pltpu.VMEM(wg_own.shape, BF),
            pltpu.VMEM((fields, rows), jnp.int32),
            pltpu.VMEM(sizes.shape, jnp.int32),
            pltpu.VMEM(labels_t.shape, jnp.int32),
            pltpu.SemaphoreType.DMA((8,)),
        ],
        mib=60,
        loose=True,
    )
    p0, q0, rows_oth = over_field(first), over_field(second), over_field(rows_away)
    feat = pinned((width, rows), BF)
    rate_s = sds((tasks, LANES), F32)

    def click_sum(rate, k, after):
        return run(add_kernel, "click_sum", [rate_s], [rate, over_rows(rate, 1 << k)], 0.3, after=after, mib=2)[0]

    rate = click_sum(rate, 0, [])
    bias = b_expert.reshape(-1, LANES)
    feat_own, w_own, wg_here, bias = run(
        look_own_kernel,
        "look_own",
        [feat, pinned((width, n_expert), BF), pinned((gates, width), BF), pinned(bias.shape, F32)],
        [where, ids_t, dense_t, table_t, w_expert, wg_own, bias],
        0.3,
        1,
        [
            pltpu.VMEM((fields, rows), jnp.int32),
            pltpu.VMEM((fields, emb, vocab), F32),
            pltpu.SemaphoreType.DMA((6,)),
        ],
        mib=58,
        loose=True,
        after=[rate],
    )
    rate = click_sum(rate, 1, [feat_own])
    (p0,) = relay([p0], 0.1, [rate])
    (q0,) = relay([q0], 0.1, [rate])
    p1 = over_rows(p0, 2)
    p2, p3 = over_rows(p0, 1), over_rows(p1, 1)
    part, gpart = run(
        partial_kernel,
        "own_share",
        [pinned((n_expert, rows), BF), sds((gates, rows), F32)],
        [feat_own, w_own, wg_here, bias],
        0.3,
        0,
        [pltpu.VMEM((n_expert, LANES), F32)],
        mib=20,
        after=[p0],
    )
    rate = click_sum(rate, 2, [gpart])
    q1 = over_rows(q0, 2)
    q2, q3 = over_rows(q0, 1), over_rows(q1, 1)
    q2, q3 = relay([q2, q3], RQ)
    (ids_oth,) = run(unpack_kernel, "unpack", [sds((fields, rows), jnp.int32)], [rows_oth], UNP, mib=4)
    look_oth, wg_oth = run(
        look_other_kernel,
        "look_other",
        [pinned((fields * emb, rows), BF), sds((gates, width), BF)],
        [where, ids_oth, p0, p1, p2, p3],
        LO,
        1,
        [pltpu.VMEM((fields, emb, vocab), F32)],
            )

    for k in range(3, n_bits):
        rate = click_sum(rate, k, [look_oth])
    wide_rows = experts * h1 + tasks * tower
    small_rows = experts * h2 + 2 * tasks * tower + gates + 8
    mix_rows = wide_rows // 2 + 192
    blocks = n_expert // LANES // 2
    lanes = chunk_of(rows, 2304)
    mix_rows = wide_rows // 2 + 192
    blocks = n_expert // LANES // 2
    d_pre, feat_oth, d_gates, w_oth, _, mix_keep, mix_send, pred = run(
        functools.partial(middle_kernel, float(sizes.shape[1] * n_rows)),
        "middle",
        [
            pinned((n_expert, rows), BF),
            feat,
            sds((gates, rows), BF),
            sds((width, n_expert), BF),
            sds((tasks, rows), F32),
            sds((mix_rows, h2), BF),
            sds((mix_rows, h2), BF),
            sds((4 * (rows // LANES) + 8, LANES), BF),
        ],
        [
            where,
            rate,
            feat_own,
            look_oth,
            rows_oth,
            p0,
            p1,
            p2,
            p3,
            q0,
            q1,
            q2,
            q3,
            wg_oth,
            part,
            gpart,
            b_gate.reshape(1, -1),
            w_inner,
            b_inner,
            jnp.transpose(w_tower, (0, 2, 1)),
            b_tower,
            w_head,
            b_head.reshape(1, -1),
            labels_t,
            weight,
        ],
        23.0,
        1,
        [
            pltpu.VMEM((gates, LANES), F32),
            pltpu.VMEM((experts, h1, h2), BF),
            pltpu.VMEM((experts * h2, LANES), BF),
            pltpu.VMEM((tasks * tower, LANES), F32),
            pltpu.VMEM((tasks * tower, LANES), F32),
            pltpu.VMEM((tasks, LANES), F32),
            pltpu.VMEM((wide_rows, h2), BF),
            pltpu.VMEM((96, LANES), F32),
            pltpu.VMEM((small_rows, LANES), F32),
            pltpu.VMEM((n_expert, rows), BF),
            pltpu.VMEM((experts * h2, rows), BF),
            pltpu.VMEM((experts, h2, lanes), BF),
            pltpu.VMEM((experts, h2, lanes), BF),
            pltpu.VMEM((tasks * tower, h2), F32),
        ],
        mib=36,
        alias={14: 0},
    )

    held = pinned((n_expert, rows), BF)
    deep = (fields + 1) // 2 * emb
    highs = vocab // LANES
    quarter_rows = wide_rows // 4
    mix_s = sds((quarter_rows + 128, h2), BF)
    mix_long = sds((quarter_rows + 128 + pred.shape[0], h2), BF)

    def blocks_s(*shape):
        return sds(shape + (width, LANES), BF)

    def planes_s(count):
        return sds((count, deep, LANES), BF)

    def features_back(part, parts, ids_half, d_pre, w_half, wg_half, carried, dtype, name, after):
        outs = [sds((dense_cols, rows), dtype), held]
        scratch = [pltpu.VMEM((fields, highs * emb, LANES), F32)]
        if part == parts - 1:
            outs = [planes_s(highs), planes_s(highs // 2), planes_s(highs // 2)] + outs
        else:
            outs, scratch = [sds((fields, highs * emb, LANES), F32)] + outs, []
        alias = {2: len(outs) - 1}
        if part > 0:
            alias[7] = len(outs) - 2
        return run(
            functools.partial(feature_kernel, part, parts),
            name,
            outs,
            [where, ids_half, d_pre, d_gates, w_half, wg_half] + carried,
            FB / parts,
            1,
            scratch,
            alias=alias,
            after=after,
        )

    mix_got = over_rows(mix_send, 1)
    ((mix, mix_send),) = take_step("step_0", where, [(work_mix_core, [mix_got, mix_keep, pred], [mix_s, mix_long])])
    mix_got = over_field(mix_send)
    dw_keep, dw_send, d_pre = run(
        first_weight_kernel,
        "first_weights",
        [blocks_s(2, blocks), blocks_s(2, blocks), held],
        [where, d_pre, feat_own, feat_oth],
        FW,
        1,
        alias={1: 2},
        after=[mix],
    )
    predicted_s = sds((tasks, rows_all), F32)
    pred_work = (work_pred, [pred, mix_got], [predicted_s])
    (mix,) = take_step("step_1", where, [(work_mix, [mix_got, mix], [mix_s])], [dw_keep])
    if fast:
        (dw_send,) = relay([dw_send], 0.0, [mix])
        dw_got = over_rows(dw_send, 1)
    mix_got = over_rows(mix, 2)
    dt_keep, *dt_send, dd_oth, d_pre = features_back(
        0, 1, ids_oth, d_pre, w_oth, wg_oth, [], BF, "features_other", [mix]
    )
    mix_work = (work_mix, [mix_got, mix], [mix_s])
    if fast:
        dt_got = [over_rows(value, 1) for value in dt_send]
        (a_keep, a_send, b_keep, b_send), mix = take_step(
            "step_2",
            where,
            [
                (work_two_ways, [dw_got, dw_keep], [blocks_s(4), blocks_s(4), blocks_s(2, 2), blocks_s(2, 2)]),
                mix_work,
            ],
            [dt_keep],
        )
        a_got = over_field(a_send)
        b_got = over_rows(b_send, 2)
        mix_got = over_rows(mix, 4)
    else:
        (mix,) = take_step("step_2", where, [mix_work], [dt_keep])
    acc, dd_own, d_pre = features_back(0, 2, ids_t, d_pre, w_own, wg_own, [], F32, "features_own_0", [mix])
    if fast:
        dt_oth, mix = take_step(
            "step_3",
            where,
            [(work_planes, dt_got + [dt_keep], [planes_s(highs)]), (work_mix, [mix_got, mix], [mix_s])],
            [acc],
        )
        mix_got = over_rows(mix, 8)
        dt_far = over_field(dt_oth)
        after = [dt_oth]
    else:
        after = []
    do_keep, *do_send, dd_own, _ = features_back(
        1, 2, ids_t, d_pre, w_own, wg_own, [acc, dd_own], F32, "features_own_1", after
    )
    dense_s = sds((dense_cols, rows_all), F32)
    if fast:
        do_got = [over_rows(value, 1) for value in do_send]
        (a_keep, a_send), (b_keep, b_send) = take_step(
            "step_4",
            where,
            [
                (work_halve(1), [a_got, a_keep], [blocks_s(2)] * 2),
                (work_sides, [b_got, b_keep], [blocks_s(2)] * 2),
            ],
            [do_keep],
        )
        a_got = over_rows(a_send, 2)
        b_got = over_field(b_send)
        (do_keep,) = take_step("step_5", where, [(work_sum, [dt_far, do_keep], [planes_s(highs)])], [a_keep])
        (d_keep, d_send), dd_oth = take_step(
            "step_5b",
            where,
            [
                (work_planes_halve, do_got + [do_keep], [planes_s(highs // 2)] * 2),
                (work_pass, [dd_oth], [sds(dd_oth.shape, BF)]),
            ],
        )
        dd_got = over_field(dd_oth)
        d_got = over_rows(d_send, 2)
        ends_s = sds((width + deep, h2), BF)
        finals, predicted = take_step(
            "step_5c",
            where,
            [
                (
                    work_mix_last,
                    [mix_got, mix],
                    [
                        sds((quarter_rows, h2), BF),
                        sds((experts, h2), F32),
                        sds((tasks, tower), F32),
                        sds((tasks, tower), F32),
                        sds((1, gates), F32),
                        sds((1, tasks), F32),
                        sds((1, 1), F32),
                        sds((n_expert // LANES, LANES), F32),
                        sds((gates, width), F32),
                    ],
                ),
                pred_work,
            ],
            [d_keep],
        )
        (e_keep, e_low, e_high, e_both), = take_step(
            "step_6",
            where,
            [
                (work_ends, [a_got, a_keep, b_got, b_keep, d_got, d_keep], [ends_s] * 4),
            ],
            finals[:1],
        )
        e_got = [over_rows(value, bit) for value, bit in ((e_low, 4), (e_high, 8), (e_both, 12))]
        wide, d_b_inner, d_b_tower, d_w_head, d_b_gate, d_b_head, loss, d_b_expert, d_w_gate = finals
        wide_f, wide_c = over_field(wide), over_rows(wide, 1)
        wide_fc = lax.ppermute(wide, ("rows", "field"), [(i, i ^ 3) for i in range(2 * n_rows)])
        (d_w_expert, d_table), (d_w_inner, d_w_tower), d_dense = take_step(
            "step_8",
            where,
            [
                (
                    work_ends_last,
                    [e_keep] + e_got,
                    [sds((width, LANES), F32), sds((fields, emb, vocab // n_rows), F32)],
                ),
                (
                    work_wide,
                    [wide, wide_f, wide_c, wide_fc],
                    [sds((4, experts * h1 // 4, h2), F32), sds((4, tasks * tower // 4, h2), F32)],
                ),
                (work_dense, [dd_own, dd_got], [dense_s]),
            ],
        )
        d_table = jnp.transpose(d_table, (0, 2, 1))
        d_w_inner = d_w_inner.reshape(experts, h1, h2)
        d_w_tower = jnp.transpose(d_w_tower.reshape(tasks, tower, h2), (0, 2, 1))
    else:

        def by_core(keep, send, axis):
            return jnp.where(core == 0, jnp.stack([keep, send], axis), jnp.stack([send, keep], axis))

        def tables(keep, send):
            value = by_core(keep, send, 1).reshape(highs, 2, deep // emb, emb, 2, LANES // 2)
            return jnp.transpose(value, (2, 4, 3, 0, 1, 5)).reshape(deep // emb * 2, emb, vocab)[:fields]

        do_send, dt_send = jnp.concatenate(do_send), jnp.concatenate(dt_send)
        d_t = add_low(tables(do_keep, do_send), over_field(tables(dt_keep, dt_send))).astype(F32)
        d_table = jnp.transpose(lax.psum_scatter(d_t, "rows", scatter_dimension=2, tiled=True), (0, 2, 1))
        d_w = by_core(dw_keep, dw_send, 2).reshape(2, 2 * blocks, width, LANES)
        d_w = add_low(d_w[0], over_field(d_w[1])).astype(F32)
        d_w = jnp.transpose(d_w, (1, 0, 2)).reshape(width, n_expert)
        d_w_expert = lax.psum_scatter(d_w, "rows", scatter_dimension=1, tiled=True)
        sums = get_split(mix, quarter_rows, 64)
        wide = mix[:quarter_rows]
        for k in range(2, n_bits):
            wide = add_low(wide, over_rows(wide, 1 << k))
            sums = sums + over_rows(sums, 1 << k)
        wide = ordered(j, wide, over_field(wide), 0)
        wide = ordered(core, wide, over_rows(wide, 1), 0).astype(F32).reshape(4, quarter_rows, h2)
        cut = experts * h1 // 4
        d_w_inner = wide[:, :cut].reshape(experts, h1, h2)
        d_w_tower = jnp.transpose(wide[:, cut:].reshape(tasks, tower, h2), (0, 2, 1))
        d_b_inner, d_b_tower, d_w_head = sums[:8], sums[8], sums[9]
        d_b_gate, d_b_head = sums[10, :gates], sums[10, gates : gates + tasks]
        loss = jnp.sum(sums[10, gates + tasks : gates + 2 * tasks])
        d_b_expert = sums[16:32]
        d_w_gate = jnp.concatenate([sums[32:48], sums[48:64]], axis=1)
        d_dense, predicted = take_step(
            "rest", where, [(work_dense, [dd_own, over_field(dd_oth)], [dense_s]), pred_work]
        )

    return (
        predicted.T,
        loss.reshape(()),
        d_dense.T,
        d_table,
        d_w_expert,
        d_b_expert.reshape(n_expert),
        d_w_gate.T,
        d_b_gate.reshape(gates),
        d_w_inner,
        d_b_inner.reshape(experts, h2),
        d_w_tower,
        d_b_tower.reshape(tasks, tower),
        d_w_head.reshape(tasks, tower),
        d_b_head.reshape(tasks),
    )


def solution(mesh):
    return jax.shard_map(
        per_device,
        mesh=mesh,
        in_specs=(
            P("rows", "field"),
            P("rows", "field"),
            P("field", None, None),
            P("rows", None),
            P("rows", None),
            P("field", None),
            P(),
            P("field", None),
            P(),
            P(),
            P(),
            P(),
            P(),
            P(),
            P(),
        ),
        out_specs=(
            P("rows", None),
            P(),
            P("rows", "field"),
            P("field", "rows", None),
            P("field", "rows"),
            P(),
            P("field", None),
            P(),
            P(),
            P(),
            P(),
            P(),
            P(),
            P(),
        ),
        check_vma=False,
    )
```

```python
import functools

import jax
import jax.numpy as jnp
from jax import lax
from jax.experimental import pallas as pl
from jax.experimental.pallas import tpu as pltpu
from jax.sharding import PartitionSpec as P

BF = jnp.bfloat16
F32 = jnp.float32
LANES = 128
SCALE = 1.0e9
UNP = 2.0
FW, FB, ST = 0.5, 0.5, 0.3
LO = 4.0
RQ = 0.1

NN = (((1,), (0,)), ((), ()))
TN = (((0,), (0,)), ((), ()))
NT = (((1,), (1,)), ((), ()))


def dot(a, b, dims=NN):
    return lax.dot_general(a, b, dims, preferred_element_type=F32)


def swap(value, axis, bit):
    size = lax.axis_size(axis)
    return lax.ppermute(value, axis, [(i, i ^ bit) for i in range(size)])


def columns_of(row):
    return jnp.broadcast_to(row, (LANES, LANES)).T


def tile_lanes(column, lanes):
    return jnp.concatenate([column] * (lanes // LANES), axis=1)


def fold_lanes(value):
    total = value[:, :LANES]
    for start in range(LANES, value.shape[1], LANES):
        total = total + value[:, start : start + LANES]
    return total


def pack_kernel(
    where_ref,
    w_ref,
    table_ref,
    wg_ref,
    ids_ref,
    dense_ref,
    sizes_ref,
    labels_ref,
    first_ref,
    second_ref,
    rows_ref,
    weight_ref,
    rate_ref,
    table_s,
    wg_s,
    ids_s,
    sizes_s,
    labels_s,
    sems,
):
    quarter = jnp.bitwise_and(where_ref[0], 3)
    fields, emb, vocab = table_ref.shape
    lanes = table_s.shape[2]
    dense_cols, rows = dense_ref.shape[0], rows_ref.shape[1]
    some, count = w_ref.shape[0] // 4 - second_ref.shape[0], w_ref.shape[0] // 4
    away = pl.ds(pl.multiple_of((1 - where_ref[1]) * rows, LANES), rows)
    base = pl.multiple_of(quarter * count, 16)
    copies = [
        pltpu.make_async_copy(w_ref.at[pl.ds(base, some), :], first_ref.at[:some, :], sems.at[0]),
        pltpu.make_async_copy(w_ref.at[pl.ds(base + some, count - some), :], second_ref, sems.at[1]),
        pltpu.make_async_copy(
            table_ref.at[:, :, pl.ds(pl.multiple_of(quarter * lanes, LANES), lanes)], table_s, sems.at[2]
        ),
        pltpu.make_async_copy(wg_ref, wg_s, sems.at[3]),
        pltpu.make_async_copy(ids_ref.at[:, away], ids_s, sems.at[4]),
        pltpu.make_async_copy(dense_ref.at[:, away], rows_ref.at[:dense_cols, :], sems.at[5]),
        pltpu.make_async_copy(sizes_ref, sizes_s, sems.at[6]),
        pltpu.make_async_copy(labels_ref, labels_s, sems.at[7]),
    ]
    for copy in copies:
        copy.start()
    for copy in copies:
        copy.wait()
    sizes_ref, labels_ref = sizes_s, labels_s
    for f in range(fields):
        at = some + f % 2 * emb
        first_ref[at : at + emb, f // 2 * lanes : (f // 2 + 1) * lanes] = table_s[f].astype(BF)
    at = some + fields % 2 * emb
    first_ref[at : at + emb, fields // 2 * lanes : (fields // 2 + 1) * lanes] = wg_s[...]
    first_ref[some:, (fields // 2 + 1) * lanes :] = jnp.zeros_like(first_ref[some:, (fields // 2 + 1) * lanes :])
    ids = ids_s[...]
    value = (jnp.bitwise_and(ids, 127) + 128).astype(F32)
    for k in range(3):
        up = float(1 << (1 << k))
        value = value * jnp.where(jnp.bitwise_and(jnp.right_shift(ids, 7 + k), 1) == 1, up, 1.0)
    rows_ref[dense_cols : dense_cols + fields, :] = value.astype(BF)
    rows_ref[dense_cols + fields :, :] = jnp.zeros_like(rows_ref[dense_cols + fields :, :])
    groups, rows = sizes_ref.shape[1], labels_ref.shape[1]
    sizes = jnp.broadcast_to(sizes_ref[...].astype(F32), (groups, groups))
    below = lax.broadcasted_iota(jnp.int32, (groups, groups), 0)
    across = lax.broadcasted_iota(jnp.int32, (groups, groups), 1)
    starts = jnp.sum(jnp.where(across < below, sizes, 0.0), axis=1, keepdims=True)
    own = jnp.sum(jnp.where(across == below, sizes, 0.0), axis=1, keepdims=True)
    ends = starts + own
    share = 1.0 / own
    rate = jnp.zeros((2, LANES), F32)
    for at in range(0, rows, 256):
        place = (lax.broadcasted_iota(jnp.int32, (groups, 256), 1) + at).astype(F32)
        inside = (place >= starts) & (place < ends)
        weight = jnp.sum(jnp.where(inside, share, 0.0), axis=0, keepdims=True)
        weight_ref[:, at : at + 256] = weight
        rate = rate + fold_lanes(weight * labels_ref[:, at : at + 256].astype(F32))
    rate_ref[...] = jnp.broadcast_to(jnp.sum(rate, axis=1, keepdims=True), rate_ref.shape)


def fold_low(value):
    total = None
    for start in range(0, value.shape[1], 2 * LANES):
        part = value[:, start : start + LANES] + value[:, start + LANES : start + 2 * LANES]
        total = part.astype(F32) if total is None else total + part.astype(F32)
    return total


def look_up(ids_ref, first, table_ref, feat_ref, rows, dense_ref=None):
    fields, emb, vocab = table_ref.shape
    lanes = 256

    def block(i, carry):
        source = pl.ds(pl.multiple_of(first + i * lanes, lanes), lanes)
        target = pl.multiple_of(i * lanes, lanes)
        every = ids_ref[:, source]
        for f in range(fields):
            for at in range(0, lanes, LANES):
                ids = every[f : f + 1, at : at + LANES]
                low = jnp.broadcast_to(jnp.bitwise_and(ids, LANES - 1), (emb, LANES))
                high = jnp.broadcast_to(jnp.right_shift(ids, 7), (emb, LANES))
                found = None
                for h in range(vocab // LANES):
                    piece = table_ref[f, :, h * LANES : (h + 1) * LANES]
                    piece = jnp.take_along_axis(piece, low, axis=1, mode="promise_in_bounds")
                    found = piece if found is None else jnp.where(high == h, piece, found)
                feat_ref[f * emb : (f + 1) * emb, pl.ds(target + at, LANES)] = found.astype(BF)
        if dense_ref is not None:
            feat_ref[fields * emb :, pl.ds(target, lanes)] = dense_ref[:, source]
        return carry

    lax.fori_loop(0, rows // lanes, block, 0)


def look_own_kernel(
    where_ref, ids_ref, dense_ref, table_ref, w_in, wg_in, bias_in, feat_ref, w_ref, wg_ref, bias_ref, ids_s, table_s, sems
):
    rows = feat_ref.shape[1]
    fields, emb, _ = table_ref.shape
    mine = pl.ds(pl.multiple_of(where_ref[1] * rows, LANES), rows)
    copies = [
        pltpu.make_async_copy(ids_ref.at[:, mine], ids_s, sems.at[0]),
        pltpu.make_async_copy(table_ref, table_s, sems.at[1]),
        pltpu.make_async_copy(dense_ref.at[:, mine], feat_ref.at[fields * emb :, :], sems.at[2]),
        pltpu.make_async_copy(bias_in, bias_ref, sems.at[3]),
        pltpu.make_async_copy(wg_in, wg_ref, sems.at[4]),
        pltpu.make_async_copy(w_in, w_ref, sems.at[5]),
    ]
    for copy in copies:
        copy.start()
    for copy in copies[:2]:
        copy.wait()
    look_up(ids_s, 0, table_s, feat_ref, rows)
    for copy in copies[2:]:
        copy.wait()


def unpack_kernel(rows_ref, ids_ref):
    fields = ids_ref.shape[0]
    dense_cols = rows_ref.shape[0] - 16
    value = rows_ref[dense_cols : dense_cols + fields, :].astype(F32)
    high = jnp.zeros(value.shape, jnp.int32)
    for k in range(2, -1, -1):
        up = float(1 << (1 << k))
        over = value >= 128.0 * up
        value = jnp.where(over, value * (1.0 / up), value)
        high = high + jnp.where(over, 1 << k, 0)
    ids_ref[...] = high * 128 + (value.astype(jnp.int32) - 128)


def look_other_kernel(where_ref, ids_ref, p0_ref, p1_ref, p2_ref, p3_ref, feat_ref, wg_ref, table_s):
    fields, emb, vocab = table_s.shape
    lanes, some = vocab // 4, p0_ref.shape[0] - 2 * emb
    quarter = jnp.bitwise_and(where_ref[0], 3)
    for flip, source in ((0, p0_ref), (2, p1_ref), (1, p2_ref), (3, p3_ref)):
        at = pl.multiple_of(jnp.bitwise_xor(quarter, flip) * lanes, LANES)
        for f in range(fields):
            top = some + f % 2 * emb
            piece = source[top : top + emb, f // 2 * lanes : (f // 2 + 1) * lanes]
            table_s[f, :, pl.ds(at, lanes)] = piece.astype(F32)
    top = some + fields % 2 * emb
    wg_ref[...] = p0_ref[top : top + emb, fields // 2 * lanes : (fields // 2 + 1) * lanes]
    look_up(ids_ref, 0, table_s, feat_ref, feat_ref.shape[1])


def partial_kernel(feat_ref, w_ref, wg_ref, bias_ref, part_ref, gpart_ref, bias_s):
    rows = feat_ref.shape[1]
    for n in range(bias_ref.shape[0]):
        bias_s[n * LANES : (n + 1) * LANES, :] = 0.5 * columns_of(bias_ref[n : n + 1, :])
    lanes = chunk_of(rows, 768)

    def block(i, carry):
        cols = pl.ds(pl.multiple_of(i * lanes, lanes), lanes)
        half = feat_ref[:, cols] * jnp.asarray(0.5, BF)
        for at in range(0, w_ref.shape[1], 256):
            acc = dot(w_ref[:, at : at + 256], half, TN)
            part_ref[at : at + 256, cols] = (acc + tile_lanes(bias_s[at : at + 256, :], lanes)).astype(BF)
        gpart_ref[:, cols] = dot(wg_ref[...], half)
        return carry

    lax.fori_loop(0, rows // lanes, block, 0)


def relay_kernel(*refs):
    pass


def add_kernel(a_ref, b_ref, out_ref):
    out_ref[...] = a_ref[...] + b_ref[...]


def middle_kernel(
    groups_total,
    where_ref,
    rate_ref,
    own_ref,
    look_ref,
    rows_ref,
    p0_ref,
    p1_ref,
    p2_ref,
    p3_ref,
    q0_ref,
    q1_ref,
    q2_ref,
    q3_ref,
    wg_ref,
    part_ref,
    gpart_ref,
    bg_raw,
    wi_raw,
    bi_raw,
    wt_ref,
    bt_raw,
    wh_raw,
    bh_raw,
    labels_ref,
    weight_ref,
    slope_ref,
    feat_ref,
    dg_ref,
    w_ref,
    pred_ref,
    mix_keep_ref,
    mix_send_ref,
    pred_out_ref,
    bg_ref,
    wi_ref,
    bi_ref,
    bt_ref,
    wh_ref,
    bh_ref,
    wide_ref,
    sums_s,
    small_ref,
    hidden_ref,
    ds_ref,
    out_s,
    slope_s,
    dwt_s,
):
    rows = feat_ref.shape[1]
    lanes = out_s.shape[2]
    experts, h1, h2 = wi_raw.shape
    tasks, tower = wt_ref.shape[0], wt_ref.shape[1]
    one = jnp.asarray(1.0, BF)
    wi_ref[...] = wi_raw[...] * jnp.asarray(0.5, BF)
    for n in range(bi_raw.shape[0]):
        bi_ref[n * LANES : (n + 1) * LANES, :] = (0.5 * columns_of(bi_raw[n : n + 1, :])).astype(BF)
    bt_ref[...] = columns_of(jnp.concatenate([bt_raw[t : t + 1, :] for t in range(tasks)], axis=1))
    wh_ref[...] = columns_of(jnp.concatenate([wh_raw[...][t : t + 1, :].astype(F32) for t in range(tasks)], axis=1))
    bg_ref[...] = small_column(bg_raw)
    bh_ref[...] = small_column(bh_raw)
    small_ref[...] = jnp.zeros_like(small_ref)
    dwt_s[...] = jnp.zeros_like(dwt_s)
    feat_ref[: look_ref.shape[0], :] = look_ref[...]
    feat_ref[look_ref.shape[0] :, :] = rows_ref[: feat_ref.shape[0] - look_ref.shape[0], :]
    quarter = jnp.bitwise_and(where_ref[0], 3)
    count = w_ref.shape[0] // 4
    some = count - q0_ref.shape[0]
    for flip, upper, lower in ((0, p0_ref, q0_ref), (2, p1_ref, q1_ref), (1, p2_ref, q2_ref), (3, p3_ref, q3_ref)):
        at = pl.multiple_of(jnp.bitwise_xor(quarter, flip) * count, 16)
        w_ref[pl.ds(at, some), :] = upper[:some, :]
        w_ref[pl.ds(at + some, count - some), :] = lower[...]
    rate = rate_ref[...]
    click = (rate + 1.0) / (groups_total + 2.0)
    entropy = -(click * jnp.log(click) + (1.0 - click) * jnp.log(1.0 - click))
    scale = tile_lanes(1.0 / (groups_total * entropy), lanes)

    def block(i, carry):
        cols = pl.ds(pl.multiple_of(i * lanes, lanes), lanes)
        source = pl.ds(pl.multiple_of(where_ref[1] * rows + i * lanes, LANES), lanes)
        half = feat_ref[:, cols] * jnp.asarray(0.5, BF)
        gate_logits = 2.0 * (gpart_ref[:, cols] + dot(wg_ref[...], half)) + tile_lanes(bg_ref[...], lanes)
        gates = []
        for t in range(tasks):
            logits = gate_logits[t * experts : (t + 1) * experts]
            top = jnp.exp(logits - jnp.max(logits, axis=0, keepdims=True))
            gates.append(top / jnp.sum(top, axis=0, keepdims=True))
        mixed = [jnp.zeros((h2, lanes), BF) for _ in range(tasks)]
        for e in range(experts):
            at = e * h1
            u = dot(w_ref[:, at : at + h1], half, TN).astype(BF) + part_ref[at : at + h1, cols]
            t1 = jnp.tanh(u)
            hidden = u + u * t1
            hidden_ref[at : at + h1, cols] = hidden
            slope_ref[at : at + h1, cols] = (one + hidden) + t1 * (one - hidden)
            u2 = dot(wi_ref[e], hidden, TN).astype(BF) + tile_lanes(bi_ref[e * h2 : (e + 1) * h2, :], lanes)
            t2 = jnp.tanh(u2)
            out = u2 + u2 * t2
            out_s[e] = out
            slope_s[e] = (one + out) + t2 * (one - out)
            for t in range(tasks):
                mixed[t] = mixed[t] + gates[t][e : e + 1, :].astype(BF) * out
        labels = labels_ref[:, source].astype(F32)
        weight = weight_ref[:, source]
        preds, d_logits, losses, d_mixed = [], [], [], []
        for t in range(tasks):
            mine = slice(t * tower, (t + 1) * tower)
            low = mixed[t]
            tower_pre = dot(wt_ref[t], low) + tile_lanes(bt_ref[mine, :], lanes)
            sigma = 0.5 + 0.5 * jnp.tanh(0.5 * tower_pre)
            tower_out = (tower_pre * sigma).astype(BF).astype(F32)
            head = tile_lanes(wh_ref[mine, :], lanes)
            logit = jnp.sum(tower_out * head, axis=0, keepdims=True) + tile_lanes(bh_ref[t : t + 1, :], lanes)
            label = labels[t : t + 1]
            pred = jax.nn.sigmoid(logit)
            share = weight * scale[t : t + 1]
            plus = jnp.maximum(logit, 0.0) + jnp.log1p(jnp.exp(-jnp.abs(logit)))
            losses.append(share * (plus - label * logit))
            d_logit = share * (pred - label)
            preds.append(pred)
            d_logits.append(d_logit)
            d_tower = d_logit * head * (sigma * (1.0 + tower_pre * (1.0 - sigma)))
            d_low = d_tower.astype(BF)
            base = experts * h2
            small_ref[base + t * tower : base + (t + 1) * tower, :] += fold_lanes(d_tower)
            base = base + tasks * tower
            small_ref[base + t * tower : base + (t + 1) * tower, :] += fold_lanes(d_logit * tower_out)
            dwt_s[mine, :] += dot(d_low, low, NT)
            d_mixed.append(dot(wt_ref[t], d_low, TN))
        pred_ref[:, cols] = jnp.concatenate(preds, axis=0)
        base = experts * h2 + 2 * tasks * tower + tasks * experts
        small_ref[base : base + 8, :] += fold_lanes(
            jnp.concatenate(d_logits + losses + [jnp.zeros((8 - 2 * tasks, lanes), F32)], axis=0)
        )
        halves = [(0.5 * gate).astype(BF) for gate in gates]
        d_lows = [value.astype(BF) for value in d_mixed]
        d_gates = [[] for _ in range(tasks)]
        for e in range(experts):
            out = out_s[e]
            d_out = None
            for t in range(tasks):
                product = d_lows[t] * out
                product = (product[: h2 // 2] + product[h2 // 2 :]).astype(F32)
                d_gates[t].append(jnp.sum(product, axis=0, keepdims=True))
                term = halves[t][e : e + 1, :] * d_lows[t]
                d_out = term if d_out is None else d_out + term
            d_second = d_out * slope_s[e]
            small_ref[e * h2 : (e + 1) * h2, :] += fold_low(d_second)
            ds_ref[e * h2 : (e + 1) * h2, cols] = d_second
        d_all = []
        for t in range(tasks):
            d_gate = jnp.concatenate(d_gates[t], axis=0)
            d_all.append(gates[t] * (d_gate - jnp.sum(gates[t] * d_gate, axis=0, keepdims=True)))
        d_all = jnp.concatenate(d_all, axis=0)
        base = experts * h2 + 2 * tasks * tower
        small_ref[base : base + tasks * experts, :] += fold_lanes(d_all)
        dg_ref[:, cols] = d_all.astype(BF)
        return carry

    lax.fori_loop(0, rows // lanes, block, 0)

    part, tail = experts * h1 // 4, tasks * tower // 4
    for e in range(experts):
        d_wi = dot(hidden_ref[e * h1 : (e + 1) * h1, :], ds_ref[e * h2 : (e + 1) * h2, :], NT).astype(BF)
        at = e * h1
        base = at // part * (part + tail) + at % part
        wide_ref[base : base + h1, :] = d_wi
    for q in range(4):
        base = q * (part + tail) + part
        wide_ref[base : base + tail, :] = dwt_s[q * tail : (q + 1) * tail, :].astype(BF)
    core = jnp.bitwise_and(where_ref[0], 1)
    count = 2 * (part + tail)
    mix_keep_ref[:count, :] = wide_ref[pl.ds(pl.multiple_of(core * count, 32), count), :]
    mix_send_ref[:count, :] = wide_ref[pl.ds(pl.multiple_of((1 - core) * count, 32), count), :]

    sums_s[...] = jnp.zeros_like(sums_s)
    whole = experts * h2 // LANES + 2 * tasks * tower // LANES
    for g in range(whole):
        sums_s[g : g + 1, :] = jnp.sum(small_ref[g * LANES : (g + 1) * LANES, :].T, axis=0, keepdims=True)
    left = small_ref.shape[0] - whole * LANES
    sums_s[whole : whole + 1, :left] = jnp.sum(small_ref[whole * LANES :, :].T, axis=0, keepdims=True)
    step = chunk_of(rows, 768)
    for e in range(experts):
        r1, r2 = slice(e * h1, (e + 1) * h1), slice(e * h2, (e + 1) * h2)
        bias = jnp.zeros((h1, LANES), F32)
        for at in range(0, rows, step):
            cols = slice(at, at + step)
            d_pre = dot(wi_ref[e], ds_ref[r2, cols]).astype(BF) * slope_ref[r1, cols]
            bias = bias + fold_low(d_pre)
            slope_ref[r1, cols] = d_pre
        row = jnp.sum(bias.T, axis=0, keepdims=True)
        for m in range(h1 // LANES):
            at = 16 + e * (h1 // LANES) + m
            sums_s[at : at + 1, :] = row[:, m * LANES : (m + 1) * LANES]
    for side, source in enumerate((own_ref, feat_ref)):
        d_wg = dot(dg_ref[...], source[...], NT)
        for m in range(d_wg.shape[1] // LANES):
            at = 32 + (2 * side + m) * 16
            sums_s[at : at + 16, :] = d_wg[:, m * LANES : (m + 1) * LANES]
    put_split(mix_keep_ref, count, sums_s[...])
    put_split(mix_send_ref, count, sums_s[...])
    pred = pred_ref[...]
    for m in range(rows // LANES):
        piece = pred[:, m * LANES : (m + 1) * LANES]
        high = piece.astype(BF)
        low = (piece - high.astype(F32)).astype(BF)
        split = jnp.concatenate([high.astype(F32), low.astype(F32)], axis=0)
        pred_out_ref[4 * m : 4 * m + 4, :] = split.astype(BF)
    pred_out_ref[4 * (rows // LANES) :, :] = jnp.zeros_like(pred_out_ref[4 * (rows // LANES) :, :])


def small_column(raw):
    count = raw.shape[1]
    same = lax.broadcasted_iota(jnp.int32, (count, count), 0) == lax.broadcasted_iota(jnp.int32, (count, count), 1)
    column = jnp.sum(jnp.where(same, jnp.broadcast_to(raw[...], (count, count)), 0.0), axis=1, keepdims=True)
    return jnp.broadcast_to(column, (count, LANES))


def put_split(target, at, value):
    count = value.shape[0]
    high = value.astype(BF)
    target[at : at + count, :] = high
    target[at + count : at + 2 * count, :] = (value - high.astype(F32)).astype(BF)


def get_split(source, at, count):
    return source[at : at + count, :].astype(F32) + source[at + count : at + 2 * count, :].astype(F32)


def weight_gradients(where_ref, dpre_ref, first, own_ref, oth_ref, keep_ref, send_ref):
    even = jnp.bitwise_and(where_ref[0], 1) == 0
    for n in range(keep_ref.shape[1]):
        at = first + n * 2 * LANES
        for side, source in enumerate((own_ref, oth_ref)):
            d_w = dot(source[...], dpre_ref[at : at + 2 * LANES, :], NT)
            one, two = d_w[:, :LANES], d_w[:, LANES:]
            keep_ref[side, n] = jnp.where(even, one, two).astype(BF)
            send_ref[side, n] = jnp.where(even, two, one).astype(BF)


def first_weight_kernel(where_ref, dpre_ref, own_ref, oth_ref, keep_ref, send_ref, _):
    weight_gradients(where_ref, dpre_ref, 0, own_ref, oth_ref, keep_ref, send_ref)


def feature_kernel(part, parts, where_ref, ids_ref, dpre_ref, dg_ref, w_ref, wg_ref, *refs):
    fields, emb = ids_ref.shape[0], 16
    rows = dg_ref.shape[1]
    lanes = chunk_of(rows, 2304 if parts == 1 else 1152)
    carried = refs[0] if part > 0 else None
    first = where_ref[1] * rows if ids_ref.shape[1] > rows else 0
    if part > 0:
        refs = refs[2:]
    if part == parts - 1:
        keep_ref, send_ref, send2_ref, ddense_ref, _, acc_s = refs
    else:
        acc_s, ddense_ref, _ = refs
    highs = acc_s.shape[1] // emb
    acc_s[...] = jnp.zeros_like(acc_s) if carried is None else carried[...]

    def block(i, carry):
        cols = pl.ds(pl.multiple_of(i * lanes, lanes), lanes)
        source = pl.ds(pl.multiple_of(first + i * lanes, LANES), lanes)
        d_feat = dot(w_ref[...], dpre_ref[:, cols]) + dot(wg_ref[...], dg_ref[:, cols], TN)
        ddense_ref[:, cols] = d_feat[fields * emb :, :].astype(ddense_ref.dtype)
        every = ids_ref[:, source]
        low = jnp.bitwise_and(every, LANES - 1)
        every = jnp.right_shift(every, 7)
        places = lax.broadcasted_iota(jnp.int32, (LANES, lanes), 0)
        for f in range(fields):
            hot = jnp.where(places == low[f : f + 1, :], 1.0, 0.0).astype(BF)
            high = jnp.broadcast_to(every[f : f + 1, :], (emb, lanes))
            grad = d_feat[f * emb : (f + 1) * emb, :]
            spread = jnp.concatenate([jnp.where(high == h, grad, 0.0) for h in range(highs)], axis=0)
            acc_s[f] += dot(spread.astype(BF), hot, NT)
        return carry

    steps = rows // lanes
    lax.fori_loop(steps * part // parts, steps * (part + 1) // parts, block, 0)
    if part < parts - 1:
        return
    even = jnp.bitwise_and(where_ref[0], 1) == 0
    left = lax.broadcasted_iota(jnp.int32, (emb, LANES), 1) < LANES // 2
    for p in range((fields + 1) // 2):
        rows_p = slice(p * emb, (p + 1) * emb)
        for h in range(highs):
            a = acc_s[2 * p, h * emb : (h + 1) * emb, :]
            b = acc_s[2 * p + 1, h * emb : (h + 1) * emb, :] if 2 * p + 1 < fields else jnp.zeros_like(a)
            first = jnp.where(left, a, pltpu.roll(b, LANES // 2, 1))
            second = jnp.where(left, pltpu.roll(a, LANES // 2, 1), b)
            keep_ref[h, rows_p, :] = jnp.where(even, first, second).astype(BF)
            out_ref, place = (send_ref, h) if h < highs // 2 else (send2_ref, h - highs // 2)
            out_ref[place, rows_p, :] = jnp.where(even, second, first).astype(BF)


def step_kernel(works, counts, where_ref, *refs):
    def bit(k):
        return jnp.bitwise_and(jnp.right_shift(where_ref[0], k), 1)

    ins = sum(n for n, _ in counts)
    a, b = 0, ins
    for work, (n_in, n_out) in zip(works, counts):
        work(refs[a : a + n_in], refs[b : b + n_out], bit, where_ref)
        a, b = a + n_in, b + n_out


def total(a, b, at, at_a=None):
    return a[at if at_a is None else at_a].astype(F32) + b[at].astype(F32)


def work_sum(ins, outs, bit, where):
    outs[0][...] = total(ins[0], ins[1], ...).astype(outs[0].dtype)


def work_sides(ins, outs, bit, where):
    for side in range(2):
        outs[side][...] = total(ins[0], ins[1], side).astype(outs[side].dtype)


def work_mix_core(ins, outs, bit, where):
    got, mine, pred = ins
    keep, send = outs
    count = keep.shape[0] - 128
    send[count + 128 :, :] = pred[...]
    sums = get_split(got, 2 * count, 96) + get_split(mine, 2 * count, 96)
    for out, half in ((keep, where[1]), (send, 1 - where[1])):
        out[:count, :] = total(got, mine, pl.ds(pl.multiple_of(half * count, 32), count)).astype(BF)
    put_split(keep, count, jnp.concatenate([sums[:32], sums[32:64]], axis=0))
    put_split(send, count, jnp.concatenate([sums[:32], sums[64:96]], axis=0))


def work_pred(ins, outs, bit, where):
    rows = outs[0].shape[1] // 2
    for side, source in ((where[1], ins[0]), (1 - where[1], ins[1])):
        base = source.shape[0] - ins[0].shape[0]
        for m in range(rows // LANES):
            at = base + 4 * m
            value = source[at : at + 2, :].astype(F32) + source[at + 2 : at + 4, :].astype(F32)
            outs[0][:, pl.ds(pl.multiple_of(side * rows + m * LANES, LANES), LANES)] = value


def work_mix(ins, outs, bit, where):
    count = outs[0].shape[0] - 128
    outs[0][:count, :] = total(ins[0], ins[1], slice(0, count)).astype(BF)
    put_split(outs[0], count, get_split(ins[0], count, 64) + get_split(ins[1], count, 64))


def work_mix_last(ins, outs, bit, where):
    quarter, inner, tower, head, gate, ends, loss, first, weights = outs
    count = ins[0].shape[0] - 128
    quarter[...] = total(ins[0], ins[1], slice(0, count)).astype(BF)
    sums = get_split(ins[0], count, 64) + get_split(ins[1], count, 64)
    inner[...] = sums[:8]
    half = tower.shape[1]
    for n in range(2):
        tower[n : n + 1, :] = sums[8:9, n * half : (n + 1) * half]
        head[n : n + 1, :] = sums[9:10, n * half : (n + 1) * half]
    gates = gate.shape[1]
    gate[...] = sums[10:11, :gates]
    ends[...] = sums[10:11, gates : gates + 2]
    loss[...] = sums[10:11, gates + 2 : gates + 3] + sums[10:11, gates + 3 : gates + 4]
    first[...] = sums[16:32]
    weights[:, :LANES] = sums[32:48]
    weights[:, LANES:] = sums[48:64]


def work_wide(ins, outs, bit, where):
    here = bit(0) * 2 + where[1]
    cut = outs[0].shape[1]
    for n, source in enumerate(ins):
        at = (here, jnp.bitwise_xor(here, 1), jnp.bitwise_xor(here, 2), jnp.bitwise_xor(here, 3))[n]
        outs[0][at] = source[:cut, :].astype(F32)
        outs[1][at] = source[cut:, :].astype(F32)


def work_dense(ins, outs, bit, where):
    mine, theirs = ins
    rows = mine.shape[1]
    outs[0][:, pl.ds(pl.multiple_of(where[1] * rows, LANES), rows)] = mine[...]
    outs[0][:, pl.ds(pl.multiple_of((1 - where[1]) * rows, LANES), rows)] = theirs[...].astype(F32)


def work_table(ins, outs, bit, where):
    value = total(ins[0], ins[1], 0)
    emb, half = outs[0].shape[1:]
    for f in range(outs[0].shape[0]):
        piece = value[f // 2 * emb : (f // 2 + 1) * emb]
        if f % 2:
            piece = pltpu.roll(piece, half, 1)
        outs[0][f] = piece[:, :half]


def work_add(ins, outs, bit, where):
    outs[0][...] = total(ins[0], ins[1], ...)


def work_pass(ins, outs, bit, where):
    outs[0][...] = ins[0][...]


def work_planes(ins, outs, bit, where):
    half = ins[0].shape[0]
    for n in range(2):
        outs[0][n * half : (n + 1) * half] = total(ins[n], ins[2], slice(n * half, (n + 1) * half), slice(None)).astype(BF)


def work_planes_halve(ins, outs, bit, where):
    count = outs[0].shape[0]
    for out, half in ((outs[0], bit(1)), (outs[1], 1 - bit(1))):
        for n in range(count):
            got, base = (ins[0], 0) if n < count // 2 else (ins[1], ins[0].shape[0])
            at = 2 * n + half
            out[n] = total(got, ins[2], at, at - base).astype(BF)


def work_halve(k):
    def work(ins, outs, bit, where):
        for out, half in ((outs[0], bit(k)), (outs[1], 1 - bit(k))):
            for n in range(out.shape[0]):
                out[n] = total(ins[0], ins[1], 2 * n + half).astype(out.dtype)

    return work


def work_two_ways(ins, outs, bit, where):
    half = ins[0].shape[1] // 2
    for side in range(2):
        for n in range(half):
            outs[side][n] = total(ins[0], ins[1], (side, n)).astype(BF)
    for out, which in ((outs[2], bit(1)), (outs[3], 1 - bit(1))):
        for side in range(2):
            for n in range(half // 2):
                out[side, n] = total(ins[0], ins[1], (side, half + 2 * n + which)).astype(BF)


def work_ends(ins, outs, bit, where):
    here = bit(3) * 2 + bit(2)
    for n, out in enumerate(outs):
        there = jnp.bitwise_xor(here, n)
        low = jnp.bitwise_and(there, 1)
        one, two = total(ins[0], ins[1], low), total(ins[2], ins[3], low)
        count = one.shape[0]
        out[:count, :] = jnp.where(there < 2, one, two).astype(BF)
        out[count:, :] = total(ins[4], ins[5], there).astype(BF)


def work_ends_last(ins, outs, bit, where):
    value = ins[0][...].astype(F32)
    for source in ins[1:]:
        value = value + source[...].astype(F32)
    count = outs[0].shape[0]
    outs[0][...] = value[:count]
    emb, half = outs[1].shape[1:]
    for f in range(outs[1].shape[0]):
        piece = value[count + f // 2 * emb : count + (f // 2 + 1) * emb]
        if f % 2:
            piece = pltpu.roll(piece, half, 1)
        outs[1][f] = piece[:, :half]


def chunk_of(rows, most):
    lanes = LANES
    for size in range(LANES, most + 1, LANES):
        if rows % size == 0:
            lanes = size
    return lanes


def sds(shape, dtype):
    return jax.ShapeDtypeStruct(shape, dtype)


def pinned(shape, dtype):
    return pltpu.VMEM(shape, dtype)


def run(kernel, name, outs, args, us, scalars=0, scratch=(), mib=16, alias=None, after=(), loose=False):
    vmem, smem = pl.BlockSpec(memory_space=pltpu.VMEM), pl.BlockSpec(memory_space=pltpu.SMEM)
    free = pl.BlockSpec(memory_space=pltpu.HBM if loose else pl.ANY)
    count = len(args)

    def body(*refs):
        kernel(*refs[:count], *refs[count + len(after) :])

    return pl.pallas_call(
        body,
        in_specs=[smem] * scalars + [free if loose else vmem] * (count - scalars) + [free] * len(after),
        out_specs=[vmem] * len(outs),
        out_shape=list(outs),
        scratch_shapes=list(scratch),
        input_output_aliases=alias or {},
        compiler_params=pltpu.CompilerParams(vmem_limit_bytes=mib * 1024 * 1024),
        cost_estimate=pl.CostEstimate(flops=int(us * SCALE), bytes_accessed=0, transcendentals=0),
        name=name,
    )(*args, *after)


def take_step(name, where, items, after=()):
    ins = [value for item in items for value in item[1]]
    outs = [shape for item in items for shape in item[2]]
    counts = [(len(item[1]), len(item[2])) for item in items]
    kernel = functools.partial(step_kernel, [item[0] for item in items], counts)
    got = run(kernel, name, outs, [where] + ins, ST, 1, mib=6, after=after)
    split, at = [], 0
    for _, count in counts:
        split.append(list(got[at : at + count]) if count > 1 else got[at])
        at += count
    return split


def relay(values, us, after=()):
    free = pl.BlockSpec(memory_space=pl.ANY)
    return pl.pallas_call(
        relay_kernel,
        in_specs=[free] * (len(values) + len(after)),
        out_specs=[free] * len(values),
        out_shape=[sds(value.shape, value.dtype) for value in values],
        input_output_aliases={n: n for n in range(len(values))},
        compiler_params=pltpu.CompilerParams(vmem_limit_bytes=1 << 20),
        cost_estimate=pl.CostEstimate(flops=int(us * SCALE), bytes_accessed=0, transcendentals=0),
        name="relay",
    )(*values, *after)


def add_low(a, b):
    return (a.astype(F32) + b.astype(F32)).astype(BF)


def ordered(bit, mine, theirs, axis):
    return jnp.where(
        bit == 0,
        jnp.concatenate([mine, theirs], axis=axis),
        jnp.concatenate([theirs, mine], axis=axis),
    )


def bit_of(rank, k):
    return jnp.bitwise_and(jnp.right_shift(rank, k), 1)


def per_device(
    dense, ids, table, sizes, labels, w_expert, b_expert, w_gate, b_gate, w_inner, b_inner, w_tower, b_tower, w_head, b_head
):
    n_rows = lax.axis_size("rows")
    n_bits = n_rows.bit_length() - 1
    rank, j = lax.axis_index("rows"), lax.axis_index("field")
    core = bit_of(rank, 0)
    rows_all, fields = ids.shape
    rows = rows_all // 2
    vocab, emb = table.shape[1], table.shape[2]
    dense_cols = dense.shape[1]
    width, n_expert = w_expert.shape
    experts, h1, h2 = w_inner.shape
    tasks, tower = w_head.shape
    gates = tasks * experts

    ids_t, dense_t, labels_t = ids.T, dense.T, labels.T
    table_t = jnp.transpose(table, (0, 2, 1))
    wg_own = w_gate.T
    where = jnp.stack([rank, j]).astype(jnp.int32)
    fast = n_rows * LANES == n_expert and n_rows * LANES == 2 * vocab

    def over_rows(value, bit):
        return swap(value, "rows", bit)

    def over_field(value):
        return swap(value, "field", 1)

    some = width // 16
    first, second, rows_away, weight, rate = run(
        pack_kernel,
        "pack",
        [
            sds((some + 2 * emb, n_expert), BF),
            sds((width // 4 - some, n_expert), BF),
            sds((dense_cols + 16, rows), BF),
            sds((1, rows_all), F32),
            sds((tasks, LANES), F32),
        ],
        [where, w_expert, table_t, wg_own, ids_t, dense_t, sizes, labels_t],
        2.0,
        1,
        [
            pltpu.VMEM((fields, emb, vocab // 4), F32),
            pltpu.VMEM(wg_own.shape, BF),
            pltpu.VMEM((fields, rows), jnp.int32),
            pltpu.VMEM(sizes.shape, jnp.int32),
            pltpu.VMEM(labels_t.shape, jnp.int32),
            pltpu.SemaphoreType.DMA((8,)),
        ],
        mib=60,
        loose=True,
    )
    p0, q0, rows_oth = over_field(first), over_field(second), over_field(rows_away)
    feat = pinned((width, rows), BF)
    rate_s = sds((tasks, LANES), F32)

    def click_sum(rate, k, after):
        return run(add_kernel, "click_sum", [rate_s], [rate, over_rows(rate, 1 << k)], 0.3, after=after, mib=2)[0]

    rate = click_sum(rate, 0, [])
    bias = b_expert.reshape(-1, LANES)
    feat_own, w_own, wg_here, bias = run(
        look_own_kernel,
        "look_own",
        [feat, pinned((width, n_expert), BF), pinned((gates, width), BF), pinned(bias.shape, F32)],
        [where, ids_t, dense_t, table_t, w_expert, wg_own, bias],
        0.3,
        1,
        [
            pltpu.VMEM((fields, rows), jnp.int32),
            pltpu.VMEM((fields, emb, vocab), F32),
            pltpu.SemaphoreType.DMA((6,)),
        ],
        mib=58,
        loose=True,
        after=[rate],
    )
    rate = click_sum(rate, 1, [feat_own])
    (p0,) = relay([p0], 0.1, [rate])
    (q0,) = relay([q0], 0.1, [rate])
    p1 = over_rows(p0, 2)
    p2, p3 = over_rows(p0, 1), over_rows(p1, 1)
    part, gpart = run(
        partial_kernel,
        "own_share",
        [pinned((n_expert, rows), BF), sds((gates, rows), F32)],
        [feat_own, w_own, wg_here, bias],
        0.3,
        0,
        [pltpu.VMEM((n_expert, LANES), F32)],
        mib=20,
        after=[p0],
    )
    rate = click_sum(rate, 2, [gpart])
    q1 = over_rows(q0, 2)
    q2, q3 = over_rows(q0, 1), over_rows(q1, 1)
    q2, q3 = relay([q2, q3], RQ)
    (ids_oth,) = run(unpack_kernel, "unpack", [sds((fields, rows), jnp.int32)], [rows_oth], UNP, mib=4)
    look_oth, wg_oth = run(
        look_other_kernel,
        "look_other",
        [pinned((fields * emb, rows), BF), sds((gates, width), BF)],
        [where, ids_oth, p0, p1, p2, p3],
        LO,
        1,
        [pltpu.VMEM((fields, emb, vocab), F32)],
            )

    for k in range(3, n_bits):
        rate = click_sum(rate, k, [look_oth])
    wide_rows = experts * h1 + tasks * tower
    small_rows = experts * h2 + 2 * tasks * tower + gates + 8
    mix_rows = wide_rows // 2 + 192
    blocks = n_expert // LANES // 2
    lanes = chunk_of(rows, 2304)
    mix_rows = wide_rows // 2 + 192
    blocks = n_expert // LANES // 2
    d_pre, feat_oth, d_gates, w_oth, _, mix_keep, mix_send, pred = run(
        functools.partial(middle_kernel, float(sizes.shape[1] * n_rows)),
        "middle",
        [
            pinned((n_expert, rows), BF),
            feat,
            sds((gates, rows), BF),
            sds((width, n_expert), BF),
            sds((tasks, rows), F32),
            sds((mix_rows, h2), BF),
            sds((mix_rows, h2), BF),
            sds((4 * (rows // LANES) + 8, LANES), BF),
        ],
        [
            where,
            rate,
            feat_own,
            look_oth,
            rows_oth,
            p0,
            p1,
            p2,
            p3,
            q0,
            q1,
            q2,
            q3,
            wg_oth,
            part,
            gpart,
            b_gate.reshape(1, -1),
            w_inner,
            b_inner,
            jnp.transpose(w_tower, (0, 2, 1)),
            b_tower,
            w_head,
            b_head.reshape(1, -1),
            labels_t,
            weight,
        ],
        23.0,
        1,
        [
            pltpu.VMEM((gates, LANES), F32),
            pltpu.VMEM((experts, h1, h2), BF),
            pltpu.VMEM((experts * h2, LANES), BF),
            pltpu.VMEM((tasks * tower, LANES), F32),
            pltpu.VMEM((tasks * tower, LANES), F32),
            pltpu.VMEM((tasks, LANES), F32),
            pltpu.VMEM((wide_rows, h2), BF),
            pltpu.VMEM((96, LANES), F32),
            pltpu.VMEM((small_rows, LANES), F32),
            pltpu.VMEM((n_expert, rows), BF),
            pltpu.VMEM((experts * h2, rows), BF),
            pltpu.VMEM((experts, h2, lanes), BF),
            pltpu.VMEM((experts, h2, lanes), BF),
            pltpu.VMEM((tasks * tower, h2), F32),
        ],
        mib=36,
        alias={14: 0},
    )

    held = pinned((n_expert, rows), BF)
    deep = (fields + 1) // 2 * emb
    highs = vocab // LANES
    quarter_rows = wide_rows // 4
    mix_s = sds((quarter_rows + 128, h2), BF)
    mix_long = sds((quarter_rows + 128 + pred.shape[0], h2), BF)

    def blocks_s(*shape):
        return sds(shape + (width, LANES), BF)

    def planes_s(count):
        return sds((count, deep, LANES), BF)

    def features_back(part, parts, ids_half, d_pre, w_half, wg_half, carried, dtype, name, after):
        outs = [sds((dense_cols, rows), dtype), held]
        scratch = [pltpu.VMEM((fields, highs * emb, LANES), F32)]
        if part == parts - 1:
            outs = [planes_s(highs), planes_s(highs // 2), planes_s(highs // 2)] + outs
        else:
            outs, scratch = [sds((fields, highs * emb, LANES), F32)] + outs, []
        alias = {2: len(outs) - 1}
        if part > 0:
            alias[7] = len(outs) - 2
        return run(
            functools.partial(feature_kernel, part, parts),
            name,
            outs,
            [where, ids_half, d_pre, d_gates, w_half, wg_half] + carried,
            FB / parts,
            1,
            scratch,
            alias=alias,
            after=after,
        )

    mix_got = over_rows(mix_send, 1)
    ((mix, mix_send),) = take_step("step_0", where, [(work_mix_core, [mix_got, mix_keep, pred], [mix_s, mix_long])])
    mix_got = over_field(mix_send)
    dw_keep, dw_send, d_pre = run(
        first_weight_kernel,
        "first_weights",
        [blocks_s(2, blocks), blocks_s(2, blocks), held],
        [where, d_pre, feat_own, feat_oth],
        FW,
        1,
        alias={1: 2},
        after=[mix],
    )
    predicted_s = sds((tasks, rows_all), F32)
    pred_work = (work_pred, [pred, mix_got], [predicted_s])
    (mix,) = take_step("step_1", where, [(work_mix, [mix_got, mix], [mix_s])], [dw_keep])
    if fast:
        (dw_send,) = relay([dw_send], 0.0, [mix])
        dw_got = over_rows(dw_send, 1)
    mix_got = over_rows(mix, 2)
    dt_keep, *dt_send, dd_oth, d_pre = features_back(
        0, 1, ids_oth, d_pre, w_oth, wg_oth, [], BF, "features_other", [mix]
    )
    mix_work = (work_mix, [mix_got, mix], [mix_s])
    if fast:
        dt_got = [over_rows(value, 1) for value in dt_send]
        (a_keep, a_send, b_keep, b_send), mix = take_step(
            "step_2",
            where,
            [
                (work_two_ways, [dw_got, dw_keep], [blocks_s(4), blocks_s(4), blocks_s(2, 2), blocks_s(2, 2)]),
                mix_work,
            ],
            [dt_keep],
        )
        a_got = over_field(a_send)
        b_got = over_rows(b_send, 2)
        mix_got = over_rows(mix, 4)
    else:
        (mix,) = take_step("step_2", where, [mix_work], [dt_keep])
    acc, dd_own, d_pre = features_back(0, 2, ids_t, d_pre, w_own, wg_own, [], F32, "features_own_0", [mix])
    if fast:
        dt_oth, mix = take_step(
            "step_3",
            where,
            [(work_planes, dt_got + [dt_keep], [planes_s(highs)]), (work_mix, [mix_got, mix], [mix_s])],
            [acc],
        )
        mix_got = over_rows(mix, 8)
        dt_far = over_field(dt_oth)
        after = [dt_oth]
    else:
        after = []
    do_keep, *do_send, dd_own, _ = features_back(
        1, 2, ids_t, d_pre, w_own, wg_own, [acc, dd_own], F32, "features_own_1", after
    )
    dense_s = sds((dense_cols, rows_all), F32)
    if fast:
        do_got = [over_rows(value, 1) for value in do_send]
        (a_keep, a_send), (b_keep, b_send) = take_step(
            "step_4",
            where,
            [
                (work_halve(1), [a_got, a_keep], [blocks_s(2)] * 2),
                (work_sides, [b_got, b_keep], [blocks_s(2)] * 2),
            ],
            [do_keep],
        )
        a_got = over_rows(a_send, 2)
        b_got = over_field(b_send)
        (do_keep,) = take_step("step_5", where, [(work_sum, [dt_far, do_keep], [planes_s(highs)])], [a_keep])
        (d_keep, d_send), dd_oth = take_step(
            "step_5b",
            where,
            [
                (work_planes_halve, do_got + [do_keep], [planes_s(highs // 2)] * 2),
                (work_pass, [dd_oth], [sds(dd_oth.shape, BF)]),
            ],
        )
        dd_got = over_field(dd_oth)
        d_got = over_rows(d_send, 2)
        ends_s = sds((width + deep, h2), BF)
        finals, predicted = take_step(
            "step_5c",
            where,
            [
                (
                    work_mix_last,
                    [mix_got, mix],
                    [
                        sds((quarter_rows, h2), BF),
                        sds((experts, h2), F32),
                        sds((tasks, tower), F32),
                        sds((tasks, tower), F32),
                        sds((1, gates), F32),
                        sds((1, tasks), F32),
                        sds((1, 1), F32),
                        sds((n_expert // LANES, LANES), F32),
                        sds((gates, width), F32),
                    ],
                ),
                pred_work,
            ],
            [d_keep],
        )
        (e_keep, e_low, e_high, e_both), = take_step(
            "step_6",
            where,
            [
                (work_ends, [a_got, a_keep, b_got, b_keep, d_got, d_keep], [ends_s] * 4),
            ],
            finals[:1],
        )
        e_got = [over_rows(value, bit) for value, bit in ((e_low, 4), (e_high, 8), (e_both, 12))]
        wide, d_b_inner, d_b_tower, d_w_head, d_b_gate, d_b_head, loss, d_b_expert, d_w_gate = finals
        wide_f, wide_c = over_field(wide), over_rows(wide, 1)
        wide_fc = lax.ppermute(wide, ("rows", "field"), [(i, i ^ 3) for i in range(2 * n_rows)])
        (d_w_expert, d_table), (d_w_inner, d_w_tower), d_dense = take_step(
            "step_8",
            where,
            [
                (
                    work_ends_last,
                    [e_keep] + e_got,
                    [sds((width, LANES), F32), sds((fields, emb, vocab // n_rows), F32)],
                ),
                (
                    work_wide,
                    [wide, wide_f, wide_c, wide_fc],
                    [sds((4, experts * h1 // 4, h2), F32), sds((4, tasks * tower // 4, h2), F32)],
                ),
                (work_dense, [dd_own, dd_got], [dense_s]),
            ],
        )
        d_table = jnp.transpose(d_table, (0, 2, 1))
        d_w_inner = d_w_inner.reshape(experts, h1, h2)
        d_w_tower = jnp.transpose(d_w_tower.reshape(tasks, tower, h2), (0, 2, 1))
    else:

        def by_core(keep, send, axis):
            return jnp.where(core == 0, jnp.stack([keep, send], axis), jnp.stack([send, keep], axis))

        def tables(keep, send):
            value = by_core(keep, send, 1).reshape(highs, 2, deep // emb, emb, 2, LANES // 2)
            return jnp.transpose(value, (2, 4, 3, 0, 1, 5)).reshape(deep // emb * 2, emb, vocab)[:fields]

        do_send, dt_send = jnp.concatenate(do_send), jnp.concatenate(dt_send)
        d_t = add_low(tables(do_keep, do_send), over_field(tables(dt_keep, dt_send))).astype(F32)
        d_table = jnp.transpose(lax.psum_scatter(d_t, "rows", scatter_dimension=2, tiled=True), (0, 2, 1))
        d_w = by_core(dw_keep, dw_send, 2).reshape(2, 2 * blocks, width, LANES)
        d_w = add_low(d_w[0], over_field(d_w[1])).astype(F32)
        d_w = jnp.transpose(d_w, (1, 0, 2)).reshape(width, n_expert)
        d_w_expert = lax.psum_scatter(d_w, "rows", scatter_dimension=1, tiled=True)
        sums = get_split(mix, quarter_rows, 64)
        wide = mix[:quarter_rows]
        for k in range(2, n_bits):
            wide = add_low(wide, over_rows(wide, 1 << k))
            sums = sums + over_rows(sums, 1 << k)
        wide = ordered(j, wide, over_field(wide), 0)
        wide = ordered(core, wide, over_rows(wide, 1), 0).astype(F32).reshape(4, quarter_rows, h2)
        cut = experts * h1 // 4
        d_w_inner = wide[:, :cut].reshape(experts, h1, h2)
        d_w_tower = jnp.transpose(wide[:, cut:].reshape(tasks, tower, h2), (0, 2, 1))
        d_b_inner, d_b_tower, d_w_head = sums[:8], sums[8], sums[9]
        d_b_gate, d_b_head = sums[10, :gates], sums[10, gates : gates + tasks]
        loss = jnp.sum(sums[10, gates + tasks : gates + 2 * tasks])
        d_b_expert = sums[16:32]
        d_w_gate = jnp.concatenate([sums[32:48], sums[48:64]], axis=1)
        d_dense, predicted = take_step(
            "rest", where, [(work_dense, [dd_own, over_field(dd_oth)], [dense_s]), pred_work]
        )

    return (
        predicted.T,
        loss.reshape(()),
        d_dense.T,
        d_table,
        d_w_expert,
        d_b_expert.reshape(n_expert),
        d_w_gate.T,
        d_b_gate.reshape(gates),
        d_w_inner,
        d_b_inner.reshape(experts, h2),
        d_w_tower,
        d_b_tower.reshape(tasks, tower),
        d_w_head.reshape(tasks, tower),
        d_b_head.reshape(tasks),
    )


def solution(mesh):
    return jax.shard_map(
        per_device,
        mesh=mesh,
        in_specs=(
            P("rows", "field"),
            P("rows", "field"),
            P("field", None, None),
            P("rows", None),
            P("rows", None),
            P("field", None),
            P(),
            P("field", None),
            P(),
            P(),
            P(),
            P(),
            P(),
            P(),
            P(),
        ),
        out_specs=(
            P("rows", None),
            P(),
            P("rows", "field"),
            P("field", "rows", None),
            P("field", "rows"),
            P(),
            P("field", None),
            P(),
            P(),
            P(),
            P(),
            P(),
            P(),
            P(),
        ),
        check_vma=False,
    )
```
